32 devices in a mesh: dp: 8 (over z, y), seq: 4 (over x, core).
Axes of the slice: x: 2, y: 2, z: 4, core: 2. Of those that a mesh axis runs over, the one named last changes fastest.
Arguments:
- tokens: bfloat16 [8, 2048, 768], P('dp', 'seq'), may hold values from -6 to 6
- tissue: int32 [8], P('dp'), may hold values from 0 to 15
- norm1_gain: float32 [768], replicated, may hold values from 0.5 to 1.5
- norm1_bias: float32 [768], replicated, may hold values from -3 to 3
- norm2_gain: float32 [768], replicated, may hold values from 0.5 to 1.5
- norm2_bias: float32 [768], replicated, may hold values from -3 to 3
- qkv_weight: bfloat16 [768, 2304], replicated, may hold values from -0.21875 to 0.21875
- qkv_bias: float32 [2304], replicated, may hold values from -3 to 3
- out_weight: bfloat16 [768, 768], replicated, may hold values from -0.875 to 0.875
- out_bias: float32 [768], replicated, may hold values from -3 to 3
- up_weight: bfloat16 [768, 3072], replicated, may hold values from -0.21875 to 0.21875
- up_bias: float32 [3072], replicated, may hold values from -3 to 3
- down_weight: bfloat16 [3072, 768], replicated, may hold values from -0.109375 to 0.109375
- down_bias: float32 [768], replicated, may hold values from -3 to 3
- cotangent: bfloat16 [8, 2048, 768], P('dp', 'seq'), may hold values from -6 to 6
Outputs:
- mixed: bfloat16 [8, 2048, 768], P('dp', 'seq')
- input_grad: float32 [8, 2048, 768], P('dp', 'seq')
- norm1_gain_grad: float32 [768], replicated
- norm1_bias_grad: float32 [768], replicated
- norm2_gain_grad: float32 [768], replicated
- norm2_bias_grad: float32 [768], replicated
- qkv_weight_grad: float32 [768, 2304], replicated
- qkv_bias_grad: float32 [2304], replicated
- out_weight_grad: float32 [768, 768], replicated
- out_bias_grad: float32 [768], replicated
- up_weight_grad: float32 [768, 3072], replicated
- up_bias_grad: float32 [3072], replicated
- down_weight_grad: float32 [3072, 768], replicated
- down_bias_grad: float32 [768], replicated
The draws below stay inside these ranges and needn't reach their ends.
All inputs are finite; a program needn't handle non-finite values.
Results may differ from the reference program's by a relative error of at most 0.01.
Values may be sent and summed in bfloat16 or wider, within the bound.
A program may use at most 192 MiB of HBM per device.

```python
import math
import jax
import jax.numpy as jnp
import numpy as np
from jax import lax

D = 768
H = 12
E = 64
ROT = 16
FF = 3072
LEN = 2048
TISSUES = 16
SENTENCES = 8


def with_ends(array, stream_key, least, high):
    index_at = [jax.random.randint(jax.random.fold_in(stream_key, axis), (), 0, length) for axis, length in enumerate(array.shape)]
    main_axis = array.shape.index(max(array.shape))
    next_to = index_at[:main_axis] + [(index_at[main_axis] + 1) % array.shape[main_axis]] + index_at[main_axis + 1:]
    return array.at[tuple(index_at)].set(least).at[tuple(next_to)].set(high)


def level_of(stream_key, shape, shards, least, top_value):
    def one(dim, shards_of):
        heights = jax.random.uniform(jax.random.fold_in(jax.random.fold_in(stream_key, 6), dim), (shards_of,), jnp.float32, least / len(shards), top_value / len(shards))
        return jnp.repeat(jnp.exp(heights), shape[dim] // shards_of).reshape((-1,) + (1,) * (len(shape) - dim - 1))

    loudness = one(*shards[0])
    for cut in shards[1:]:
        loudness = loudness * one(*cut)
    return loudness


def rank_table(number_of, lean):
    weights = [(1 << 20) // math.isqrt(standing ** lean) + 1 for standing in range(1, number_of + 1)]
    width = 1 + sum(weights) // (1 << 30)
    return np.cumsum(np.array([max(1, weight // width) for weight in weights]))


def ranked_ids(rng, shape, amount, skew):
    table = rank_table(amount, skew)
    lot = jax.random.randint(jax.random.fold_in(rng, 1), shape, 0, int(table[amount - 1]))
    grade = jnp.searchsorted(jnp.asarray(table, jnp.int32), lot, side="right")
    return jax.random.permutation(jax.random.fold_in(rng, 2), amount)[grade].astype(jnp.int32)


def bell_draw(stream_key, shape, deviation, reach, cuts=(), kind=jnp.bfloat16):
    factor_of = level_of(stream_key, shape, cuts, -0.22, 0.18) if cuts else 1.0
    entries = jax.random.normal(stream_key, shape, jnp.float32) * deviation * factor_of
    return jnp.minimum(jnp.maximum(entries, -reach), reach).astype(kind)


def setup_inputs(seed: int = 0) -> dict:
    splits = jax.random.split(jax.random.key(seed), 16)
    return {
        "tokens": bell_draw(splits[0], (SENTENCES, LEN, D), 1.0, 6.0, ((0, 8), (1, 4))),
        "tissue": with_ends(ranked_ids(splits[1], (SENTENCES,), TISSUES, 2), jax.random.fold_in(splits[1], 3), 0, TISSUES - 1).astype(jnp.int32),
        "norm1_gain": jnp.clip(1.0 + 0.1 * jax.random.normal(splits[2], (D,), jnp.float32), 0.5, 1.5),
        "norm1_bias": bell_draw(splits[3], (D,), 0.3, 3.0, (), jnp.float32),
        "norm2_gain": jnp.clip(1.0 + 0.1 * jax.random.normal(splits[4], (D,), jnp.float32), 0.5, 1.5),
        "norm2_bias": bell_draw(splits[5], (D,), 0.3, 3.0, (), jnp.float32),
        "qkv_weight": bell_draw(splits[6], (D, 3 * D), D ** -0.5, 0.21875),
        "qkv_bias": bell_draw(splits[7], (3 * D,), 0.3, 3.0, (), jnp.float32),
        "out_weight": bell_draw(splits[8], (D, D), (D // 16) ** -0.5, 0.875),
        "out_bias": bell_draw(splits[9], (D,), 0.3, 3.0, (), jnp.float32),
        "up_weight": bell_draw(splits[10], (D, FF), D ** -0.5, 0.21875),
        "up_bias": bell_draw(splits[11], (FF,), 0.3, 3.0, (), jnp.float32),
        "down_weight": bell_draw(splits[12], (FF, D), FF ** -0.5, 0.109375),
        "down_bias": bell_draw(splits[13], (D,), 0.3, 3.0, (), jnp.float32),
        "cotangent": bell_draw(splits[14], (SENTENCES, LEN, D), 1.0, 6.0, ((0, 8), (1, 4))),
    }


highest = lax.Precision.HIGHEST
norm_eps = 1e-05
masked_score = -1e+30

@jax.custom_vjp
def low(v):
    return lax.optimization_barrier(v.astype(jnp.bfloat16)).astype(jnp.float32)

@jax.custom_vjp
def low_back(v):
    return v

def low_keep(v):
    return (low(v), None)

def low_pass(kept, grad):
    return (grad,)

def back_keep(v):
    return (v, None)

def back_low(kept, grad):
    return (low(grad),)
low.defvjp(low_keep, low_pass)
low_back.defvjp(back_keep, back_low)

def layer_norm(row_data, norm_gain, norm_shift):
    centred = row_data - lax.optimization_barrier(jnp.mean(row_data, axis=-1, keepdims=True))
    inverse = lax.rsqrt(lax.optimization_barrier(jnp.mean(centred * centred, axis=-1, keepdims=True)) + norm_eps)
    return centred * inverse * norm_gain + norm_shift

def rotary_tables(places, rotary_width):
    half_width = rotary_width // 2
    frequency = 10000.0 ** (-2.0 * jnp.arange(half_width, dtype=jnp.float32) / rotary_width)
    angles = places.astype(jnp.float32)[:, None] * frequency[None, :]
    return (jnp.cos(angles), jnp.sin(angles))

def rotate(head_data, cosine, sine):
    half_width = cosine.shape[-1]
    cos_wide = cosine[:, None, :]
    sin_wide = sine[:, None, :]
    leading = head_data[..., :half_width]
    trailing = head_data[..., half_width:2 * half_width]
    others = head_data[..., 2 * half_width:]
    return jnp.concatenate([leading * cos_wide - trailing * sin_wide, trailing * cos_wide + leading * sin_wide, others], axis=-1)

def attention(query, keys, values):
    block_rows = min(512, LEN)
    block_count = LEN // block_rows
    score_scale = 1.0 / math.sqrt(E)
    key_places = jnp.arange(LEN, dtype=jnp.int32)

    def one_block(block_index):
        first_row = (block_index * block_rows).astype(jnp.int32)
        query_rows = lax.dynamic_slice_in_dim(query, first_row, block_rows, 0)
        raw_scores = low_back(jnp.einsum('qhe,khe->hqk', query_rows, keys, precision=highest) * score_scale)
        query_places = first_row + jnp.arange(block_rows, dtype=jnp.int32)
        allowed = key_places[None, :] <= query_places[:, None]
        masked = jnp.where(allowed[None, :, :], raw_scores, masked_score)
        largest = lax.optimization_barrier(jnp.max(masked, axis=-1, keepdims=True))
        log_total = largest + jnp.log(lax.optimization_barrier(jnp.sum(jnp.exp(masked - largest), axis=-1, keepdims=True)))
        prob_low = low(jnp.exp(masked - log_total))
        return jnp.einsum('hqk,khe->qhe', prob_low, values, precision=highest)
    blocks_out = lax.map(jax.checkpoint(one_block), jnp.arange(block_count, dtype=jnp.int32))
    return blocks_out.reshape(LEN, H, E)

def sentence_layer(inputs, params):
    norm1_gain, norm1_bias, norm2_gain, norm2_bias, qkv_weight, qkv_bias, out_weight, out_bias, up_weight, up_bias, down_weight, down_bias = params
    first_in = low(layer_norm(inputs, norm1_gain, norm1_bias))
    second_in = low(layer_norm(inputs, norm2_gain, norm2_bias))
    joint = low_back(jnp.dot(first_in, qkv_weight, precision=highest, preferred_element_type=jnp.float32) + qkv_bias)
    joint = joint.reshape(LEN, 3, H, E)
    cosine, sine = rotary_tables(jnp.arange(LEN, dtype=jnp.int32), ROT)
    query = low(rotate(joint[:, 0], cosine, sine))
    keys = low(rotate(joint[:, 1], cosine, sine))
    values = low(joint[:, 2])
    attended = attention(query, keys, values).reshape(LEN, D)
    heads_out = low(low_back(attended))
    attn = low_back(jnp.dot(heads_out, out_weight, precision=highest, preferred_element_type=jnp.float32) + out_bias)
    pre = low_back(jnp.dot(second_in, up_weight, precision=highest, preferred_element_type=jnp.float32) + up_bias)
    act = low(jax.nn.gelu(pre, approximate=False))
    branch = low_back(jnp.dot(act, down_weight, precision=highest, preferred_element_type=jnp.float32) + down_bias)
    return inputs + attn + branch

def reference(tokens, tissue, norm1_gain, norm1_bias, norm2_gain, norm2_bias, qkv_weight, qkv_bias, out_weight, out_bias, up_weight, up_bias, down_weight, down_bias, cotangent):
    params = tuple((item.astype(jnp.float32) for item in (norm1_gain, norm1_bias, norm2_gain, norm2_bias, qkv_weight, qkv_bias, out_weight, out_bias, up_weight, up_bias, down_weight, down_bias)))
    labels = jnp.arange(TISSUES, dtype=jnp.int32)
    table = (tissue[:, None] == labels[None, :]).astype(jnp.float32)
    counts = lax.optimization_barrier(jnp.sum(table, axis=0))
    sentence_weight = SENTENCES / (TISSUES * lax.optimization_barrier(jnp.sum(table * counts[None, :], axis=1)))

    def one_sentence(totals, sentence_item):
        sentence_tokens, sentence_cot, sentence_scale = sentence_item
        layer_out, pullback = jax.vjp(sentence_layer, sentence_tokens.astype(jnp.float32), params)
        token_grad, param_grads = pullback(sentence_cot.astype(jnp.float32) * sentence_scale)
        totals = jax.tree.map(jnp.add, totals, param_grads)
        return (totals, (layer_out.astype(jnp.bfloat16), token_grad))
    zeros_init = tuple((jnp.zeros(item.shape, jnp.float32) for item in params))
    grads, (mixed, input_grad) = lax.scan(one_sentence, zeros_init, (tokens, cotangent, sentence_weight))
    return (mixed, input_grad) + tuple(grads)
```

```python
import functools
import math

import jax
import jax.numpy as jnp
from jax import lax
from jax.experimental import pallas as pl
from jax.experimental.pallas import tpu as pltpu
from jax.sharding import PartitionSpec as P

H = 12
E = 64
ROT = 16
TISSUES = 16
norm_eps = 1e-05
masked_score = -1e30
f32 = jnp.float32
bf16 = jnp.bfloat16
MESH = pl.DeviceIdType.MESH
ANY = pl.BlockSpec(memory_space=pl.ANY)
VMEM = pl.BlockSpec(memory_space=pltpu.VMEM)
VECTOR_ROWS = 16
CORE, CHIP = 1, 2


def bits_of(count):
    return count.bit_length() - 1


def flip(index, bit):
    return index + bit - 2 * bit * (lax.div(index, bit) % 2)


def bit_at(index, bit):
    return lax.div(index, bit) % 2


class Links:
    def __init__(self, dp_count, send_sems, recv_sems):
        self.dp = lax.axis_index("dp")
        self.seq = lax.axis_index("seq")
        self.dp_bits = [1 << j for j in range(bits_of(dp_count))]
        self.send_sems, self.recv_sems, self.used = send_sems, recv_sems, 0

    def over(self, axis, bit):
        if axis == "seq":
            return (self.dp, flip(self.seq, bit))
        return (flip(self.dp, bit), self.seq)

    def barrier(self):
        semaphore = pltpu.get_barrier_semaphore()
        partners = [self.over("seq", CORE), self.over("seq", CHIP)]
        partners += [self.over("dp", bit) for bit in self.dp_bits]
        for partner in partners:
            pl.semaphore_signal(semaphore, inc=1, device_id=partner, device_id_type=MESH)
        pl.semaphore_wait(semaphore, len(partners))

    def send(self, source, target, partner):
        copy = pltpu.make_async_remote_copy(
            src_ref=source,
            dst_ref=target,
            send_sem=self.send_sems.at[self.used],
            recv_sem=self.recv_sems.at[self.used],
            device_id=partner,
            device_id_type=MESH,
        )
        self.used += 1
        copy.start()
        return copy


def drive(tasks):
    tasks = list(tasks)
    while tasks:
        tasks = [task for task in tasks if next(task, "done") != "done"]


def add_up_everywhere(links, steps, buffer):
    for number, (axis, bit) in enumerate(steps):
        copy = links.send(buffer.at[2 * number], buffer.at[2 * number + 1], links.over(axis, bit))
        yield
        copy.wait()
        buffer[2 * number + 2] = buffer[2 * number] + buffer[2 * number + 1]


def gather_kernel(dp_count, pieces, x_ref, c_ref, t_ref, xo_ref, co_ref, t_out, t_buf, sends, recvs, own_sem):
    links = Links(dp_count, sends, recvs)
    links.barrier()
    places = x_ref.shape[0]
    rows = places // pieces

    def block(owner, piece):
        return pl.ds(pl.multiple_of(owner * places + piece * rows, rows), rows)

    def one_piece(source, target, piece):
        mine = source.at[pl.ds(piece * rows, rows)]
        own = target.at[block(links.seq, piece)]
        across = links.send(mine, own, links.over("seq", CHIP))
        beside = links.send(mine, own, links.over("seq", CORE))
        yield
        across.wait()
        passed = target.at[block(flip(links.seq, CHIP), piece)]
        onward = links.send(passed, passed, links.over("seq", CORE))
        yield
        beside.wait()
        onward.wait()

    locals_ = []
    for number, (source, target) in enumerate(((x_ref, xo_ref), (c_ref, co_ref))):
        copy = pltpu.make_async_copy(
            source, target.at[pl.ds(pl.multiple_of(links.seq * places, places), places)], own_sem.at[number]
        )
        copy.start()
        locals_.append(copy)
    t_buf[0] = t_ref[...]
    tasks = [
        one_piece(source, target, piece)
        for source, target in ((x_ref, xo_ref), (c_ref, co_ref))
        for piece in range(pieces)
    ]
    tasks.append(add_up_everywhere(links, [("dp", bit) for bit in links.dp_bits], t_buf))
    drive(tasks)
    t_out[...] = t_buf[2 * len(links.dp_bits)]
    for copy in locals_:
        copy.wait()


def gather(dp_count, seq_count, x, c, table):
    pieces = 4
    places, width = x.shape
    copies = 3 * 2 * pieces + bits_of(dp_count)
    whole = jax.ShapeDtypeStruct((places * seq_count, width), x.dtype)
    return pl.pallas_call(
        functools.partial(gather_kernel, dp_count, pieces),
        out_shape=(whole, whole, jax.ShapeDtypeStruct(table.shape, f32)),
        in_specs=[ANY, ANY, VMEM],
        out_specs=(ANY, ANY, VMEM),
        scratch_shapes=[
            pltpu.VMEM((2 * bits_of(dp_count) + 1,) + table.shape, f32),
            pltpu.SemaphoreType.DMA((copies,)),
            pltpu.SemaphoreType.DMA((copies,)),
            pltpu.SemaphoreType.DMA((2,)),
        ],
        compiler_params=pltpu.CompilerParams(collective_id=0, has_side_effects=True),
        name="gather_sentence",
    )(x, c, table)


def dot(a, b, dims):
    return lax.dot_general(a, b, (dims, ((), ())), preferred_element_type=f32)


NN = ((1,), (0,))
NT = ((1,), (1,))


def attention_kernel(block, q_ref, k_ref, v_ref, g_ref, qt_ref, gt_ref, o_ref, dq_ref, dkt_ref, dvt_ref):
    length = q_ref.shape[1]
    dkt_ref[...] = jnp.zeros_like(dkt_ref)
    dvt_ref[...] = jnp.zeros_like(dvt_ref)
    for i in range(length // block):
        own = pl.ds(i * block, block)
        past = pl.ds(0, (i + 1) * block)
        q, g = q_ref[0, own, :], g_ref[0, own, :]
        keys, values = k_ref[0, past, :], v_ref[0, past, :]
        scores = dot(q, keys, NT)
        row = lax.broadcasted_iota(jnp.int32, scores.shape, 0) + i * block
        column = lax.broadcasted_iota(jnp.int32, scores.shape, 1)
        scores = jnp.where(column <= row, scores, masked_score)
        largest = jnp.max(scores, axis=1, keepdims=True)
        weight = jnp.exp(scores - largest)
        prob = weight * (1.0 / jnp.sum(weight, axis=1, keepdims=True))
        prob_low = prob.astype(bf16)
        attended = dot(prob_low, values, NN)
        o_ref[0, own, :] = attended.astype(bf16)
        delta = jnp.sum(attended * g.astype(f32), axis=1, keepdims=True)
        prob_grad = dot(g, values, NT)
        score_grad = (prob * (prob_grad - delta)).astype(bf16)
        dq_ref[0, own, :] = dot(score_grad, keys, NN) * (1.0 / math.sqrt(E))
        dkt_ref[0, :, past] += dot(qt_ref[0, :, own], score_grad, NN)
        dvt_ref[0, :, past] += dot(gt_ref[0, :, own], prob_low, NN)


def attention(q, k, v, g, qt, gt):
    heads, length, size = q.shape
    tall = pl.BlockSpec((1, length, size), lambda h: (h, 0, 0))
    wide = pl.BlockSpec((1, size, length), lambda h: (h, 0, 0))
    return pl.pallas_call(
        functools.partial(attention_kernel, min(256, length)),
        grid=(heads,),
        out_shape=(
            jax.ShapeDtypeStruct((heads, length, size), bf16),
            jax.ShapeDtypeStruct((heads, length, size), f32),
            jax.ShapeDtypeStruct((heads, size, length), f32),
            jax.ShapeDtypeStruct((heads, size, length), f32),
        ),
        in_specs=[tall, tall, tall, tall, wide, wide],
        out_specs=(tall, tall, wide, wide),
        compiler_params=pltpu.CompilerParams(vmem_limit_bytes=48 * 2**20),
        name="attention",
    )(q, k, v, g, qt, gt)


def sum_kernel(dp_count, orders, grads_ref, vec_ref, part_ref, full_ref, vec_out, sum_ref, *scratch):
    groups, rows, width = grads_ref.shape
    halves = scratch[: bits_of(dp_count)]
    vec_buf, core_buf, chip_buf, sends, recvs, own_sems = scratch[bits_of(dp_count) :]
    links = Links(dp_count, sends, recvs)
    links.barrier()

    def one_group(group):
        scatter, collect = orders[group]
        held, start, size = grads_ref.at[group], 0, rows
        for number, bit in enumerate(scatter):
            size //= 2
            mine = bit_at(links.dp, bit)
            keep = pl.ds(pl.multiple_of(mine * size, size), size)
            give = pl.ds(pl.multiple_of((1 - mine) * size, size), size)
            arrived = halves[number].at[group]
            copy = links.send(held.at[give], arrived, links.over("dp", bit))
            yield
            copy.wait()
            arrived[...] = (held[keep, :].astype(f32) + arrived[...].astype(f32)).astype(bf16)
            held, start = arrived, start + mine * size
        owners = [links.seq]

        def region(owner):
            return full_ref.at[owner, group, pl.ds(pl.multiple_of(start, size), size)]

        own = pltpu.make_async_copy(held, region(links.seq), own_sems.at[group])
        own.start()
        yield
        own.wait()
        for axis, bit in collect:
            partner = links.over(axis, bit)
            copies = [links.send(region(owner), region(owner), partner) for owner in owners]
            yield
            for copy in copies:
                copy.wait()
            if axis == "dp":
                start = start - bit_at(links.dp, bit) * size
                size *= 2
            else:
                owners = owners + [flip(owner, bit) for owner in owners]

    def one_part(which):
        core, chip = bit_at(links.seq, CORE), bit_at(links.seq, CHIP)
        copies = [
            links.send(part_ref.at[which, 2 * at + 1 - core], core_buf.at[which, at], links.over("seq", CORE))
            for at in range(2)
        ]
        yield
        for at in range(2):
            copies[at].wait()
            own = part_ref[which, 2 * at + core].astype(f32)
            core_buf[which, at] = (own + core_buf[which, at].astype(f32)).astype(bf16)
        copy = links.send(core_buf.at[which, 1 - chip], chip_buf.at[which], links.over("seq", CHIP))
        yield
        yield
        yield
        copy.wait()
        sum_ref[which] = core_buf[which, chip].astype(f32) + chip_buf[which].astype(f32)

    vec_buf[0] = vec_ref[...]
    vec_steps = [("seq", CORE), ("seq", CHIP)] + [("dp", bit) for bit in links.dp_bits]
    tasks = [one_part(which) for which in range(2)]
    tasks += [one_group(group) for group in range(groups)]
    tasks.append(add_up_everywhere(links, vec_steps, vec_buf))
    drive(tasks)
    vec_out[...] = vec_buf[2 * len(vec_steps)]


def orders_for(dp_count, groups):
    bits = [1 << j for j in range(bits_of(dp_count))]
    turned = bits[1:] + bits[:1]
    core, chip = ("seq", CORE), ("seq", CHIP)

    def both(scatter, chip_at):
        collect = [("dp", bit) for bit in reversed(scatter)]
        collect.insert(chip_at, chip)
        return (scatter, collect + [core])

    kinds = [
        both(bits, len(bits)),
        both(turned, len(bits)),
        both(bits, len(bits) - 1),
    ]
    return [kinds[group * 3 // groups] for group in range(groups)]


def sums(dp_count, seq_count, grads, vec, part):
    groups, rows, width = grads.shape
    _, _, places, _ = part.shape
    bits = bits_of(dp_count)
    copies = groups * (bits + bits + 2 * bits + 3) + 6 + bits + 2
    scratch = [pltpu.VMEM((groups, rows >> (j + 1), width), bf16) for j in range(bits)]
    scratch += [
        pltpu.VMEM((2 * (bits + 2) + 1,) + vec.shape, f32),
        pltpu.VMEM((2, 2, places, width), bf16),
        pltpu.VMEM((2, places, width), bf16),
        pltpu.SemaphoreType.DMA((copies,)),
        pltpu.SemaphoreType.DMA((copies,)),
        pltpu.SemaphoreType.DMA((groups,)),
    ]
    return pl.pallas_call(
        functools.partial(sum_kernel, dp_count, orders_for(dp_count, groups)),
        out_shape=(
            jax.ShapeDtypeStruct((seq_count, groups, rows, width), bf16),
            jax.ShapeDtypeStruct(vec.shape, f32),
            jax.ShapeDtypeStruct((2, places, width), f32),
        ),
        in_specs=[VMEM, VMEM, VMEM],
        out_specs=(ANY, VMEM, VMEM),
        scratch_shapes=scratch,
        compiler_params=pltpu.CompilerParams(
            collective_id=1, has_side_effects=True, vmem_limit_bytes=48 * 2**20
        ),
        name="sums",
    )(grads, vec, part)


def rotary_tables(length):
    half = ROT // 2
    frequency = 10000.0 ** (-2.0 * jnp.arange(half, dtype=f32) / ROT)
    angles = jnp.arange(length, dtype=jnp.int32).astype(f32)[:, None] * frequency[None, :]
    return jnp.cos(angles), jnp.sin(angles)


def rotate(heads, cosine, sine):
    half = cosine.shape[-1]
    a, b = heads[..., :half], heads[..., half : 2 * half]
    c, s = cosine[:, None, :], sine[:, None, :]
    return jnp.concatenate([a * c - b * s, b * c + a * s, heads[..., 2 * half :]], axis=-1)


def normalise(rows):
    centred = rows - jnp.mean(rows, axis=-1, keepdims=True)
    inverse = lax.rsqrt(jnp.mean(centred * centred, axis=-1, keepdims=True) + norm_eps)
    return centred * inverse, inverse


def body(
    tokens,
    tissue,
    norm1_gain,
    norm1_bias,
    norm2_gain,
    norm2_bias,
    qkv_weight,
    qkv_bias,
    out_weight,
    out_bias,
    up_weight,
    up_bias,
    down_weight,
    down_bias,
    cotangent,
):
    dp_count, seq_count = lax.axis_size("dp"), lax.axis_size("seq")
    rank = lax.axis_index("seq")
    _, places, width = tokens.shape
    length = places * seq_count
    heads = H // seq_count
    attn_width = heads * E
    hidden = up_weight.shape[1] // seq_count
    own_x, own_c = tokens.reshape(places, width), cotangent.reshape(places, width)

    labels = lax.broadcasted_iota(jnp.int32, (8, 128), 1)
    own_table = (labels == tissue[0]).astype(f32)
    x_all, c_all, table = gather(dp_count, seq_count, own_x, own_c, own_table)
    count = jnp.sum(table[0] * own_table[0])
    weight = dp_count / (TISSUES * count)

    q_w = lax.dynamic_slice_in_dim(
        qkv_weight.reshape(width, 3, H * E), rank * attn_width, attn_width, 2
    ).reshape(width, 3 * attn_width)
    q_b = lax.dynamic_slice_in_dim(qkv_bias.reshape(3, H * E), rank * attn_width, attn_width, 1).reshape(-1)
    o_w = lax.dynamic_slice_in_dim(out_weight, rank * attn_width, attn_width, 0)
    u_w = lax.dynamic_slice_in_dim(up_weight, rank * hidden, hidden, 1)
    u_b = lax.dynamic_slice_in_dim(up_bias, rank * hidden, hidden, 0)
    d_w = lax.dynamic_slice_in_dim(down_weight, rank * hidden, hidden, 0)

    normed, _ = normalise(x_all.astype(f32))
    first_in = (normed * norm1_gain + norm1_bias).astype(bf16)
    second_in = (normed * norm2_gain + norm2_bias).astype(bf16)
    grad_low = (c_all.astype(f32) * weight).astype(bf16)

    joint = (dot(first_in, q_w, NN) + q_b).reshape(length, 3, heads, E)
    cosine, sine = rotary_tables(length)
    query = (rotate(joint[:, 0], cosine, sine).astype(bf16) * (1.0 / math.sqrt(E))).astype(bf16)
    keys = rotate(joint[:, 1], cosine, sine).astype(bf16)
    values = joint[:, 2].astype(bf16)
    heads_grad = dot(grad_low, o_w, NT).astype(bf16).reshape(length, heads, E)

    tall = lambda a: jnp.transpose(a, (1, 0, 2))
    wide = lambda a: jnp.transpose(a, (1, 2, 0))
    heads_out, dq, dkt, dvt = attention(
        tall(query), tall(keys), tall(values), tall(heads_grad), wide(query), wide(heads_grad)
    )
    heads_out = tall(heads_out).reshape(length, attn_width)
    dq = rotate(tall(dq), cosine, -sine)
    dk = rotate(jnp.transpose(dkt, (2, 0, 1)), cosine, -sine)
    dv = jnp.transpose(dvt, (2, 0, 1))
    joint_grad = jnp.stack([dq, dk, dv], axis=1).reshape(length, 3 * attn_width).astype(bf16)

    pre = dot(second_in, u_w, NN) + u_b
    gate = 0.5 * (1.0 + lax.erf(pre * (1.0 / math.sqrt(2.0))))
    act = (pre * gate).astype(bf16)
    slope = gate + pre * jnp.exp(-0.5 * pre * pre) * (1.0 / math.sqrt(2.0 * math.pi))
    pre_grad = (dot(grad_low, d_w, NT) * slope).astype(bf16)
    second_grad = dot(pre_grad, u_w, NT)
    first_grad = dot(joint_grad, q_w, NT)

    mixed_part = dot(act, d_w, NN) + dot(heads_out, o_w, NN)
    row_part = first_grad * norm1_gain + second_grad * norm2_gain
    part = jnp.stack([mixed_part.astype(bf16), row_part.astype(bf16)]).reshape(2, seq_count, places, width)

    TN = ((0,), (0,))
    up_grad = dot(second_in, pre_grad, TN)
    down_grad = dot(act, grad_low, TN)
    qkv_grad = dot(first_in, joint_grad, TN)
    out_grad = dot(grad_low, heads_out, TN)
    grads = jnp.concatenate(
        [up_grad.astype(bf16), down_grad.astype(bf16), jnp.concatenate([qkv_grad, out_grad], axis=1).astype(bf16)]
    )
    groups = 6
    group_rows = grads.shape[0] // groups
    padded = -(-group_rows // (16 * dp_count)) * 16 * dp_count
    grads = jnp.pad(grads.reshape(groups, group_rows, width), ((0, 0), (0, padded - group_rows), (0, 0)))

    low_sum = jnp.sum(grad_low.astype(f32), axis=0) * (1.0 / seq_count)
    placed_up = lax.dynamic_update_slice_in_dim(
        jnp.zeros((seq_count * hidden,), f32), jnp.sum(pre_grad.astype(f32), axis=0), rank * hidden, 0
    ).reshape(-1, width)
    placed_qkv = lax.dynamic_update_slice_in_dim(
        jnp.zeros((3, H * E), f32),
        jnp.sum(joint_grad.astype(f32), axis=0).reshape(3, attn_width),
        rank * attn_width,
        1,
    ).reshape(-1, width)
    vec = jnp.concatenate(
        [
            jnp.sum(first_grad * normed, axis=0)[None],
            jnp.sum(first_grad, axis=0)[None],
            jnp.sum(second_grad * normed, axis=0)[None],
            jnp.sum(second_grad, axis=0)[None],
            low_sum[None],
            placed_up,
            placed_qkv,
        ]
    )
    used = vec.shape[0]
    vec = jnp.pad(vec, ((0, VECTOR_ROWS - used), (0, 0)))

    full, vec, part_sum = sums(dp_count, seq_count, grads, vec, part)

    x32 = own_x.astype(f32)
    mixed = (x32 + part_sum[0] + (out_bias + down_bias)).astype(bf16).reshape(tokens.shape)
    own_normed, own_inverse = normalise(x32)
    scaled = part_sum[1]
    rows_grad = own_inverse * (
        scaled
        - jnp.mean(scaled, axis=-1, keepdims=True)
        - own_normed * jnp.mean(scaled * own_normed, axis=-1, keepdims=True)
    )
    input_grad = (own_c.astype(f32) * weight + rows_grad).reshape(tokens.shape)

    full = full[:, :, :group_rows].reshape(seq_count, 3, width, width)
    up_total = jnp.transpose(full[:, 0], (1, 0, 2)).reshape(width, seq_count * hidden).astype(f32)
    down_total = full[:, 1].reshape(seq_count * hidden, width).astype(f32)
    mixed_block = full[:, 2]
    qkv_total = (
        jnp.transpose(mixed_block[:, :, : 3 * attn_width].reshape(seq_count, width, 3, attn_width), (1, 2, 0, 3))
        .reshape(width, 3 * H * E)
        .astype(f32)
    )
    out_total = jnp.transpose(mixed_block[:, :, 3 * attn_width :], (0, 2, 1)).reshape(H * E, width).astype(f32)
    return (
        mixed,
        input_grad,
        vec[0],
        vec[1],
        vec[2],
        vec[3],
        qkv_total,
        vec[9:12].reshape(-1),
        out_total,
        vec[4],
        up_total,
        vec[5:9].reshape(-1),
        down_total,
        vec[4],
    )


def solution(mesh):
    rows = P("dp", "seq", None)
    return jax.shard_map(
        body,
        mesh=mesh,
        in_specs=(rows, P("dp")) + (P(),) * 12 + (rows,),
        out_specs=(rows, rows) + (P(),) * 12,
        check_vma=False,
    )
```

```python
import functools
import math

import jax
import jax.numpy as jnp
from jax import lax
from jax.experimental import pallas as pl
from jax.experimental.pallas import tpu as pltpu
from jax.sharding import PartitionSpec as P

H = 12
E = 64
ROT = 16
TISSUES = 16
norm_eps = 1e-05
masked_score = -1e30
f32 = jnp.float32
bf16 = jnp.bfloat16
MESH = pl.DeviceIdType.MESH
ANY = pl.BlockSpec(memory_space=pl.ANY)
VMEM = pl.BlockSpec(memory_space=pltpu.VMEM)
VECTOR_ROWS = 16
CORE, CHIP = 1, 2
PAIR = 2 * E
CHUNK = 256
GROUPS = 6

NN = ((1,), (0,))
NT = ((1,), (1,))
TN = ((0,), (0,))


def dot(a, b, dims):
    return lax.dot_general(a, b, (dims, ((), ())), preferred_element_type=f32)


def bits_of(count):
    return count.bit_length() - 1


def bit_at(index, bit):
    return lax.div(index, bit) % 2


def flip(index, bit):
    return index + bit - 2 * bit * bit_at(index, bit)


def aligned(start, size):
    return pl.ds(pl.multiple_of(start, size), size)


class Links:
    def __init__(self, dp_count, send_sems, recv_sems):
        self.dp = lax.axis_index("dp")
        self.seq = lax.axis_index("seq")
        self.dp_bits = [1 << j for j in range(bits_of(dp_count))]
        self.send_sems, self.recv_sems, self.used = send_sems, recv_sems, 0

    def over(self, axis, bit):
        if axis == "seq":
            return (self.dp, flip(self.seq, bit))
        return (flip(self.dp, bit), self.seq)

    def barrier(self):
        semaphore = pltpu.get_barrier_semaphore()
        partners = [self.over("seq", CORE), self.over("seq", CHIP)]
        partners += [self.over("dp", bit) for bit in self.dp_bits]
        for partner in partners:
            pl.semaphore_signal(semaphore, inc=1, device_id=partner, device_id_type=MESH)
        pl.semaphore_wait(semaphore, len(partners))

    def send(self, source, target, partner):
        copy = pltpu.make_async_remote_copy(
            src_ref=source,
            dst_ref=target,
            send_sem=self.send_sems.at[self.used],
            recv_sem=self.recv_sems.at[self.used],
            device_id=partner,
            device_id_type=MESH,
        )
        self.used += 1
        copy.start()
        return copy


class Turns:
    def __init__(self):
        self.tasks = []

    def add(self, tasks):
        self.tasks += list(tasks)

    def step(self, count=1):
        for _ in range(count):
            if self.tasks:
                task = self.tasks.pop(0)
                if next(task, "done") != "done":
                    self.tasks.append(task)

    def finish(self):
        while self.tasks:
            self.step()


def add_up_everywhere(links, steps, buffer):
    for number, (axis, bit) in enumerate(steps):
        copy = links.send(buffer.at[2 * number], buffer.at[2 * number + 1], links.over(axis, bit))
        yield
        copy.wait()
        buffer[2 * number + 2] = buffer[2 * number] + buffer[2 * number + 1]


def orders_for(dp_count):
    bits = [1 << j for j in range(bits_of(dp_count))]
    turned = bits[1:] + bits[:1]
    core, chip = ("seq", CORE), ("seq", CHIP)

    def both(scatter, chip_at):
        collect = [("dp", bit) for bit in reversed(scatter)]
        collect.insert(chip_at, chip)
        return (scatter, collect + [core])

    kinds = [
        both(bits, len(bits)),
        both(turned, len(bits)),
        both(bits, len(bits) - 1),
    ]
    return [kinds[group * 3 // GROUPS] for group in range(GROUPS)]


def normalise(rows):
    centred = rows - jnp.mean(rows, axis=-1, keepdims=True)
    inverse = lax.rsqrt(jnp.mean(centred * centred, axis=-1, keepdims=True) + norm_eps)
    return centred * inverse, inverse


def swapped(pairs):
    lane = lax.broadcasted_iota(jnp.int32, pairs.shape, 1)
    half = ROT // 2
    return jnp.where(lane < half, pltpu.roll(pairs, PAIR - half, 1), pltpu.roll(pairs, half, 1))


def layer_kernel(
    dp_count,
    x_in,
    c_in,
    label_in,
    gain1,
    bias1,
    gain2,
    bias2,
    qkv_w,
    qkv_b,
    out_w,
    up_w,
    up_b,
    down_w,
    end_bias,
    turn_in,
    full,
    vec_out,
    mixed_out,
    input_grad_out,
    x_all,
    c_all,
    grad_low,
    first_in,
    kv,
    q0,
    g0,
    heads_out,
    pair_grad,
    o_ext,
    u_w,
    d_w,
    part,
    up_acc,
    down_acc,
    grads,
    core_buf,
    chip_buf,
    label_buf,
    vec_buf,
    sends,
    recvs,
    own_sems,
    *halves,
):
    links = Links(dp_count, sends, recvs)
    rank = links.seq
    places, width = x_in.shape
    length = x_all.shape[0]
    heads = o_ext.shape[0] // PAIR
    hidden = u_w.shape[1]
    pieces = places // CHUNK
    score_scale = 1.0 / math.sqrt(E)

    loads = [
        (up_w.at[:, aligned(rank * hidden, hidden)], u_w),
        (down_w.at[aligned(rank * hidden, hidden)], d_w),
        (x_in, x_all.at[aligned(rank * places, places)]),
        (c_in, c_all.at[aligned(rank * places, places)]),
    ]
    loads += [
        (out_w.at[aligned((rank * heads + h) * E, E)], o_ext.at[pl.ds(h * PAIR + E, E)]) for h in range(heads)
    ]
    loads = [pltpu.make_async_copy(source, target, own_sems.at[i]) for i, (source, target) in enumerate(loads)]
    for copy in loads:
        copy.start()
    links.barrier()

    def rows_of(owner, piece):
        return aligned(owner * places + piece * CHUNK, CHUNK)

    def spread(piece):
        copies = []
        for source, target in ((x_in, x_all), (c_in, c_all)):
            mine = source.at[pl.ds(piece * CHUNK, CHUNK)]
            own = target.at[rows_of(rank, piece)]
            copies.append(links.send(mine, own, links.over("seq", CHIP)))
            copies.append(links.send(mine, own, links.over("seq", CORE)))
        return copies

    def pass_on(piece):
        copies = []
        for target in (x_all, c_all):
            held = target.at[rows_of(flip(rank, CHIP), piece)]
            copies.append(links.send(held, held, links.over("seq", CORE)))
        return copies

    label_buf[0] = label_in[...]
    counting = add_up_everywhere(links, [("dp", bit) for bit in links.dp_bits], label_buf)
    next(counting)
    spreads = [spread(piece) for piece in range(pieces)]
    for h in range(heads):
        o_ext[pl.ds(h * PAIR, E), :] = jnp.zeros((E, width), bf16)
    up_acc[...] = jnp.zeros_like(up_acc)
    down_acc[...] = jnp.zeros_like(down_acc)
    vec_buf[0] = jnp.zeros(vec_buf.shape[1:], f32)
    for _ in counting:
        pass
    count = jnp.sum(label_buf[2 * len(links.dp_bits)] * label_in[...], axis=1, keepdims=True)[:1]
    weight = dp_count / (TISSUES * count)
    for copy in loads:
        copy.wait()

    def add_vec(row, value):
        vec_buf[0, pl.ds(row, 1), :] += value

    def total(value):
        return jnp.sum(value, axis=0, keepdims=True)

    def chunk(start):
        rows = aligned(start, CHUNK)
        normed, _ = normalise(x_all[rows, :].astype(f32))
        first = (normed * gain1[...] + bias1[...]).astype(bf16)
        second = (normed * gain2[...] + bias2[...]).astype(bf16)
        first_in[rows, :] = first
        low = (c_all[rows, :].astype(f32) * weight).astype(bf16)
        grad_low[rows, :] = low
        add_vec(4, total(low.astype(f32)) * (places / length))

        joint = dot(first, qkv_w[...], NN) + qkv_b[...]
        turn = turn_in[rows, :]
        cosine, sine = turn[:, :PAIR], turn[:, PAIR:]
        back = dot(low, o_ext[...], NT)
        for h in range(heads):
            pair = joint[:, h * PAIR : (h + 1) * PAIR]
            kv[h, rows, :] = (pair * cosine + swapped(pair) * sine).astype(bf16)
            pair = joint[:, (heads + h) * PAIR : (heads + h + 1) * PAIR]
            pair = (pair * cosine + swapped(pair) * sine).astype(bf16).astype(f32) * score_scale
            q0[h, rows, :] = pair.astype(bf16)
            g0[h, rows, :] = back[:, h * PAIR : (h + 1) * PAIR].astype(bf16)

        pre = dot(second, u_w[...], NN) + up_b[pl.ds(rank, 1), :]
        gate = 0.5 * (1.0 + lax.erf(pre * (1.0 / math.sqrt(2.0))))
        act = (pre * gate).astype(bf16)
        slope = gate + pre * jnp.exp(-0.5 * pre * pre) * (1.0 / math.sqrt(2.0 * math.pi))
        part[0, rows, :] = dot(act, d_w[...], NN).astype(bf16)
        pre_grad = (dot(low, d_w[...], NT) * slope).astype(bf16)
        add_vec(5 + rank, total(pre_grad.astype(f32)))
        second_grad = dot(pre_grad, u_w[...], NT)
        part[1, rows, :] = (second_grad * gain2[...]).astype(bf16)
        add_vec(2, total(second_grad * normed))
        add_vec(3, total(second_grad))
        up_acc[...] += dot(second, pre_grad, TN)
        down_acc[...] += dot(act, low, TN)

    def chunks(starts):
        def one(index, _):
            start = starts[0]
            for number in range(1, len(starts)):
                start = jnp.where(index == number, starts[number], start)
            chunk(start)
            return 0

        lax.fori_loop(0, len(starts), one, 0)

    def starts_of(owner):
        return [owner * places + piece * CHUNK for piece in range(pieces)]

    chunks(starts_of(rank))
    for piece in range(pieces):
        spreads[piece][1].wait()
        spreads[piece][3].wait()
    chunks(starts_of(flip(rank, CORE)))
    far, beside = flip(rank, CHIP), flip(flip(rank, CHIP), CORE)
    for piece in range(pieces):
        spreads[piece][0].wait()
        spreads[piece][2].wait()
        onward = pass_on(piece)
        for copy in onward:
            copy.wait()
        chunks([far * places + piece * CHUNK, beside * places + piece * CHUNK])

    rows_in_group = grads.shape[1]
    real_rows = 2 * width // (GROUPS - 2)
    orders = orders_for(dp_count)

    def one_group(group):
        scatter, collect = orders[group]
        held, start, size = grads.at[group], 0, rows_in_group
        for number, bit in enumerate(scatter):
            size //= 2
            mine = bit_at(links.dp, bit)
            keep = aligned(mine * size, size)
            give = aligned((1 - mine) * size, size)
            arrived = halves[number].at[group]
            copy = links.send(held.at[give], arrived, links.over("dp", bit))
            yield
            copy.wait()
            arrived[...] = (held[keep, :].astype(f32) + arrived[...].astype(f32)).astype(bf16)
            held, start = arrived, start + mine * size
        owners = [rank]

        def region(owner):
            return full.at[owner, group, aligned(start, size)]

        own = pltpu.make_async_copy(held, region(rank), own_sems.at[len(loads) + group])
        own.start()
        yield
        own.wait()
        for axis, bit in collect:
            partner = links.over(axis, bit)
            copies = [links.send(region(owner), region(owner), partner) for owner in owners]
            yield
            for copy in copies:
                copy.wait()
            if axis == "dp":
                start = start - bit_at(links.dp, bit) * size
                size *= 2
            else:
                owners = owners + [flip(owner, bit) for owner in owners]

    def one_part(which):
        core, chip = bit_at(rank, CORE), bit_at(rank, CHIP)
        copies = [
            links.send(
                part.at[which, aligned((2 * at + 1 - core) * places, places)],
                core_buf.at[which, at],
                links.over("seq", CORE),
            )
            for at in range(2)
        ]
        yield
        for at in range(2):
            copies[at].wait()
            own = part[which, aligned((2 * at + core) * places, places), :].astype(f32)
            core_buf[which, at] = (own + core_buf[which, at].astype(f32)).astype(bf16)
        copy = links.send(core_buf.at[which, 1 - chip], chip_buf.at[which], links.over("seq", CHIP))
        yield
        yield
        yield
        copy.wait()
        chip_buf[which] = (core_buf[which, chip].astype(f32) + chip_buf[which].astype(f32)).astype(bf16)

    turns = Turns()
    for group in range(4):
        source = (up_acc, down_acc)[group // 2]
        grads[group, pl.ds(0, real_rows), :] = source[pl.ds(group % 2 * real_rows, real_rows), :].astype(bf16)
        if rows_in_group > real_rows:
            grads[group, pl.ds(real_rows, rows_in_group - real_rows), :] = jnp.zeros(
                (rows_in_group - real_rows, width), bf16
            )
        turns.add([one_group(group)])
        turns.step(1)

    blocks = length // CHUNK
    for h in range(heads):

        def kvt(block):
            third = width // CHUNK
            return up_acc.at[pl.ds(block // third * PAIR, PAIR), pl.ds(block % third * CHUNK, CHUNK)]

        for i in range(blocks):
            own = pl.ds(i * CHUNK, CHUNK)
            q, g = q0[h, own, :], g0[h, own, :]
            spans = ([(0, i * CHUNK)] if i else []) + [(i * CHUNK, CHUNK)]
            scores = [dot(q, kv[h, pl.ds(at, size), :], NT) for at, size in spans]
            row = lax.broadcasted_iota(jnp.int32, (CHUNK, CHUNK), 0)
            column = lax.broadcasted_iota(jnp.int32, (CHUNK, CHUNK), 1)
            scores[-1] = jnp.where(column <= row, scores[-1], masked_score)
            largest = functools.reduce(jnp.maximum, [jnp.max(s, axis=1, keepdims=True) for s in scores])
            probs = [jnp.exp(s - largest) for s in scores]
            inverse = 1.0 / sum(jnp.sum(p, axis=1, keepdims=True) for p in probs)
            probs = [p * inverse for p in probs]
            lows = [p.astype(bf16) for p in probs]
            attended = sum(dot(low, kv[h, pl.ds(at, size), :], NN) for low, (at, size) in zip(lows, spans))
            heads_out[own, pl.ds(h * PAIR, PAIR)] = attended.astype(bf16)
            delta = jnp.sum(attended * g.astype(f32), axis=1, keepdims=True)
            grads_s = [
                (p * (dot(g, kv[h, pl.ds(at, size), :], NT) - delta)).astype(bf16)
                for p, (at, size) in zip(probs, spans)
            ]
            q_grad = sum(dot(s, kv[h, pl.ds(at, size), :], NN) for s, (at, size) in zip(grads_s, spans)) * score_scale
            turn = turn_in[own, :]
            q_grad = q_grad * turn[:, :PAIR] - swapped(q_grad) * turn[:, PAIR:]
            pair_grad[own, pl.ds((heads + h) * PAIR, PAIR)] = q_grad.astype(bf16)
            for s, low, (at, size) in zip(grads_s, lows, spans):
                term = dot(q, s, TN) + dot(g, low, TN)
                for block in range(size // CHUNK):
                    piece = term[:, block * CHUNK : (block + 1) * CHUNK]
                    if at // CHUNK + block == i:
                        kvt(i)[...] = piece
                    else:
                        kvt(at // CHUNK + block)[...] += piece
            turns.step(1)
        for block in range(blocks):
            rows = pl.ds(block * CHUNK, CHUNK)
            turn = turn_in[rows, :]
            pair = jnp.transpose(kvt(block)[...])
            pair = pair * turn[:, :PAIR] - swapped(pair) * turn[:, PAIR:]
            pair_grad[rows, pl.ds(h * PAIR, PAIR)] = pair.astype(bf16)

    tile = 128
    for at in range(width // tile):
        rows = pl.ds(at * tile, tile)
        qkv_term = dot(first_in[:, rows], pair_grad[...], TN)
        out_term = dot(grad_low[:, rows], heads_out[...], TN)
        lane = lax.broadcasted_iota(jnp.int32, out_term.shape, 1)
        tail = jnp.where(lane % PAIR < E, qkv_term[:, heads * PAIR :], out_term)
        group, offset = 4 + at * tile // real_rows, at * tile % real_rows
        grads[group, pl.ds(offset, tile), pl.ds(0, heads * PAIR)] = qkv_term[:, : heads * PAIR].astype(bf16)
        grads[group, pl.ds(offset, tile), pl.ds(heads * PAIR, heads * PAIR)] = tail.astype(bf16)
        turns.step(1)
    for group in range(4, 6):
        if rows_in_group > real_rows:
            grads[group, pl.ds(real_rows, rows_in_group - real_rows), :] = jnp.zeros(
                (rows_in_group - real_rows, width), bf16
            )
        turns.add([one_group(group)])
        turns.step(1)

    def last(start):
        rows = aligned(start, CHUNK)
        normed, _ = normalise(x_all[rows, :].astype(f32))
        attn = dot(heads_out[rows, :], o_ext[...], NN)
        part[0, rows, :] = (part[0, rows, :].astype(f32) + attn).astype(bf16)
        pairs = pair_grad[rows, :]
        first_grad = dot(pairs, qkv_w[...], NT)
        part[1, rows, :] = (part[1, rows, :].astype(f32) + first_grad * gain1[...]).astype(bf16)
        add_vec(0, total(first_grad * normed))
        add_vec(1, total(first_grad))
        add_vec(9 + rank, total(pairs.astype(f32)))

    def last_loop(index, _):
        last(index * CHUNK)
        return 0

    lax.fori_loop(0, length // CHUNK, last_loop, 0)
    turns.add([one_part(0), one_part(1)])
    vec_steps = [("seq", CORE), ("seq", CHIP)] + [("dp", bit) for bit in links.dp_bits]
    turns.add([add_up_everywhere(links, vec_steps, vec_buf)])
    turns.finish()

    vec_out[...] = vec_buf[2 * len(vec_steps)]
    for piece in range(pieces):
        rows = pl.ds(piece * CHUNK, CHUNK)
        own_rows = rows_of(rank, piece)
        x = x_all[own_rows, :].astype(f32)
        mixed_out[rows, :] = (x + chip_buf[0, rows, :].astype(f32) + end_bias[...]).astype(bf16)
        normed, inverse = normalise(x)
        scaled = chip_buf[1, rows, :].astype(f32)
        rows_grad = inverse * (
            scaled
            - jnp.mean(scaled, axis=-1, keepdims=True)
            - normed * jnp.mean(scaled * normed, axis=-1, keepdims=True)
        )
        input_grad_out[rows, :] = c_all[own_rows, :].astype(f32) * weight + rows_grad


def layer(dp_count, seq_count, *operands):
    places, width = operands[0].shape
    length = places * seq_count
    heads = H // seq_count
    hidden = operands[10].shape[1] // seq_count
    bits = bits_of(dp_count)
    real_rows = 2 * width // (GROUPS - 2)
    rows = -(-real_rows // (16 * dp_count)) * 16 * dp_count
    pieces = places // CHUNK
    copies = bits + 6 * pieces + GROUPS * (bits + 2 * bits + 3) + 6 + bits + 2
    scratch = [
        pltpu.VMEM((length, width), bf16),
        pltpu.VMEM((length, width), bf16),
        pltpu.VMEM((length, width), bf16),
        pltpu.VMEM((length, width), bf16),
        pltpu.VMEM((heads, length, PAIR), bf16),
        pltpu.VMEM((heads, length, PAIR), bf16),
        pltpu.VMEM((heads, length, PAIR), bf16),
        pltpu.VMEM((length, heads * PAIR), bf16),
        pltpu.VMEM((length, 2 * heads * PAIR), bf16),
        pltpu.VMEM((heads * PAIR, width), bf16),
        pltpu.VMEM((width, hidden), bf16),
        pltpu.VMEM((hidden, width), bf16),
        pltpu.VMEM((2, length, width), bf16),
        pltpu.VMEM((width, hidden), f32),
        pltpu.VMEM((hidden, width), f32),
        pltpu.VMEM((GROUPS, rows, width), bf16),
        pltpu.VMEM((2, 2, places, width), bf16),
        pltpu.VMEM((2, places, width), bf16),
        pltpu.VMEM((2 * bits + 1, 8, 128), f32),
        pltpu.VMEM((2 * (bits + 2) + 1, VECTOR_ROWS, width), f32),
        pltpu.SemaphoreType.DMA((copies,)),
        pltpu.SemaphoreType.DMA((copies,)),
        pltpu.SemaphoreType.DMA((4 + heads + GROUPS,)),
    ]
    scratch += [pltpu.VMEM((GROUPS, rows >> (j + 1), width), bf16) for j in range(bits)]
    return pl.pallas_call(
        functools.partial(layer_kernel, dp_count),
        out_shape=(
            jax.ShapeDtypeStruct((seq_count, GROUPS, rows, width), bf16),
            jax.ShapeDtypeStruct((VECTOR_ROWS, width), f32),
            jax.ShapeDtypeStruct((places, width), bf16),
            jax.ShapeDtypeStruct((places, width), f32),
        ),
        in_specs=[ANY, ANY] + [VMEM] * 7 + [ANY, ANY, VMEM, ANY, VMEM, VMEM],
        out_specs=(ANY, VMEM, VMEM, VMEM),
        scratch_shapes=scratch,
        compiler_params=pltpu.CompilerParams(
            collective_id=0, has_side_effects=True, vmem_limit_bytes=62 * 2**20
        ),
        name="layer",
    )(*operands)


def finish_kernel(up_in, down_in, mix_in, vec, up_out, down_out, qkv_out, out_out, *vectors):
    owner = pl.program_id(1)
    up_out[...] = up_in[0, 0].astype(f32)
    down_out[...] = down_in[0, 0].astype(f32)
    owners, _, _, width = mix_in.shape
    heads = H // owners
    half = heads * PAIR

    @pl.when(owner == 0)
    def _():
        for r in range(owners):
            block = mix_in[r, 0].astype(f32)
            for h in range(heads):
                head = r * heads + h
                pair = block[:, h * PAIR : (h + 1) * PAIR]
                tail = block[:, half + h * PAIR : half + (h + 1) * PAIR]
                qkv_out[:, pl.ds(head * E, E)] = tail[:, :E]
                qkv_out[:, pl.ds((H + head) * E, E)] = pair[:, :E]
                qkv_out[:, pl.ds((2 * H + head) * E, E)] = pair[:, E:]
                out_out[pl.ds(head * E, E), :] = jnp.transpose(tail)[E:, :]

    @pl.when((owner == 0) & (pl.program_id(0) == 0))
    def _():
        gain1, bias1, gain2, bias2, low, qkv, up = vectors
        for row, target in enumerate((gain1, bias1, gain2, bias2, low)):
            target[...] = vec[pl.ds(row, 1), :]
        for r in range(owners):
            up[:, pl.ds(r * width, width)] = vec[pl.ds(5 + r, 1), :]
            line = vec[pl.ds(5 + owners + r, 1), :]
            for h in range(heads):
                head = r * heads + h
                qkv[:, pl.ds(head * E, E)] = line[:, half + h * PAIR : half + h * PAIR + E]
                qkv[:, pl.ds((H + head) * E, E)] = line[:, h * PAIR : h * PAIR + E]
                qkv[:, pl.ds((2 * H + head) * E, E)] = line[:, h * PAIR + E : (h + 1) * PAIR]


def finish(full, vec):
    owners, groups, _, width = full.shape
    rows = 2 * width // (groups - 2)
    steps = width // rows
    line = jax.ShapeDtypeStruct((1, width), f32)
    line_spec = pl.BlockSpec((1, width), lambda m, r: (0, 0))
    return pl.pallas_call(
        finish_kernel,
        grid=(steps, owners),
        out_shape=(
            jax.ShapeDtypeStruct((width, owners * width), f32),
            jax.ShapeDtypeStruct((owners * width, width), f32),
            jax.ShapeDtypeStruct((width, 3 * H * E), f32),
            jax.ShapeDtypeStruct((H * E, width), f32),
        )
        + (line,) * 5
        + (jax.ShapeDtypeStruct((1, 3 * H * E), f32), jax.ShapeDtypeStruct((1, owners * width), f32)),
        in_specs=[
            pl.BlockSpec((1, 1, rows, width), lambda m, r: (r, m, 0, 0)),
            pl.BlockSpec((1, 1, rows, width), lambda m, r: (r, steps + m, 0, 0)),
            pl.BlockSpec((owners, 1, rows, width), lambda m, r: (0, 2 * steps + m, 0, 0)),
            pl.BlockSpec(vec.shape, lambda m, r: (0, 0)),
        ],
        out_specs=(
            pl.BlockSpec((rows, width), lambda m, r: (m, r)),
            pl.BlockSpec((rows, width), lambda m, r: (r * steps + m, 0)),
            pl.BlockSpec((rows, 3 * H * E), lambda m, r: (m, 0)),
            pl.BlockSpec((H * E, rows), lambda m, r: (0, m)),
        )
        + (line_spec,) * 5
        + (
            pl.BlockSpec((1, 3 * H * E), lambda m, r: (0, 0)),
            pl.BlockSpec((1, owners * width), lambda m, r: (0, 0)),
        ),
        compiler_params=pltpu.CompilerParams(vmem_limit_bytes=48 * 2**20),
        name="finish",
    )(full, full, full, vec)


def turn_table(length):
    half = ROT // 2
    frequency = 10000.0 ** (-2.0 * jnp.arange(half, dtype=f32) / ROT)
    angles = jnp.arange(length, dtype=jnp.int32).astype(f32)[:, None] * frequency[None, :]
    cosine, sine = jnp.cos(angles), jnp.sin(angles)
    rest = PAIR - ROT
    return jnp.concatenate(
        [cosine, cosine, jnp.ones((length, rest), f32), -sine, sine, jnp.zeros((length, rest), f32)], axis=1
    )


def body(
    tokens,
    tissue,
    norm1_gain,
    norm1_bias,
    norm2_gain,
    norm2_bias,
    qkv_weight,
    qkv_bias,
    out_weight,
    out_bias,
    up_weight,
    up_bias,
    down_weight,
    down_bias,
    cotangent,
):
    dp_count, seq_count = lax.axis_size("dp"), lax.axis_size("seq")
    rank = lax.axis_index("seq")
    _, places, width = tokens.shape
    heads = H // seq_count

    labels = lax.broadcasted_iota(jnp.int32, (8, 128), 1)
    own_label = (labels == tissue[0]).astype(f32)

    def in_pairs(array):
        query, key, value = [
            lax.dynamic_slice_in_dim(array, (part * H + rank * heads) * E, heads * E, 1) for part in range(3)
        ]
        empty = jnp.zeros((array.shape[0], E), array.dtype)
        columns = []
        for h in range(heads):
            columns += [key[:, h * E : (h + 1) * E], value[:, h * E : (h + 1) * E]]
        for h in range(heads):
            columns += [query[:, h * E : (h + 1) * E], empty]
        return jnp.concatenate(columns, axis=1)

    full, vec, mixed, input_grad = layer(
        dp_count,
        seq_count,
        tokens.reshape(places, width),
        cotangent.reshape(places, width),
        own_label,
        norm1_gain[None],
        norm1_bias[None],
        norm2_gain[None],
        norm2_bias[None],
        in_pairs(qkv_weight),
        in_pairs(qkv_bias[None]),
        out_weight,
        up_weight,
        up_bias.reshape(seq_count, -1),
        down_weight,
        (out_bias + down_bias)[None],
        turn_table(places * seq_count),
    )
    up, down, qkv, out, gain1, bias1, gain2, bias2, low, qkv_b, up_b = finish(full, vec)
    flat = lambda a: a.reshape(-1)
    return (
        mixed.reshape(tokens.shape),
        input_grad.reshape(tokens.shape),
        flat(gain1),
        flat(bias1),
        flat(gain2),
        flat(bias2),
        qkv,
        flat(qkv_b),
        out,
        flat(low),
        up,
        flat(up_b),
        down,
        flat(low),
    )


def solution(mesh):
    rows = P("dp", "seq", None)
    return jax.shard_map(
        body,
        mesh=mesh,
        in_specs=(rows, P("dp")) + (P(),) * 12 + (rows,),
        out_specs=(rows, rows) + (P(),) * 12,
        check_vma=False,
    )
```

```python
import functools
import math

import jax
import jax.numpy as jnp
import numpy as np
from jax import lax
from jax.experimental import pallas as pl
from jax.experimental.pallas import tpu as pltpu
from jax.sharding import PartitionSpec as P

H = 12
E = 64
ROT = 16
TISSUES = 16
norm_eps = 1e-05
masked_score = -1e30
f32 = jnp.float32
bf16 = jnp.bfloat16
MESH = pl.DeviceIdType.MESH
ANY = pl.BlockSpec(memory_space=pl.ANY)
VMEM = pl.BlockSpec(memory_space=pltpu.VMEM)
VECTOR_ROWS = 16
CORE, CHIP = 1, 2
PAIR = 2 * E
CHUNK = 256

NN = ((1,), (0,))
NT = ((1,), (1,))
TN = ((0,), (0,))


def dot(a, b, dims):
    return lax.dot_general(a, b, (dims, ((), ())), preferred_element_type=f32)


def bits_of(count):
    return count.bit_length() - 1


def bit_at(index, bit):
    return lax.div(index, bit) % 2


def flip(index, bit):
    return index + bit - 2 * bit * bit_at(index, bit)


def aligned(start, size):
    return pl.ds(pl.multiple_of(start, size), size)


class Links:
    def __init__(self, dp_count, send_sems, recv_sems):
        self.dp = lax.axis_index("dp")
        self.seq = lax.axis_index("seq")
        self.dp_bits = [1 << j for j in range(bits_of(dp_count))]
        self.send_sems, self.recv_sems, self.used = send_sems, recv_sems, 0

    def over(self, axis, bit):
        if axis == "seq":
            return (self.dp, flip(self.seq, bit))
        return (flip(self.dp, bit), self.seq)

    def barrier(self):
        semaphore = pltpu.get_barrier_semaphore()
        partners = [self.over("seq", CORE), self.over("seq", CHIP)]
        partners += [self.over("dp", bit) for bit in self.dp_bits]
        for partner in partners:
            pl.semaphore_signal(semaphore, inc=1, device_id=partner, device_id_type=MESH)
        pl.semaphore_wait(semaphore, len(partners))

    def send(self, source, target, partner):
        copy = pltpu.make_async_remote_copy(
            src_ref=source,
            dst_ref=target,
            send_sem=self.send_sems.at[self.used],
            recv_sem=self.recv_sems.at[self.used],
            device_id=partner,
            device_id_type=MESH,
        )
        self.used += 1
        copy.start()
        return copy


def add_up_everywhere(links, steps, buffer):
    for number, (axis, bit) in enumerate(steps):
        copy = links.send(buffer.at[0], buffer.at[number + 1], links.over(axis, bit))
        yield
        copy.wait()
        buffer[0] = buffer[0] + buffer[number + 1]


def axes_of(word):
    return [("seq", CHIP) if letter == "x" else ("dp", 1 << "yzw".index(letter)) for letter in word]


def plain_order(dp_count, blocks):
    scatter = [("dp", 1 << j) for j in range(bits_of(dp_count))]
    collect = [("seq", CHIP)] + scatter[::-1]
    return (scatter + ([("seq", CHIP)] if blocks == 2 else []), collect)


def orders_of(dp_count, plan, blocks, few):
    if dp_count == 8:
        return [(axes_of(scatter), axes_of(collect)) for scatter, collect in plan]
    return [plain_order(dp_count, blocks)] * few


MLP_PLAN = [
    ("yzwx", "wzxy"),
    ("zwyx", "ywzx"),
    ("yxzw", "xwzy"),
    ("xyzw", "wzyx"),
    ("yzwx", "wzxy"),
    ("yzxw", "wzxy"),
    ("xzwy", "ywzx"),
    ("zywx", "wyzx"),
    ("zyxw", "wxyz"),
    ("zxyw", "wxyz"),
    ("yzwx", "wzxy"),
    ("yxzw", "wzxy"),
]
HEAD_PLAN = [
    ("zyw", "wyxz"),
    ("zwy", "yxwz"),
    ("yzw", "wzxy"),
    ("yzw", "wzyx"),
    ("yzw", "xwzy"),
    ("yzw", "xwzy"),
]
AGENDA = [
    (28.7, "m1"),
    (32.4, "m0"),
    (41.2, "m1"),
    (41.6, "m2"),
    (45.3, "m0"),
    (45.4, "m7"),
    (46.0, "m4"),
    (47.3, "m5"),
    (47.4, "m8"),
    (47.8, "m9"),
    (48.6, "m1"),
    (50.4, "m0"),
    (51.4, "m2"),
    (51.7, "m10"),
    (52.5, "m11"),
    (52.6, "m3"),
    (53.3, "m4"),
    (53.4, "m1"),
    (53.7, "m1"),
    (53.7, "m6"),
    (54.0, "m5"),
    (54.3, "m7"),
    (54.5, "m0"),
    (54.8, "m0"),
    (55.0, "m8"),
    (55.5, "m9"),
    (56.0, "m2"),
    (57.9, "m1"),
    (58.0, "m3"),
    (59.2, "m9"),
    (60.7, "m10"),
    (61.0, "m5"),
    (61.3, "m4"),
    (61.5, "m11"),
    (61.8, "m8"),
    (63.4, "m7"),
    (64.4, "m0"),
    (65.3, "m4"),
    (65.4, "m2"),
    (65.6, "m4"),
    (65.7, "m2"),
    (67.7, "m7"),
    (68.0, "m7"),
    (68.6, "m9"),
    (68.9, "m9"),
    (70.4, "m10"),
    (70.4, "m2"),
    (70.4, "m5"),
    (70.7, "m5"),
    (70.9, "m8"),
    (71.2, "m8"),
    (71.7, "a2"),
    (72.2, "a3"),
    (72.2, "m3"),
    (72.8, "m1"),
    (74.2, "m4"),
    (74.9, "m10"),
    (75.2, "m10"),
    (76.3, "m11"),
    (77.4, "m7"),
    (78.8, "m9"),
    (79.7, "m0"),
    (79.8, "m6"),
    (80.1, "m2"),
    (81.0, "a0"),
    (81.1, "m5"),
    (81.6, "m8"),
    (81.7, "a1"),
    (81.9, "m3"),
    (82.2, "m3"),
    (83.1, "m7"),
    (83.8, "a4"),
    (83.8, "m10"),
    (84.1, "m11"),
    (84.4, "m11"),
    (84.8, "a5"),
    (85.4, "a0"),
    (85.6, "m9"),
    (86.2, "a2"),
    (86.7, "a3"),
    (88.2, "m4"),
    (88.6, "m8"),
    (90.1, "m9"),
    (90.6, "m0"),
    (92.5, "m3"),
    (93.5, "m8"),
    (95.8, "m11"),
    (96.0, "m6"),
    (96.3, "a0"),
    (96.4, "m2"),
    (96.6, "a0"),
    (97.2, "a2"),
    (97.2, "m4"),
    (97.5, "a2"),
    (97.6, "m0"),
    (97.7, "a3"),
    (97.9, "m5"),
    (98.0, "a3"),
    (98.9, "a1"),
    (100.2, "m6"),
    (100.5, "m6"),
    (100.8, "m0"),
    (101.2, "m10"),
    (101.5, "a4"),
    (102.1, "m1"),
    (102.5, "a5"),
    (104.4, "a1"),
    (104.7, "a1"),
    (105.4, "m5"),
    (105.9, "a0"),
    (106.4, "m6"),
    (106.7, "a2"),
    (107.1, "a3"),
    (107.7, "m3"),
    (109.0, "m2"),
    (109.4, "a4"),
    (109.7, "a4"),
    (109.7, "m10"),
    (109.7, "m11"),
    (110.3, "a5"),
    (110.6, "a5"),
    (110.8, "m4"),
    (111.3, "a1"),
    (111.3, "m7"),
    (112.3, "m2"),
    (112.4, "m1"),
    (114.0, "m4"),
    (114.3, "a4"),
    (114.6, "a0"),
    (115.0, "m9"),
    (115.6, "m1"),
    (116.0, "a5"),
    (116.0, "m8"),
    (116.2, "m6"),
    (116.3, "a2"),
    (116.4, "a3"),
    (117.8, "a1"),
    (118.1, "m11"),
    (118.2, "m9"),
    (119.3, "m8"),
    (119.4, "a4"),
    (119.9, "m5"),
    (121.6, "m3"),
    (121.9, "a5"),
    (123.1, "m5"),
    (123.4, "a0"),
    (123.7, "m10"),
    (125.0, "a2"),
    (126.4, "m7"),
    (126.9, "m10"),
    (127.5, "a1"),
    (127.5, "a3"),
    (128.8, "a4"),
    (128.8, "m11"),
    (129.6, "m7"),
    (129.7, "m3"),
    (130.9, "m6"),
    (131.8, "a5"),
    (132.1, "m11"),
    (133.0, "m3"),
    (133.7, "a2"),
    (135.2, "a3"),
    (136.9, "a2"),
    (137.0, "a0"),
    (138.2, "a1"),
    (138.4, "a3"),
    (138.6, "m6"),
    (139.5, "a4"),
    (140.2, "a0"),
    (141.2, "a5"),
    (141.8, "a1"),
    (142.6, "m6"),
    (143.1, "a4"),
    (144.4, "a5"),
]


class Turns:
    def __init__(self, agenda):
        self.agenda, self.tasks, self.left = list(agenda), {}, []

    def add(self, name, task):
        self.tasks[name] = task
        self.advance(name)

    def advance(self, name):
        task = self.tasks.get(name)
        if task is not None and next(task, "done") == "done":
            del self.tasks[name]

    def until(self, when):
        if not self.agenda:
            return
        while self.agenda and self.agenda[0][0] <= when:
            self.advance(self.agenda.pop(0)[1])

    def step(self):
        if not self.agenda and self.tasks:
            name = next(iter(self.tasks))
            task = self.tasks.pop(name)
            if next(task, "done") != "done":
                self.tasks[name] = task

    def finish(self):
        while self.agenda:
            self.advance(self.agenda.pop(0)[1])
        while self.tasks:
            self.step()


def normalise(rows):
    centred = rows - jnp.mean(rows, axis=-1, keepdims=True)
    inverse = lax.rsqrt(jnp.mean(centred * centred, axis=-1, keepdims=True) + norm_eps)
    return centred * inverse, inverse


def lanes_of(shape):
    return lax.broadcasted_iota(jnp.int32, shape, 1)


def swapped(pairs):
    half = ROT // 2
    return jnp.where(
        lanes_of(pairs.shape) < half, pltpu.roll(pairs, PAIR - half, 1), pltpu.roll(pairs, half, 1)
    )


def head_columns(windows, odd, heads):
    def put(window, h, to):
        def at(place):
            block = window[:, place // 2 * PAIR : (place // 2 + 1) * PAIR]
            return block if place % 2 == to else pltpu.roll(block, E, 1)

        return jnp.where(odd == 1, at(h + 1), at(h))

    query, key, value = windows
    low = lanes_of((key.shape[0], PAIR)) < E
    blocks = []
    for h in range(heads):
        blocks.append(jnp.where(low, put(key, h, 0), put(value, h, 1)))
        blocks.append(jnp.where(low, put(query, h, 0), 0.0))
    return blocks


SMALL_ROWS = 16


def layer_kernel(
    dp_count,
    plans,
    agenda,
    x_in,
    c_in,
    tissue_in,
    small,
    qkv_w,
    out_w,
    up_w,
    down_w,
    turn_in,
    full_mlp,
    full_heads,
    vec_out,
    mixed_out,
    input_grad_out,
    x_all,
    c_all,
    low_t,
    first_t,
    kv,
    q0,
    g0,
    pairs,
    pairs_back,
    w_pairs,
    b_pairs,
    o_pairs,
    u_w,
    d_w,
    pre_grads,
    part,
    grads_mlp,
    grads_heads,
    core_buf,
    kvt,
    label_buf,
    vec_buf,
    sends,
    recvs,
    own_sems,
    *halves,
):
    links = Links(dp_count, sends, recvs)
    rank = links.seq
    chip, core = bit_at(rank, CHIP), bit_at(rank, CORE)
    places, width = x_in.shape
    length = x_all.shape[0]
    local = length // 2
    heads = kv.shape[0]
    hidden = u_w.shape[2]
    pieces = places // CHUNK
    score_scale = 1.0 / math.sqrt(E)
    ranks = (rank, flip(rank, CHIP))
    turns = Turns(agenda)

    loads = [
        (x_in, x_all.at[aligned(rank * places, places)]),
        (c_in, c_all.at[aligned(rank * places, places)]),
    ]
    for at in range(2):
        for which in range(3):
            start = which * H * E + lax.div(heads * ranks[at], 2) * PAIR
            loads.append(
                (
                    qkv_w.at[:, pl.ds(pl.multiple_of(start, PAIR), 2 * PAIR)],
                    part.at[at, pl.ds(0, width), pl.ds(which * 2 * PAIR, 2 * PAIR)],
                )
            )
    for at in range(2):
        loads.append((up_w.at[:, aligned(ranks[at] * hidden, hidden)], u_w.at[at]))
        loads.append((down_w.at[aligned(ranks[at] * hidden, hidden)], d_w.at[at]))
        for h in range(heads):
            loads.append(
                (out_w.at[aligned((ranks[at] * heads + h) * E, E)], o_pairs.at[at, pl.ds(h * PAIR + E, E)])
            )
    loads = [pltpu.make_async_copy(source, target, own_sems.at[i]) for i, (source, target) in enumerate(loads)]
    for copy in loads:
        copy.start()
    links.barrier()

    def rows_of(owner, piece):
        return aligned(owner * places + piece * CHUNK, CHUNK)

    def spread(piece):
        copies = []
        for source, target in ((x_in, x_all), (c_in, c_all)):
            mine = source.at[pl.ds(piece * CHUNK, CHUNK)]
            own = target.at[rows_of(rank, piece)]
            copies.append(links.send(mine, own, links.over("seq", CHIP)))
            copies.append(links.send(mine, own, links.over("seq", CORE)))
        return copies

    def pass_on(piece):
        copies = []
        for target in (x_all, c_all):
            held = target.at[rows_of(flip(rank, CHIP), piece)]
            copies.append(links.send(held, held, links.over("seq", CORE)))
        return copies

    own_label = (lanes_of((8, 128)) == tissue_in[0]).astype(f32)
    label_buf[0] = own_label
    counting = add_up_everywhere(links, [("dp", bit) for bit in links.dp_bits], label_buf)
    next(counting)
    spreads = [spread(piece) for piece in range(pieces)]
    for at in range(2):
        for h in range(heads):
            o_pairs[at, pl.ds(h * PAIR, E), :] = jnp.zeros((E, width), bf16)
    vec_buf[0] = jnp.zeros(vec_buf.shape[1:], f32)
    for copy in loads:
        copy.wait()

    odd = heads * rank % 2
    for at in range(2):
        for tile in range(width // CHUNK):
            rows = pl.ds(tile * CHUNK, CHUNK)
            windows = [part[at, rows, pl.ds(which * 2 * PAIR, 2 * PAIR)].astype(f32) for which in range(3)]
            for number, block in enumerate(head_columns(windows, odd, heads)):
                w_pairs[at, rows, pl.ds(number * PAIR, PAIR)] = block.astype(bf16)
    start = pl.multiple_of(lax.div(heads * rank, 2) * PAIR, PAIR)
    windows = [small[pl.ds(9 + which, 1), pl.ds(start, 2 * PAIR)] for which in range(3)]
    for number, block in enumerate(head_columns(windows, odd, heads)):
        b_pairs[:, pl.ds(number * PAIR, PAIR)] = block

    for _ in counting:
        pass
    count = jnp.sum(label_buf[0] * own_label, axis=1, keepdims=True)[:1]
    weight = dp_count / (TISSUES * count)
    gain1, bias1, gain2, bias2, end_bias = [small[pl.ds(row, 1), :] for row in range(5)]

    def add_vec(row, value):
        vec_buf[0, pl.ds(row, 1), :] += value

    def total(value):
        return jnp.sum(value, axis=0, keepdims=True)

    def turn_of(half, rows):
        table = turn_in[rows, :]
        table = jnp.where(half == 1, pltpu.roll(table, PAIR - 2 * ROT, 1), table)
        lane = lanes_of(table.shape)
        cosine = jnp.where(lane < ROT, table, 1.0)
        sine = jnp.where(lane < ROT, pltpu.roll(table, PAIR - ROT, 1), 0.0)
        return cosine, sine

    second_kept = [(keep, h) for keep in (kv, q0) for h in range(heads)]

    def chunk(start, with_mlp):
        rows = aligned(start, CHUNK)
        normed, _ = normalise(x_all[rows, :].astype(f32))
        first = normed * gain1 + bias1
        first_t[:, rows] = jnp.transpose(first).astype(bf16)
        first = first.astype(bf16)
        low = c_all[rows, :].astype(f32) * weight
        low_t[:, rows] = jnp.transpose(low).astype(bf16)
        low = low.astype(bf16)

        joint = dot(first, w_pairs[0], NN) + b_pairs[...]
        half = lax.div(start, local)
        cosine, sine = turn_of(half, aligned(start - half * local, CHUNK))
        for h in range(heads):
            pair = joint[:, 2 * h * PAIR : (2 * h + 1) * PAIR]
            kv[h, rows, :] = (pair * cosine + swapped(pair) * sine).astype(bf16)
            pair = joint[:, (2 * h + 1) * PAIR : (2 * h + 2) * PAIR]
            pair = (pair * cosine + swapped(pair) * sine).astype(bf16).astype(f32) * score_scale
            q0[h, rows, :] = pair.astype(bf16)
            g0[h, rows, :] = dot(low, o_pairs[0, pl.ds(h * PAIR, PAIR), :], NT).astype(bf16)
        if not with_mlp:
            return

        c_all[rows, :] = low
        add_vec(4, total(low.astype(f32)) * (places / local))
        second = (normed * gain2 + bias2).astype(bf16)
        near = aligned(start - chip * local, CHUNK)
        for tile, (keep, h) in enumerate(second_kept):
            rest = aligned(start + (1 - 2 * chip) * local, CHUNK)
            keep[h, rest, :] = second[:, tile * PAIR : (tile + 1) * PAIR]
        branch, second_grad = 0.0, 0.0
        for at in range(2):
            pre = dot(second, u_w[at], NN) + small[pl.ds(5 + ranks[at], 1), :]
            gate = 0.5 * (1.0 + lax.erf(pre * (1.0 / math.sqrt(2.0))))
            act = (pre * gate).astype(bf16)
            slope = gate + pre * jnp.exp(-0.5 * pre * pre) * (1.0 / math.sqrt(2.0 * math.pi))
            branch += dot(act, d_w[at], NN)
            pre_grad = (dot(low, d_w[at], NT) * slope).astype(bf16)
            add_vec(5 + ranks[at], total(pre_grad.astype(f32)))
            second_grad += dot(pre_grad, u_w[at], NT)
            pairs[at, near, :] = act
            pre_grads[at, near, :] = pre_grad
        part[0, near, :] = branch.astype(bf16)
        part[1, near, :] = (second_grad * gain2).astype(bf16)
        add_vec(2, total(second_grad * normed))
        add_vec(3, total(second_grad))

    beside = flip(rank, CORE)

    def near_chunk(index, _):
        @pl.when(index == pieces)
        def _():
            for piece in range(pieces):
                spreads[piece][1].wait()
                spreads[piece][3].wait()

        owner = jnp.where(index < pieces, rank, beside)
        chunk(owner * places + index % pieces * CHUNK, True)
        return 0

    lax.fori_loop(0, 2 * pieces, near_chunk, 0)

    halves = list(halves)

    def one_group(held, full, group, order, own_sem, arrivals):
        scatter, collect = order
        blocks, size, _ = held.shape
        start = 0
        for axis, bit in scatter:
            arrived = arrivals.pop(0)
            partner = links.over(axis, bit)
            if axis == "seq":
                copy = links.send(held.at[pl.ds(1, 1)], arrived, partner)
                yield
                copy.wait()
                arrived[...] = (held[pl.ds(0, 1)].astype(f32) + arrived[...].astype(f32)).astype(bf16)
            else:
                size //= 2
                mine = bit_at(links.dp, bit)
                copy = links.send(held.at[:, aligned((1 - mine) * size, size)], arrived, partner)
                yield
                copy.wait()
                own = held[:, aligned(mine * size, size), :].astype(f32)
                arrived[...] = (own + arrived[...].astype(f32)).astype(bf16)
                start = start + mine * size
            held = arrived
        owners = [rank]

        def region(owner):
            return full.at[owner, group, aligned(start, size)]

        own = pltpu.make_async_copy(held.at[0], region(rank), own_sem)
        own.start()
        yield
        own.wait()
        for axis, bit in collect + [("seq", CORE)]:
            partner = links.over(axis, bit)
            copies = [links.send(region(owner), region(owner), partner) for owner in owners]
            yield
            for copy in copies:
                copy.wait()
            if axis == "dp":
                start = start - bit_at(links.dp, bit) * size
                size *= 2
            else:
                owners = owners + [flip(owner, bit) for owner in owners]

    mlp_plan, head_plan = plans

    def begin(name, grads, full, group, order, number):
        count = len(order[0])
        arrivals, halves[:count] = halves[:count], []
        turns.add(name, one_group(grads.at[group], full, group, order, own_sems.at[len(loads) + number], arrivals))

    def fill(grads, group, real):
        spare = grads.shape[2] - real
        if spare:
            blocks = grads.shape[1]
            grads[group, :, pl.ds(real, spare), :] = jnp.zeros((blocks, spare, grads.shape[3]), bf16)

    near_rows = aligned(chip * local, local)
    far_rows = aligned((1 - chip) * local, local)
    mlp_groups = len(mlp_plan)
    mlp_rows = 2 * width // mlp_groups
    for group in range(mlp_groups):
        first_tile = group % (mlp_groups // 2) * mlp_rows // PAIR
        for at in range(2):
            for tile in range(mlp_rows // PAIR):
                if group < mlp_groups // 2:
                    keep, h = second_kept[first_tile + tile]
                    term = dot(keep[h, far_rows, :], pre_grads[at], TN)
                else:
                    columns = pl.ds((first_tile + tile) * PAIR, PAIR)
                    term = dot(pairs[at, :, columns], c_all[near_rows, :], TN)
                grads_mlp[group, at, pl.ds(tile * PAIR, PAIR), :] = term.astype(bf16)
        fill(grads_mlp, group, mlp_rows)
        begin("m%d" % group, grads_mlp, full_mlp, group, mlp_plan[group], group)

    far, across = flip(rank, CHIP), flip(flip(rank, CHIP), CORE)
    for piece in range(pieces):
        turns.until(27 + 7 * piece)
        spreads[piece][0].wait()
        spreads[piece][2].wait()
        onward = pass_on(piece)

        def far_chunk(index, _):
            @pl.when(index == 1)
            def _():
                for copy in onward:
                    copy.wait()

            chunk(jnp.where(index == 0, far, across) * places + piece * CHUNK, False)
            return 0

        lax.fori_loop(0, 2, far_chunk, 0)

    blocks = length // CHUNK
    clock = 43.0

    def pair_rows(block):
        return block * CHUNK // local, pl.ds(block * CHUNK % local, CHUNK)

    back = []
    for h in range(heads):
        for i in range(blocks):
            own = pl.ds(i * CHUNK, CHUNK)
            half, rows = pair_rows(i)
            q, g = q0[h, own, :], g0[h, own, :]
            spans = ([(0, i * CHUNK)] if i else []) + [(i * CHUNK, CHUNK)]
            scores = [dot(q, kv[h, pl.ds(at, size), :], NT) for at, size in spans]
            row = lax.broadcasted_iota(jnp.int32, (CHUNK, CHUNK), 0)
            column = lanes_of((CHUNK, CHUNK))
            scores[-1] = jnp.where(column <= row, scores[-1], masked_score)
            largest = functools.reduce(jnp.maximum, [jnp.max(s, axis=1, keepdims=True) for s in scores])
            probs = [jnp.exp(s - largest) for s in scores]
            inverse = 1.0 / sum(jnp.sum(p, axis=1, keepdims=True) for p in probs)
            probs = [p * inverse for p in probs]
            lows = [p.astype(bf16) for p in probs]
            attended = sum(dot(low, kv[h, pl.ds(at, size), :], NN) for low, (at, size) in zip(lows, spans))
            delta = jnp.sum(attended * g.astype(f32), axis=1, keepdims=True)
            score_grads = [
                (p * (dot(g, kv[h, pl.ds(at, size), :], NT) - delta)).astype(bf16)
                for p, (at, size) in zip(probs, spans)
            ]
            q_grad = sum(dot(s, kv[h, pl.ds(at, size), :], NN) for s, (at, size) in zip(score_grads, spans))
            q_grad = q_grad * score_scale
            cosine, sine = turn_of(half, rows)
            q_grad = q_grad * cosine - swapped(q_grad) * sine
            tail = jnp.where(lanes_of(q_grad.shape) < E, q_grad, attended)
            pairs[half, rows, pl.ds((2 * h + 1) * PAIR, PAIR)] = tail.astype(bf16)
            for s, low, (at, size) in zip(score_grads, lows, spans):
                term = dot(q, s, TN) + dot(g, low, TN)
                if at:
                    kvt[:, pl.ds(at, size)] = term
                elif i == 0:
                    kvt[:, pl.ds(0, size)] = term
                else:
                    kvt[:, pl.ds(0, size)] += term
            clock += (i + 1) * 10.5 / 36
            turns.until(clock)
            turns.step()
        for i in range(blocks):
            own = pl.ds(i * CHUNK, CHUNK)
            half, rows = pair_rows(i)
            cosine, sine = turn_of(half, rows)
            pair = jnp.transpose(kvt[:, own])
            pair = pair * cosine - swapped(pair) * sine
            pairs[half, rows, pl.ds(2 * h * PAIR, PAIR)] = pair.astype(bf16)

        columns = pl.ds(2 * h * PAIR, 2 * PAIR)
        back.append(links.send(pairs.at[1 - chip, :, columns], pairs_back.at[:, columns], links.over("seq", CHIP)))

        head_groups = len(head_plan) // heads
        head_rows = width // head_groups
        for number in range(head_groups):
            group = h * head_groups + number
            rows = pl.ds(number * head_rows, head_rows)
            term = sum(
                dot(first_t[rows, pl.ds(half * local, local)], pairs[half, :, columns], NN) for half in range(2)
            )
            out_term = sum(
                dot(
                    low_t[rows, pl.ds(half * local, local)],
                    pairs[half, :, pl.ds((2 * h + 1) * PAIR, PAIR)],
                    NN,
                )
                for half in range(2)
            )
            tail = jnp.where(lanes_of(out_term.shape) < E, term[:, PAIR:], out_term)
            grads_heads[group, 0, pl.ds(0, head_rows), pl.ds(0, PAIR)] = term[:, :PAIR].astype(bf16)
            grads_heads[group, 0, pl.ds(0, head_rows), pl.ds(PAIR, PAIR)] = tail.astype(bf16)
            fill(grads_heads, group, head_rows)
            begin("a%d" % group, grads_heads, full_heads, group, head_plan[group], mlp_groups + group)
        clock += 0.7

    add_vec(9 + rank, total(pairs[0].astype(f32)) + total(pairs[1].astype(f32)))
    turns.until(clock + 4.0)
    for copy in back:
        copy.wait()

    def last(owner, piece):
        near = aligned((owner - chip * 2) * places + piece * CHUNK, CHUNK)
        normed, _ = normalise(x_all[aligned(owner * places + piece * CHUNK, CHUNK), :].astype(f32))
        own, other = pairs[chip, near, :], pairs_back[near, :]
        attn = 0.0
        for h in range(heads):
            tail = slice((2 * h + 1) * PAIR, (2 * h + 2) * PAIR)
            attn += dot(own[:, tail], o_pairs[0, pl.ds(h * PAIR, PAIR), :], NN)
            attn += dot(other[:, tail], o_pairs[1, pl.ds(h * PAIR, PAIR), :], NN)
        first_grad = dot(own, w_pairs[0], NT) + dot(other, w_pairs[1], NT)
        part[0, near, :] = (part[0, near, :].astype(f32) + attn).astype(bf16)
        part[1, near, :] = (part[1, near, :].astype(f32) + first_grad * gain1).astype(bf16)
        add_vec(0, total(first_grad * normed))
        add_vec(1, total(first_grad))

    def last_loop(owner):
        def one(piece, _):
            last(owner, piece)
            return 0

        lax.fori_loop(0, pieces, one, 0)

    last_loop(beside)
    given = part.at[:, aligned((1 - core) * places, places)]
    crossing = links.send(given, core_buf, links.over("seq", CORE))
    turns.until(clock + 8.0)
    last_loop(rank)
    vec_steps = [("seq", CORE), ("seq", CHIP)] + [("dp", bit) for bit in links.dp_bits]
    turns.add("vec", add_up_everywhere(links, vec_steps, vec_buf))
    turns.until(clock + 12.0)

    reload = pltpu.make_async_copy(c_in, c_all.at[aligned(rank * places, places)], own_sems.at[0])
    reload.start()
    crossing.wait()
    reload.wait()
    for piece in range(pieces):
        rows = pl.ds(piece * CHUNK, CHUNK)
        own_rows = rows_of(rank, piece)
        near = aligned(core * places + piece * CHUNK, CHUNK)
        x = x_all[own_rows, :].astype(f32)
        sums = [part[which, near, :].astype(f32) + core_buf[which, rows, :].astype(f32) for which in range(2)]
        mixed_out[rows, :] = (x + sums[0] + end_bias).astype(bf16)
        normed, inverse = normalise(x)
        scaled = sums[1]
        rows_grad = inverse * (
            scaled
            - jnp.mean(scaled, axis=-1, keepdims=True)
            - normed * jnp.mean(scaled * normed, axis=-1, keepdims=True)
        )
        input_grad_out[rows, :] = c_all[own_rows, :].astype(f32) * weight + rows_grad
    turns.finish()
    vec_out[...] = vec_buf[0]


def padded(rows, dp_count):
    return -(-rows // (16 * dp_count)) * 16 * dp_count


def arrivals_of(order, blocks, rows, width):
    shapes = []
    for axis, _ in order[0]:
        if axis == "seq":
            blocks = 1
        else:
            rows //= 2
        shapes.append(pltpu.VMEM((blocks, rows, width), bf16))
    return shapes


def layer(dp_count, seq_count, *operands):
    places, width = operands[0].shape
    length = places * seq_count
    local = length // 2
    heads = H // seq_count
    hidden = operands[6].shape[1] // seq_count
    bits = bits_of(dp_count)
    mlp_plan = orders_of(dp_count, MLP_PLAN, 2, 2)
    head_plan = orders_of(dp_count, HEAD_PLAN, 1, heads)
    mlp_rows = padded(2 * width // len(mlp_plan), dp_count)
    head_rows = padded(width * heads // len(head_plan), dp_count)
    pieces = places // CHUNK
    copies = bits + 6 * pieces + len(mlp_plan) * (3 * bits + 4) + len(head_plan) * (3 * bits + 3)
    copies += heads + 1 + bits + 2
    loads = 2 + 6 + 2 * (2 + heads)
    scratch = [
        pltpu.VMEM((length, width), bf16),
        pltpu.VMEM((length, width), bf16),
        pltpu.VMEM((width, length), bf16),
        pltpu.VMEM((width, length), bf16),
        pltpu.VMEM((heads, length, PAIR), bf16),
        pltpu.VMEM((heads, length, PAIR), bf16),
        pltpu.VMEM((heads, length, PAIR), bf16),
        pltpu.VMEM((2, local, 2 * heads * PAIR), bf16),
        pltpu.VMEM((local, 2 * heads * PAIR), bf16),
        pltpu.VMEM((2, width, 2 * heads * PAIR), bf16),
        pltpu.VMEM((1, 2 * heads * PAIR), f32),
        pltpu.VMEM((2, heads * PAIR, width), bf16),
        pltpu.VMEM((2, width, hidden), bf16),
        pltpu.VMEM((2, hidden, width), bf16),
        pltpu.VMEM((2, local, hidden), bf16),
        pltpu.VMEM((2, local, width), bf16),
        pltpu.VMEM((len(mlp_plan), 2, mlp_rows, width), bf16),
        pltpu.VMEM((len(head_plan), 1, head_rows, 2 * PAIR), bf16),
        pltpu.VMEM((2, places, width), bf16),
        pltpu.VMEM((PAIR, length), f32),
        pltpu.VMEM((bits + 1, 8, 128), f32),
        pltpu.VMEM((bits + 3, VECTOR_ROWS, width), f32),
        pltpu.SemaphoreType.DMA((copies,)),
        pltpu.SemaphoreType.DMA((copies,)),
        pltpu.SemaphoreType.DMA((loads + len(mlp_plan) + len(head_plan),)),
    ]
    for order in mlp_plan:
        scratch += arrivals_of(order, 2, mlp_rows, width)
    for order in head_plan:
        scratch += arrivals_of(order, 1, head_rows, 2 * PAIR)
    smem = pl.BlockSpec(memory_space=pltpu.SMEM)
    return pl.pallas_call(
        functools.partial(
            layer_kernel, dp_count, (mlp_plan, head_plan), AGENDA if dp_count == 8 else []
        ),
        out_shape=(
            jax.ShapeDtypeStruct((seq_count, len(mlp_plan), mlp_rows, width), bf16),
            jax.ShapeDtypeStruct((seq_count, len(head_plan), head_rows, 2 * PAIR), bf16),
            jax.ShapeDtypeStruct((VECTOR_ROWS, width), f32),
            jax.ShapeDtypeStruct((places, width), bf16),
            jax.ShapeDtypeStruct((places, width), f32),
        ),
        in_specs=[ANY, ANY, smem, VMEM, ANY, ANY, ANY, ANY, VMEM],
        out_specs=(ANY, ANY, VMEM, VMEM, VMEM),
        scratch_shapes=scratch,
        compiler_params=pltpu.CompilerParams(
            collective_id=0, has_side_effects=True, vmem_limit_bytes=63 * 2**20
        ),
        name="layer",
    )(*operands)


def finish_kernel(steps, up_in, down_in, mix_in, vec, up_out, down_out, qkv_out, out_out, *vectors):
    step, owner = pl.program_id(0), pl.program_id(1)
    up_out[...] = up_in[0].reshape(up_out.shape).astype(f32)
    down_out[...] = down_in[0].reshape(down_out.shape).astype(f32)
    owners, heads = mix_in.shape[:2]

    @pl.when((owner == 0) & (step < steps))
    def _():
        for r in range(owners):
            for h in range(heads):
                head = r * heads + h
                block = mix_in[r, h, 0].astype(f32)
                tail = block[:, PAIR:]
                qkv_out[:, pl.ds(head * E, E)] = tail[:, :E]
                qkv_out[:, pl.ds((H + head) * E, E)] = block[:, :E]
                qkv_out[:, pl.ds((2 * H + head) * E, E)] = block[:, E:PAIR]
                out_out[pl.ds(head * E, E), :] = jnp.transpose(tail)[E:, :]

    @pl.when((owner == 0) & (step == 0))
    def _():
        gain1, bias1, gain2, bias2, low1, low2, qkv, up = vectors
        for target, row in zip((gain1, bias1, gain2, bias2, low1, low2), (0, 1, 2, 3, 4, 4)):
            target[...] = vec[row]
        parts = [[], [], []]
        for r in range(owners):
            line = vec[pl.ds(5 + owners + r, 1), :]
            for h in range(heads):
                at = 2 * h * PAIR
                parts[0].append(line[:, at + PAIR : at + PAIR + E])
                parts[1].append(line[:, at : at + E])
                parts[2].append(line[:, at + E : at + PAIR])
        qkv[...] = jnp.concatenate(parts[0] + parts[1] + parts[2], axis=1)[0]
        up[...] = jnp.concatenate([vec[pl.ds(5 + r, 1), :] for r in range(owners)], axis=1)[0]


def finish(full_mlp, full_heads, vec):
    owners, mlp_groups, _, width = full_mlp.shape
    _, head_groups, head_pad, _ = full_heads.shape
    heads = H // owners
    rows = 2 * width // mlp_groups
    stack = max(1, 256 // rows)
    steps = width // (stack * rows)
    mix_steps = head_groups // heads
    mix_rows = width // mix_steps
    lines = [width] * 6 + [3 * H * E, owners * width]
    last = mix_steps - 1
    return pl.pallas_call(
        functools.partial(finish_kernel, mix_steps),
        grid=(steps, owners),
        out_shape=(
            jax.ShapeDtypeStruct((width, owners * width), f32),
            jax.ShapeDtypeStruct((owners * width, width), f32),
            jax.ShapeDtypeStruct((width, 3 * H * E), f32),
            jax.ShapeDtypeStruct((H * E, width), f32),
        )
        + tuple(jax.ShapeDtypeStruct((size,), f32) for size in lines),
        in_specs=[
            pl.BlockSpec((1, stack, rows, width), lambda m, r: (r, m, 0, 0)),
            pl.BlockSpec((1, stack, rows, width), lambda m, r: (r, steps + m, 0, 0)),
            pl.BlockSpec((owners, heads, 1, mix_rows, 2 * PAIR), lambda m, r: (0, 0, jnp.minimum(m, last), 0, 0)),
            pl.BlockSpec(vec.shape, lambda m, r: (0, 0)),
        ],
        out_specs=(
            pl.BlockSpec((stack * rows, width), lambda m, r: (m, r)),
            pl.BlockSpec((stack * rows, width), lambda m, r: (r * steps + m, 0)),
            pl.BlockSpec((mix_rows, 3 * H * E), lambda m, r: (jnp.minimum(m, last), 0)),
            pl.BlockSpec((H * E, mix_rows), lambda m, r: (0, jnp.minimum(m, last))),
        )
        + tuple(pl.BlockSpec((size,), lambda m, r: (0,)) for size in lines),
        compiler_params=pltpu.CompilerParams(vmem_limit_bytes=62 * 2**20),
        name="finish",
    )(full_mlp, full_mlp, full_heads.reshape(owners, heads, mix_steps, head_pad, 2 * PAIR), vec)


def turn_table(length):
    half = ROT // 2
    frequency = (10000.0 ** (-2.0 * np.arange(half, dtype=np.float32) / ROT)).astype(np.float32)
    angles = np.arange(length, dtype=np.float32)[:, None] * frequency[None, :]
    cosine, sine = np.cos(angles), np.sin(angles)
    table = np.concatenate([cosine, cosine, -sine, sine], axis=1).astype(np.float32)
    rest = np.zeros((length // 2, PAIR - 4 * ROT), np.float32)
    return jnp.asarray(np.concatenate([table[: length // 2], table[length // 2 :], rest], axis=1))


def body(
    tokens,
    tissue,
    norm1_gain,
    norm1_bias,
    norm2_gain,
    norm2_bias,
    qkv_weight,
    qkv_bias,
    out_weight,
    out_bias,
    up_weight,
    up_bias,
    down_weight,
    down_bias,
    cotangent,
):
    dp_count, seq_count = lax.axis_size("dp"), lax.axis_size("seq")
    _, places, width = tokens.shape
    lines = [norm1_gain, norm1_bias, norm2_gain, norm2_bias, out_bias + down_bias]
    for bias in (up_bias, qkv_bias):
        lines += [bias[at : at + width] for at in range(0, bias.shape[0], width)]
    row = lax.broadcasted_iota(jnp.int32, (SMALL_ROWS, width), 0)
    small = jnp.zeros((SMALL_ROWS, width), f32)
    for number, line in enumerate(lines):
        small = jnp.where(row == number, line[None], small)
    full_mlp, full_heads, vec, mixed, input_grad = layer(
        dp_count,
        seq_count,
        tokens.reshape(places, width),
        cotangent.reshape(places, width),
        tissue,
        small,
        qkv_weight,
        out_weight,
        up_weight,
        down_weight,
        turn_table(places * seq_count),
    )
    up, down, qkv, out, gain1, bias1, gain2, bias2, low1, low2, qkv_b, up_b = finish(full_mlp, full_heads, vec)
    return (
        mixed.reshape(tokens.shape),
        input_grad.reshape(tokens.shape),
        gain1,
        bias1,
        gain2,
        bias2,
        qkv,
        qkv_b,
        out,
        low1,
        up,
        up_b,
        down,
        low2,
    )


def solution(mesh):
    rows = P("dp", "seq", None)
    return jax.shard_map(
        body,
        mesh=mesh,
        in_specs=(rows, P("dp")) + (P(),) * 12 + (rows,),
        out_specs=(rows, rows) + (P(),) * 12,
        check_vma=False,
    )
```

```python
import functools
import math

import jax
import jax.numpy as jnp
import numpy as np
from jax import lax
from jax.experimental import pallas as pl
from jax.experimental.pallas import tpu as pltpu
from jax.sharding import PartitionSpec as P

H = 12
E = 64
ROT = 16
TISSUES = 16
norm_eps = 1e-05
masked_score = -1e30
f32 = jnp.float32
bf16 = jnp.bfloat16
MESH = pl.DeviceIdType.MESH
ANY = pl.BlockSpec(memory_space=pl.ANY)
VMEM = pl.BlockSpec(memory_space=pltpu.VMEM)
VECTOR_ROWS = 16
CORE, CHIP = 1, 2
PAIR = 2 * E
CHUNK = 256

NN = ((1,), (0,))
NT = ((1,), (1,))
TN = ((0,), (0,))


def dot(a, b, dims):
    return lax.dot_general(a, b, (dims, ((), ())), preferred_element_type=f32)


def bits_of(count):
    return count.bit_length() - 1


def bit_at(index, bit):
    return lax.div(index, bit) % 2


def flip(index, bit):
    return index + bit - 2 * bit * bit_at(index, bit)


def aligned(start, size):
    return pl.ds(pl.multiple_of(start, size), size)


class Links:
    def __init__(self, dp_count, send_sems, recv_sems):
        self.dp = lax.axis_index("dp")
        self.seq = lax.axis_index("seq")
        self.dp_bits = [1 << j for j in range(bits_of(dp_count))]
        self.send_sems, self.recv_sems, self.used = send_sems, recv_sems, 0

    def over(self, axis, bit):
        if axis == "seq":
            return (self.dp, flip(self.seq, bit))
        return (flip(self.dp, bit), self.seq)

    def line(self):
        return lax.div(self.dp, 2) % 4

    def along(self, other):
        dp = self.dp
        for bit in (1, 2):
            if other & bit:
                dp = flip(dp, 2 * bit)
        return (dp, self.seq), lax.div(dp, 2) % 4

    def barrier(self):
        semaphore = pltpu.get_barrier_semaphore()
        partners = [self.over("seq", CORE), self.over("seq", CHIP)]
        partners += [self.over("dp", bit) for bit in self.dp_bits]
        if len(self.dp_bits) == 3:
            partners.append(self.along(3)[0])
        for partner in partners:
            pl.semaphore_signal(semaphore, inc=1, device_id=partner, device_id_type=MESH)
        pl.semaphore_wait(semaphore, len(partners))

    def send(self, source, target, partner):
        copy = pltpu.make_async_remote_copy(
            src_ref=source,
            dst_ref=target,
            send_sem=self.send_sems.at[self.used],
            recv_sem=self.recv_sems.at[self.used],
            device_id=partner,
            device_id_type=MESH,
        )
        self.used += 1
        copy.start()
        return copy


def add_up_everywhere(links, steps, buffer):
    for number, (axis, bit) in enumerate(steps):
        copy = links.send(buffer.at[0], buffer.at[number + 1], links.over(axis, bit))
        yield
        copy.wait()
        buffer[0] = buffer[0] + buffer[number + 1]


def axes_of(word):
    steps = {"x": ("seq", CHIP), "Z": ("line", 4), "y": ("dp", 1), "z": ("dp", 2), "w": ("dp", 4)}
    return [steps[letter] for letter in word]


def plain_order(dp_count, blocks):
    scatter = [("dp", 1 << j) for j in range(bits_of(dp_count))]
    collect = [("seq", CHIP)] + scatter[::-1]
    return (scatter + ([("seq", CHIP)] if blocks == 2 else []), collect)


def orders_of(dp_count, plan, blocks, few):
    if dp_count == 8:
        return [(axes_of(scatter), axes_of(collect)) for scatter, collect in plan]
    return [plain_order(dp_count, blocks)] * few


MLP_PLAN = [
    ("zyxw", "xwyz"),
    ("yzwx", "wzxy"),
    ("xzyw", "wyzx"),
    ("yzxw", "wxzy"),
    ("yxzw", "wzyx"),
    ("yzxw", "wzyx"),
]
HEAD_PLAN = [
    ("yzw", "wxzy"),
    ("yzw", "wxzy"),
    ("zyw", "wxyz"),
    ("zyw", "wyxz"),
    ("yzw", "wzxy"),
    ("zyw", "wxyz"),
]
AGENDA = [
    [],
    [],
    [],
    ["m1"],
    [],
    [],
    ["m0", "m3", "m1"],
    [],
    [],
    [],
    [],
    ["m1", "m4", "m2"],
    [],
    ["m3"],
    ["m1", "m5"],
    [],
    [],
    [],
    ["m3", "m2"],
    ["m4"],
    [],
    ["m1"],
    ["m0", "m4", "a0", "m3"],
    ["m1"],
    ["a1"],
    [],
    ["a0", "m2"],
    ["m0"],
    [],
    ["m1", "m3"],
    ["a5", "m5"],
    ["a1", "m4", "m0", "m2"],
    ["a1", "a3"],
    ["a3", "m2", "m1", "a0", "a2", "m4", "a5", "a3", "a4", "m1", "m3", "a1", "m5", "a2", "a4", "a3", "m4", "m5", "a0", "m0", "m2", "a2", "m3", "a5", "vec", "m4"],
    ["a4", "m5", "a0"],
    ["m0"],
    ["m4", "a4", "a5", "a1", "a2", "a3", "vec", "m5", "a2", "m0", "a4", "vec", "a0", "m2", "a1", "m4", "m3", "a2", "m5", "a3", "a0", "m0", "a5", "a1", "m2", "a1", "a4", "vec", "m3", "m2", "m0", "a5", "a3", "m5", "a4", "a2", "vec", "a0", "a3", "a5", "a4", "m5", "a5", "a2"],
]


class Turns:
    def __init__(self, agenda):
        self.agenda, self.tasks, self.ticks = agenda, {}, 0

    def add(self, name, task):
        self.tasks[name] = task
        self.advance(name)

    def advance(self, name):
        task = self.tasks.pop(name, None)
        if task is not None and next(task, "done") != "done":
            self.tasks[name] = task

    def tick(self):
        if self.ticks < len(self.agenda):
            for name in self.agenda[self.ticks]:
                self.advance(name)
        elif not self.agenda and self.tasks:
            self.advance(next(iter(self.tasks)))
        self.ticks += 1

    def finish(self):
        while self.ticks < len(self.agenda):
            self.tick()
        while self.tasks:
            self.advance(next(iter(self.tasks)))


def normalise(rows):
    centred = rows - jnp.mean(rows, axis=-1, keepdims=True)
    inverse = lax.rsqrt(jnp.mean(centred * centred, axis=-1, keepdims=True) + norm_eps)
    return centred * inverse, inverse


def lanes_of(shape):
    return lax.broadcasted_iota(jnp.int32, shape, 1)


def swapped(pairs):
    half = ROT // 2
    return jnp.where(
        lanes_of(pairs.shape) < half, pltpu.roll(pairs, PAIR - half, 1), pltpu.roll(pairs, half, 1)
    )


def head_columns(windows, odd, heads):
    def put(window, h, to):
        def at(place):
            block = window[:, place // 2 * PAIR : (place // 2 + 1) * PAIR]
            return block if place % 2 == to else pltpu.roll(block, E, 1)

        return jnp.where(odd == 1, at(h + 1), at(h))

    query, key, value = windows
    low = lanes_of((key.shape[0], PAIR)) < E
    blocks = []
    for h in range(heads):
        blocks.append(jnp.where(low, put(key, h, 0), put(value, h, 1)))
        blocks.append(jnp.where(low, put(query, h, 0), 0.0))
    return blocks


SMALL_ROWS = 16


def layer_kernel(
    dp_count,
    plans,
    agenda,
    x_in,
    c_in,
    tissue_in,
    small,
    qkv_w,
    out_w,
    up_w,
    down_w,
    turn_in,
    full_mlp,
    full_heads,
    vec_out,
    mixed_out,
    input_grad_out,
    x_all,
    c_all,
    low_t,
    first_t,
    kv,
    q0,
    g0,
    pairs,
    pairs_back,
    w_pairs,
    b_pairs,
    o_pairs,
    u_w,
    d_w,
    pre_grads,
    part,
    grads_mlp,
    grads_heads,
    core_buf,
    kvt,
    label_buf,
    vec_buf,
    sends,
    recvs,
    own_sems,
    *halves,
):
    links = Links(dp_count, sends, recvs)
    rank = links.seq
    chip, core = bit_at(rank, CHIP), bit_at(rank, CORE)
    places, width = x_in.shape
    length = x_all.shape[0]
    local = length // 2
    heads = kv.shape[0]
    hidden = u_w.shape[2]
    pieces = places // CHUNK
    score_scale = 1.0 / math.sqrt(E)
    ranks = (rank, flip(rank, CHIP))
    turns = Turns(agenda)

    loads = [
        (x_in, x_all.at[aligned(rank * places, places)]),
        (c_in, c_all.at[aligned(rank * places, places)]),
    ]
    for at in range(2):
        for which in range(3):
            start = which * H * E + lax.div(heads * ranks[at], 2) * PAIR
            loads.append(
                (
                    qkv_w.at[:, pl.ds(pl.multiple_of(start, PAIR), 2 * PAIR)],
                    part.at[at, pl.ds(0, width), pl.ds(which * 2 * PAIR, 2 * PAIR)],
                )
            )
    for at in range(2):
        loads.append((up_w.at[:, aligned(ranks[at] * hidden, hidden)], u_w.at[at]))
        loads.append((down_w.at[aligned(ranks[at] * hidden, hidden)], d_w.at[at]))
        for h in range(heads):
            loads.append(
                (out_w.at[aligned((ranks[at] * heads + h) * E, E)], o_pairs.at[at, pl.ds(h * PAIR + E, E)])
            )
    loads = [pltpu.make_async_copy(source, target, own_sems.at[i]) for i, (source, target) in enumerate(loads)]
    for copy in loads:
        copy.start()
    links.barrier()

    def rows_of(owner, piece):
        return aligned(owner * places + piece * CHUNK, CHUNK)

    def spread(piece):
        copies = []
        for source, target in ((x_in, x_all), (c_in, c_all)):
            mine = source.at[pl.ds(piece * CHUNK, CHUNK)]
            own = target.at[rows_of(rank, piece)]
            copies.append(links.send(mine, own, links.over("seq", CHIP)))
            copies.append(links.send(mine, own, links.over("seq", CORE)))
        return copies

    def pass_on(piece):
        copies = []
        for target in (x_all, c_all):
            held = target.at[rows_of(flip(rank, CHIP), piece)]
            copies.append(links.send(held, held, links.over("seq", CORE)))
        return copies

    own_label = (lanes_of((8, 128)) == tissue_in[0]).astype(f32)
    label_buf[0] = own_label
    counting = add_up_everywhere(links, [("dp", bit) for bit in links.dp_bits], label_buf)
    next(counting)
    spreads = [spread(piece) for piece in range(pieces)]
    for at in range(2):
        for h in range(heads):
            o_pairs[at, pl.ds(h * PAIR, E), :] = jnp.zeros((E, width), bf16)
    vec_buf[0] = jnp.zeros(vec_buf.shape[1:], f32)
    for copy in loads:
        copy.wait()

    odd = heads * rank % 2
    for at in range(2):
        for tile in range(width // CHUNK):
            rows = pl.ds(tile * CHUNK, CHUNK)
            windows = [part[at, rows, pl.ds(which * 2 * PAIR, 2 * PAIR)].astype(f32) for which in range(3)]
            for number, block in enumerate(head_columns(windows, odd, heads)):
                w_pairs[at, rows, pl.ds(number * PAIR, PAIR)] = block.astype(bf16)
    start = pl.multiple_of(lax.div(heads * rank, 2) * PAIR, PAIR)
    windows = [small[pl.ds(9 + which, 1), pl.ds(start, 2 * PAIR)] for which in range(3)]
    for number, block in enumerate(head_columns(windows, odd, heads)):
        b_pairs[:, pl.ds(number * PAIR, PAIR)] = block

    for _ in counting:
        pass
    count = jnp.sum(label_buf[0] * own_label, axis=1, keepdims=True)[:1]
    weight = dp_count / (TISSUES * count)
    gain1, bias1, gain2, bias2, end_bias = [small[pl.ds(row, 1), :] for row in range(5)]

    def add_vec(row, value):
        vec_buf[0, pl.ds(row, 1), :] += value

    def total(value):
        return jnp.sum(value, axis=0, keepdims=True)

    def turn_of(half, rows):
        table = turn_in[rows, :]
        table = jnp.where(half == 1, pltpu.roll(table, PAIR - 2 * ROT, 1), table)
        lane = lanes_of(table.shape)
        cosine = jnp.where(lane < ROT, table, 1.0)
        sine = jnp.where(lane < ROT, pltpu.roll(table, PAIR - ROT, 1), 0.0)
        return cosine, sine

    second_kept = [(keep, h) for keep in (kv, q0) for h in range(heads)]

    def feed_forward(start):
        rows = aligned(start, CHUNK)
        normed, _ = normalise(x_all[rows, :].astype(f32))
        low = (c_all[rows, :].astype(f32) * weight).astype(bf16)
        c_all[rows, :] = low
        second = (normed * gain2 + bias2).astype(bf16)
        near = aligned(start - chip * local, CHUNK)
        rest = aligned(start + (1 - 2 * chip) * local, CHUNK)
        for tile, (keep, h) in enumerate(second_kept):
            keep[h, rest, :] = second[:, tile * PAIR : (tile + 1) * PAIR]
        branch, second_grad = 0.0, 0.0
        for at in range(2):
            pre = dot(second, u_w[at], NN) + small[pl.ds(5 + ranks[at], 1), :]
            gate = 0.5 * (1.0 + lax.erf(pre * (1.0 / math.sqrt(2.0))))
            act = (pre * gate).astype(bf16)
            slope = gate + pre * jnp.exp(-0.5 * pre * pre) * (1.0 / math.sqrt(2.0 * math.pi))
            branch += dot(act, d_w[at], NN)
            pre_grad = (dot(low, d_w[at], NT) * slope).astype(bf16)
            add_vec(5 + ranks[at], total(pre_grad.astype(f32)))
            second_grad += dot(pre_grad, u_w[at], NT)
            pairs[at, near, :] = act
            pre_grads[at, near, :] = pre_grad
        part[0, near, :] = branch.astype(bf16)
        part[1, near, :] = (second_grad * gain2).astype(bf16)
        add_vec(2, total(second_grad * normed))
        add_vec(3, total(second_grad))
        add_vec(4, total(low.astype(f32)) * (places / local))

    def heads_in(start, scale):
        rows = aligned(start, CHUNK)
        normed, _ = normalise(x_all[rows, :].astype(f32))
        first = normed * gain1 + bias1
        first_t[:, rows] = jnp.transpose(first).astype(bf16)
        first = first.astype(bf16)
        low = c_all[rows, :].astype(f32) * scale
        low_t[:, rows] = jnp.transpose(low).astype(bf16)
        low = low.astype(bf16)
        joint = dot(first, w_pairs[0], NN) + b_pairs[...]
        half = lax.div(start, local)
        cosine, sine = turn_of(half, aligned(start - half * local, CHUNK))
        for h in range(heads):
            pair = joint[:, 2 * h * PAIR : (2 * h + 1) * PAIR]
            kv[h, rows, :] = (pair * cosine + swapped(pair) * sine).astype(bf16)
            pair = joint[:, (2 * h + 1) * PAIR : (2 * h + 2) * PAIR]
            pair = (pair * cosine + swapped(pair) * sine).astype(bf16).astype(f32) * score_scale
            q0[h, rows, :] = pair.astype(bf16)
            g0[h, rows, :] = dot(low, o_pairs[0, pl.ds(h * PAIR, PAIR), :], NT).astype(bf16)

    beside = flip(rank, CORE)

    def near_chunk(index, _):
        @pl.when(index == pieces)
        def _():
            for piece in range(pieces):
                spreads[piece][1].wait()
                spreads[piece][3].wait()

        owner = jnp.where(index < pieces, rank, beside)
        feed_forward(owner * places + index % pieces * CHUNK)
        return 0

    lax.fori_loop(0, 2 * pieces, near_chunk, 0)

    halves = list(halves)

    def one_group(held, full, group, order, own_sem, arrivals):
        scatter, collect = order
        blocks, size, _ = held.shape
        start = 0
        for axis, bit in scatter:
            arrived = arrivals.pop(0)
            if axis == "seq":
                copy = links.send(held.at[pl.ds(1, 1)], arrived, links.over(axis, bit))
                yield
                copy.wait()
                arrived[...] = (held[pl.ds(0, 1)].astype(f32) + arrived[...].astype(f32)).astype(bf16)
            elif axis == "line":
                size //= 4
                mine = links.line()
                copies = []
                for other in (3, 2, 1):
                    partner, place = links.along(other)
                    copies.append(
                        links.send(held.at[:, aligned(place * size, size)], arrived.at[other - 1], partner)
                    )
                yield
                for copy in copies:
                    copy.wait()
                own = held[:, aligned(mine * size, size), :].astype(f32)
                rest = [arrived[number].astype(f32) for number in range(3)]
                arrived[0] = ((own + rest[0]) + (rest[1] + rest[2])).astype(bf16)
                arrived = arrived.at[0]
                start = start + mine * size
            else:
                size //= 2
                mine = bit_at(links.dp, bit)
                copy = links.send(held.at[:, aligned((1 - mine) * size, size)], arrived, links.over(axis, bit))
                yield
                copy.wait()
                own = held[:, aligned(mine * size, size), :].astype(f32)
                arrived[...] = (own + arrived[...].astype(f32)).astype(bf16)
                start = start + mine * size
            held = arrived
        owners = [rank]

        def region(owner):
            return full.at[owner, group, aligned(start, size)]

        own = pltpu.make_async_copy(held.at[0], region(rank), own_sem)
        own.start()
        for number, (axis, bit) in enumerate(collect + [("seq", CORE)]):
            if axis == "line":
                partners = [links.along(other)[0] for other in (3, 2, 1)]
            else:
                partners = [links.over(axis, bit)]
            copies = [
                links.send(region(owner) if number else held.at[0], region(owner), partner)
                for partner in partners
                for owner in owners
            ]
            yield
            if number == 0:
                own.wait()
            for copy in copies:
                copy.wait()
            if axis == "line":
                start = start - links.line() * size
                size *= 4
            elif axis == "dp":
                start = start - bit_at(links.dp, bit) * size
                size *= 2
            else:
                owners = owners + [flip(owner, bit) for owner in owners]

    mlp_plan, head_plan = plans

    def begin(name, grads, full, group, order, number):
        count = len(order[0])
        arrivals, halves[:count] = halves[:count], []
        turns.add(name, one_group(grads.at[group], full, group, order, own_sems.at[len(loads) + number], arrivals))

    def fill(grads, group, real):
        spare = grads.shape[2] - real
        if spare:
            blocks = grads.shape[1]
            grads[group, :, pl.ds(real, spare), :] = jnp.zeros((blocks, spare, grads.shape[3]), bf16)

    near_rows = aligned(chip * local, local)
    far_rows = aligned((1 - chip) * local, local)
    mlp_groups = len(mlp_plan)
    mlp_rows = 2 * width // mlp_groups
    for group in range(mlp_groups):
        first_tile = group % (mlp_groups // 2) * mlp_rows // PAIR
        for at in range(2):
            for tile in range(mlp_rows // PAIR):
                if group < mlp_groups // 2:
                    keep, h = second_kept[first_tile + tile]
                    term = dot(keep[h, far_rows, :], pre_grads[at], TN)
                else:
                    columns = pl.ds((first_tile + tile) * PAIR, PAIR)
                    term = dot(pairs[at, :, columns], c_all[near_rows, :], TN)
                grads_mlp[group, at, pl.ds(tile * PAIR, PAIR), :] = term.astype(bf16)
        fill(grads_mlp, group, mlp_rows)
        begin("m%d" % group, grads_mlp, full_mlp, group, mlp_plan[group], group)
        if group >= mlp_groups // 2:
            turns.tick()

    one = jnp.ones_like(weight)
    for owner in (rank, beside):

        def near_heads(piece, _):
            heads_in(owner * places + piece * CHUNK, one)
            return 0

        lax.fori_loop(0, pieces, near_heads, 0)
        turns.tick()

    far, across = flip(rank, CHIP), flip(flip(rank, CHIP), CORE)
    for piece in range(pieces):
        turns.tick()
        spreads[piece][0].wait()
        spreads[piece][2].wait()
        onward = pass_on(piece)

        def far_chunk(index, _):
            @pl.when(index == 1)
            def _():
                for copy in onward:
                    copy.wait()

            heads_in(jnp.where(index == 0, far, across) * places + piece * CHUNK, weight)
            return 0

        lax.fori_loop(0, 2, far_chunk, 0)

    blocks = length // CHUNK

    def pair_rows(block):
        return block * CHUNK // local, pl.ds(block * CHUNK % local, CHUNK)

    back = []
    for h in range(heads):
        for i in range(blocks):
            own = pl.ds(i * CHUNK, CHUNK)
            half, rows = pair_rows(i)
            q, g = q0[h, own, :], g0[h, own, :]
            spans = ([(0, i * CHUNK)] if i else []) + [(i * CHUNK, CHUNK)]
            scores = [dot(q, kv[h, pl.ds(at, size), :], NT) for at, size in spans]
            row = lax.broadcasted_iota(jnp.int32, (CHUNK, CHUNK), 0)
            column = lanes_of((CHUNK, CHUNK))
            scores[-1] = jnp.where(column <= row, scores[-1], masked_score)
            largest = functools.reduce(jnp.maximum, [jnp.max(s, axis=1, keepdims=True) for s in scores])
            probs = [jnp.exp(s - largest) for s in scores]
            inverse = 1.0 / sum(jnp.sum(p, axis=1, keepdims=True) for p in probs)
            probs = [p * inverse for p in probs]
            lows = [p.astype(bf16) for p in probs]
            attended = sum(dot(low, kv[h, pl.ds(at, size), :], NN) for low, (at, size) in zip(lows, spans))
            delta = jnp.sum(attended * g.astype(f32), axis=1, keepdims=True)
            score_grads = [
                (p * (dot(g, kv[h, pl.ds(at, size), :], NT) - delta)).astype(bf16)
                for p, (at, size) in zip(probs, spans)
            ]
            q_grad = sum(dot(s, kv[h, pl.ds(at, size), :], NN) for s, (at, size) in zip(score_grads, spans))
            q_grad = q_grad * score_scale
            cosine, sine = turn_of(half, rows)
            q_grad = q_grad * cosine - swapped(q_grad) * sine
            tail = jnp.where(lanes_of(q_grad.shape) < E, q_grad, attended)
            pairs[half, rows, pl.ds((2 * h + 1) * PAIR, PAIR)] = tail.astype(bf16)
            for s, low, (at, size) in zip(score_grads, lows, spans):
                term = dot(q, s, TN) + dot(g, low, TN)
                if at:
                    kvt[:, pl.ds(at, size)] = term
                elif i == 0:
                    kvt[:, pl.ds(0, size)] = term
                else:
                    kvt[:, pl.ds(0, size)] += term
            turns.tick()
        for i in range(blocks):
            own = pl.ds(i * CHUNK, CHUNK)
            half, rows = pair_rows(i)
            cosine, sine = turn_of(half, rows)
            pair = jnp.transpose(kvt[:, own])
            pair = pair * cosine - swapped(pair) * sine
            pairs[half, rows, pl.ds(2 * h * PAIR, PAIR)] = pair.astype(bf16)

        columns = pl.ds(2 * h * PAIR, 2 * PAIR)
        back.append(links.send(pairs.at[1 - chip, :, columns], pairs_back.at[:, columns], links.over("seq", CHIP)))

        head_groups = len(head_plan) // heads
        head_rows = width // head_groups
        for number in range(head_groups):
            group = h * head_groups + number
            rows = pl.ds(number * head_rows, head_rows)
            term = sum(
                dot(first_t[rows, pl.ds(half * local, local)], pairs[half, :, columns], NN) for half in range(2)
            )
            out_term = sum(
                dot(
                    low_t[rows, pl.ds(half * local, local)],
                    pairs[half, :, pl.ds((2 * h + 1) * PAIR, PAIR)],
                    NN,
                )
                for half in range(2)
            )
            tail = jnp.where(lanes_of(out_term.shape) < E, term[:, PAIR:], out_term)
            grads_heads[group, 0, pl.ds(0, head_rows), pl.ds(0, PAIR)] = term[:, :PAIR].astype(bf16)
            grads_heads[group, 0, pl.ds(0, head_rows), pl.ds(PAIR, PAIR)] = tail.astype(bf16)
            fill(grads_heads, group, head_rows)
            begin("a%d" % group, grads_heads, full_heads, group, head_plan[group], mlp_groups + group)
        turns.tick()

    add_vec(9 + rank, total(pairs[0].astype(f32)) + total(pairs[1].astype(f32)))
    for copy in back:
        copy.wait()

    def last(owner, piece):
        near = aligned((owner - chip * 2) * places + piece * CHUNK, CHUNK)
        normed, _ = normalise(x_all[aligned(owner * places + piece * CHUNK, CHUNK), :].astype(f32))
        own, other = pairs[chip, near, :], pairs_back[near, :]
        attn = 0.0
        for h in range(heads):
            tail = slice((2 * h + 1) * PAIR, (2 * h + 2) * PAIR)
            attn += dot(own[:, tail], o_pairs[0, pl.ds(h * PAIR, PAIR), :], NN)
            attn += dot(other[:, tail], o_pairs[1, pl.ds(h * PAIR, PAIR), :], NN)
        first_grad = dot(own, w_pairs[0], NT) + dot(other, w_pairs[1], NT)
        part[0, near, :] = (part[0, near, :].astype(f32) + attn).astype(bf16)
        part[1, near, :] = (part[1, near, :].astype(f32) + first_grad * gain1).astype(bf16)
        add_vec(0, total(first_grad * normed))
        add_vec(1, total(first_grad))

    def last_loop(owner):
        def one(piece, _):
            last(owner, piece)
            return 0

        lax.fori_loop(0, pieces, one, 0)

    last_loop(beside)
    given = part.at[:, aligned((1 - core) * places, places)]
    crossing = links.send(given, core_buf, links.over("seq", CORE))
    turns.tick()
    last_loop(rank)
    vec_steps = [("seq", CORE), ("seq", CHIP)] + [("dp", bit) for bit in links.dp_bits]
    turns.add("vec", add_up_everywhere(links, vec_steps, vec_buf))
    turns.tick()

    reload = pltpu.make_async_copy(c_in, c_all.at[aligned(rank * places, places)], own_sems.at[0])
    reload.start()
    crossing.wait()
    reload.wait()
    for piece in range(pieces):
        rows = pl.ds(piece * CHUNK, CHUNK)
        own_rows = rows_of(rank, piece)
        near = aligned(core * places + piece * CHUNK, CHUNK)
        x = x_all[own_rows, :].astype(f32)
        sums = [part[which, near, :].astype(f32) + core_buf[which, rows, :].astype(f32) for which in range(2)]
        mixed_out[rows, :] = (x + sums[0] + end_bias).astype(bf16)
        normed, inverse = normalise(x)
        scaled = sums[1]
        rows_grad = inverse * (
            scaled
            - jnp.mean(scaled, axis=-1, keepdims=True)
            - normed * jnp.mean(scaled * normed, axis=-1, keepdims=True)
        )
        input_grad_out[rows, :] = c_all[own_rows, :].astype(f32) * weight + rows_grad
    turns.finish()
    vec_out[...] = vec_buf[0]


def padded(rows, dp_count):
    return -(-rows // (16 * dp_count)) * 16 * dp_count


def arrivals_of(order, blocks, rows, width):
    shapes = []
    for axis, _ in order[0]:
        if axis == "seq":
            blocks = 1
        else:
            rows //= 4 if axis == "line" else 2
        shape = (blocks, rows, width)
        shapes.append(pltpu.VMEM((3,) + shape if axis == "line" else shape, bf16))
    return shapes


def layer(dp_count, seq_count, *operands):
    places, width = operands[0].shape
    length = places * seq_count
    local = length // 2
    heads = H // seq_count
    hidden = operands[6].shape[1] // seq_count
    bits = bits_of(dp_count)
    mlp_plan = orders_of(dp_count, MLP_PLAN, 2, 2)
    head_plan = orders_of(dp_count, HEAD_PLAN, 1, heads)
    mlp_rows = padded(2 * width // len(mlp_plan), dp_count)
    head_rows = padded(width * heads // len(head_plan), dp_count)
    pieces = places // CHUNK
    copies = bits + 6 * pieces + (len(mlp_plan) + len(head_plan)) * 20
    copies += heads + 1 + bits + 2
    loads = 2 + 6 + 2 * (2 + heads)
    scratch = [
        pltpu.VMEM((length, width), bf16),
        pltpu.VMEM((length, width), bf16),
        pltpu.VMEM((width, length), bf16),
        pltpu.VMEM((width, length), bf16),
        pltpu.VMEM((heads, length, PAIR), bf16),
        pltpu.VMEM((heads, length, PAIR), bf16),
        pltpu.VMEM((heads, length, PAIR), bf16),
        pltpu.VMEM((2, local, 2 * heads * PAIR), bf16),
        pltpu.VMEM((local, 2 * heads * PAIR), bf16),
        pltpu.VMEM((2, width, 2 * heads * PAIR), bf16),
        pltpu.VMEM((1, 2 * heads * PAIR), f32),
        pltpu.VMEM((2, heads * PAIR, width), bf16),
        pltpu.VMEM((2, width, hidden), bf16),
        pltpu.VMEM((2, hidden, width), bf16),
        pltpu.VMEM((2, local, hidden), bf16),
        pltpu.VMEM((2, local, width), bf16),
        pltpu.VMEM((len(mlp_plan), 2, mlp_rows, width), bf16),
        pltpu.VMEM((len(head_plan), 1, head_rows, 2 * PAIR), bf16),
        pltpu.VMEM((2, places, width), bf16),
        pltpu.VMEM((PAIR, length), f32),
        pltpu.VMEM((bits + 1, 8, 128), f32),
        pltpu.VMEM((bits + 3, VECTOR_ROWS, width), f32),
        pltpu.SemaphoreType.DMA((copies,)),
        pltpu.SemaphoreType.DMA((copies,)),
        pltpu.SemaphoreType.DMA((loads + len(mlp_plan) + len(head_plan),)),
    ]
    for order in mlp_plan:
        scratch += arrivals_of(order, 2, mlp_rows, width)
    for order in head_plan:
        scratch += arrivals_of(order, 1, head_rows, 2 * PAIR)
    smem = pl.BlockSpec(memory_space=pltpu.SMEM)
    return pl.pallas_call(
        functools.partial(
            layer_kernel, dp_count, (mlp_plan, head_plan), AGENDA if dp_count == 8 else []
        ),
        out_shape=(
            jax.ShapeDtypeStruct((seq_count, len(mlp_plan), mlp_rows, width), bf16),
            jax.ShapeDtypeStruct((seq_count, len(head_plan), head_rows, 2 * PAIR), bf16),
            jax.ShapeDtypeStruct((VECTOR_ROWS, width), f32),
            jax.ShapeDtypeStruct((places, width), bf16),
            jax.ShapeDtypeStruct((places, width), f32),
        ),
        in_specs=[ANY, ANY, smem, VMEM, ANY, ANY, ANY, ANY, VMEM],
        out_specs=(ANY, ANY, VMEM, VMEM, VMEM),
        scratch_shapes=scratch,
        compiler_params=pltpu.CompilerParams(
            collective_id=0, has_side_effects=True, vmem_limit_bytes=63 * 2**20
        ),
        name="layer",
    )(*operands)


def finish_kernel(every, up_in, down_in, mix_in, vec, mixed_in, grad_in, up_out, down_out, qkv_out, out_out, *rest):
    mixed_out, grad_out, *vectors = rest
    step = pl.program_id(0)
    up_out[...] = up_in[0].reshape(up_out.shape).astype(f32)
    down_out[...] = down_in[0].reshape(down_out.shape).astype(f32)
    mixed_out[...] = mixed_in[...]
    grad_out[...] = grad_in[...]
    owners, heads = mix_in.shape[:2]

    @pl.when(step % every == 0)
    def _():
        for r in range(owners):
            for h in range(heads):
                head = r * heads + h
                block = mix_in[r, h, 0].astype(f32)
                tail = block[:, PAIR:]
                qkv_out[:, pl.ds(head * E, E)] = tail[:, :E]
                qkv_out[:, pl.ds((H + head) * E, E)] = block[:, :E]
                qkv_out[:, pl.ds((2 * H + head) * E, E)] = block[:, E:PAIR]
                out_out[pl.ds(head * E, E), :] = jnp.transpose(tail)[E:, :]

    @pl.when(step == 0)
    def _():
        gain1, bias1, gain2, bias2, low1, low2, qkv, up = vectors
        for target, row in zip((gain1, bias1, gain2, bias2, low1, low2), (0, 1, 2, 3, 4, 4)):
            target[...] = vec[row]
        parts = [[], [], []]
        for r in range(owners):
            line = vec[pl.ds(5 + owners + r, 1), :]
            for h in range(heads):
                at = 2 * h * PAIR
                parts[0].append(line[:, at + PAIR : at + PAIR + E])
                parts[1].append(line[:, at : at + E])
                parts[2].append(line[:, at + E : at + PAIR])
        qkv[...] = jnp.concatenate(parts[0] + parts[1] + parts[2], axis=1)[0]
        up[...] = jnp.concatenate([vec[pl.ds(5 + r, 1), :] for r in range(owners)], axis=1)[0]


def finish(full_mlp, full_heads, vec, mixed, input_grad):
    owners, mlp_groups, _, width = full_mlp.shape
    _, head_groups, head_pad, _ = full_heads.shape
    heads = H // owners
    rows = 2 * width // mlp_groups
    stack = max(1, 256 // rows)
    steps = width // (stack * rows)
    total = steps * owners
    mix_groups = head_groups // heads
    every = 2
    mix_rows = width // (total // every)
    in_group = width // mix_groups // mix_rows
    lines = [width] * 6 + [3 * H * E, owners * width]
    pieces = total // 3 if total % 3 == 0 else total
    own_rows = mixed.shape[0] // pieces
    own_spec = pl.BlockSpec((own_rows, width), lambda s: (s * pieces // total, 0))
    return pl.pallas_call(
        functools.partial(finish_kernel, every),
        grid=(total,),
        out_shape=(
            jax.ShapeDtypeStruct((width, owners * width), f32),
            jax.ShapeDtypeStruct((owners * width, width), f32),
            jax.ShapeDtypeStruct((width, 3 * H * E), f32),
            jax.ShapeDtypeStruct((H * E, width), f32),
            jax.ShapeDtypeStruct(mixed.shape, mixed.dtype),
            jax.ShapeDtypeStruct(input_grad.shape, input_grad.dtype),
        )
        + tuple(jax.ShapeDtypeStruct((size,), f32) for size in lines),
        in_specs=[
            pl.BlockSpec((1, stack, rows, width), lambda s: (s % owners, s // owners, 0, 0)),
            pl.BlockSpec((1, stack, rows, width), lambda s: (s % owners, steps + s // owners, 0, 0)),
            pl.BlockSpec(
                (owners, heads, 1, mix_rows, 2 * PAIR),
                lambda s: (0, 0, s // every // in_group, s // every % in_group, 0),
            ),
            pl.BlockSpec(vec.shape, lambda s: (0, 0)),
            own_spec,
            own_spec,
        ],
        out_specs=(
            pl.BlockSpec((stack * rows, width), lambda s: (s // owners, s % owners)),
            pl.BlockSpec((stack * rows, width), lambda s: (s % owners * steps + s // owners, 0)),
            pl.BlockSpec((mix_rows, 3 * H * E), lambda s: (s // every, 0)),
            pl.BlockSpec((H * E, mix_rows), lambda s: (0, s // every)),
            own_spec,
            own_spec,
        )
        + tuple(pl.BlockSpec((size,), lambda s: (0,)) for size in lines),
        compiler_params=pltpu.CompilerParams(vmem_limit_bytes=62 * 2**20),
        name="finish",
    )(full_mlp, full_mlp, full_heads.reshape(owners, heads, mix_groups, head_pad, 2 * PAIR), vec, mixed, input_grad)


def turn_table(length):
    half = ROT // 2
    frequency = (10000.0 ** (-2.0 * np.arange(half, dtype=np.float32) / ROT)).astype(np.float32)
    angles = np.arange(length, dtype=np.float32)[:, None] * frequency[None, :]
    cosine, sine = np.cos(angles), np.sin(angles)
    table = np.concatenate([cosine, cosine, -sine, sine], axis=1).astype(np.float32)
    rest = np.zeros((length // 2, PAIR - 4 * ROT), np.float32)
    return jnp.asarray(np.concatenate([table[: length // 2], table[length // 2 :], rest], axis=1))


def body(
    tokens,
    tissue,
    norm1_gain,
    norm1_bias,
    norm2_gain,
    norm2_bias,
    qkv_weight,
    qkv_bias,
    out_weight,
    out_bias,
    up_weight,
    up_bias,
    down_weight,
    down_bias,
    cotangent,
):
    dp_count, seq_count = lax.axis_size("dp"), lax.axis_size("seq")
    _, places, width = tokens.shape
    lines = [norm1_gain, norm1_bias, norm2_gain, norm2_bias, out_bias + down_bias]
    for bias in (up_bias, qkv_bias):
        lines += [bias[at : at + width] for at in range(0, bias.shape[0], width)]
    row = lax.broadcasted_iota(jnp.int32, (SMALL_ROWS, width), 0)
    small = jnp.zeros((SMALL_ROWS, width), f32)
    for number, line in enumerate(lines):
        small = jnp.where(row == number, line[None], small)
    full_mlp, full_heads, vec, mixed, input_grad = layer(
        dp_count,
        seq_count,
        tokens.reshape(places, width),
        cotangent.reshape(places, width),
        tissue,
        small,
        qkv_weight,
        out_weight,
        up_weight,
        down_weight,
        turn_table(places * seq_count),
    )
    results = finish(full_mlp, full_heads, vec, mixed, input_grad)
    up, down, qkv, out, mixed, input_grad, gain1, bias1, gain2, bias2, low1, low2, qkv_b, up_b = results
    return (
        mixed.reshape(tokens.shape),
        input_grad.reshape(tokens.shape),
        gain1,
        bias1,
        gain2,
        bias2,
        qkv,
        qkv_b,
        out,
        low1,
        up,
        up_b,
        down,
        low2,
    )


def solution(mesh):
    rows = P("dp", "seq", None)
    return jax.shard_map(
        body,
        mesh=mesh,
        in_specs=(rows, P("dp")) + (P(),) * 12 + (rows,),
        out_specs=(rows, rows) + (P(),) * 12,
        check_vma=False,
    )
```

```python
import functools
import math

import jax
import jax.numpy as jnp
import numpy as np
from jax import lax
from jax.experimental import pallas as pl
from jax.experimental.pallas import tpu as pltpu
from jax.sharding import PartitionSpec as P

H = 12
E = 64
ROT = 16
TISSUES = 16
norm_eps = 1e-05
masked_score = -1e30
f32 = jnp.float32
bf16 = jnp.bfloat16
MESH = pl.DeviceIdType.MESH
ANY = pl.BlockSpec(memory_space=pl.ANY)
VMEM = pl.BlockSpec(memory_space=pltpu.VMEM)
VECTOR_ROWS = 16
CORE, CHIP = 1, 2
PAIR = 2 * E
CHUNK = 256

NN = ((1,), (0,))
NT = ((1,), (1,))
TN = ((0,), (0,))


def dot(a, b, dims):
    return lax.dot_general(a, b, (dims, ((), ())), preferred_element_type=f32)


def bits_of(count):
    return count.bit_length() - 1


def bit_at(index, bit):
    return lax.div(index, bit) % 2


def flip(index, bit):
    return index + bit - 2 * bit * bit_at(index, bit)


def aligned(start, size):
    return pl.ds(pl.multiple_of(start, size), size)


class Links:
    def __init__(self, dp_count, send_sems, recv_sems):
        self.dp = lax.axis_index("dp")
        self.seq = lax.axis_index("seq")
        self.dp_bits = [1 << j for j in range(bits_of(dp_count))]
        self.send_sems, self.recv_sems, self.used = send_sems, recv_sems, 0

    def over(self, axis, bit):
        if axis == "seq":
            return (self.dp, flip(self.seq, bit))
        return (flip(self.dp, bit), self.seq)

    def line(self):
        return lax.div(self.dp, 2) % 4

    def along(self, other):
        dp = self.dp
        for bit in (1, 2):
            if other & bit:
                dp = flip(dp, 2 * bit)
        return (dp, self.seq), lax.div(dp, 2) % 4

    def barrier(self):
        semaphore = pltpu.get_barrier_semaphore()
        partners = [self.over("seq", CORE), self.over("seq", CHIP)]
        partners += [self.over("dp", bit) for bit in self.dp_bits]
        if len(self.dp_bits) == 3:
            partners.append(self.along(3)[0])
        for partner in partners:
            pl.semaphore_signal(semaphore, inc=1, device_id=partner, device_id_type=MESH)
        pl.semaphore_wait(semaphore, len(partners))

    def send(self, source, target, partner):
        copy = pltpu.make_async_remote_copy(
            src_ref=source,
            dst_ref=target,
            send_sem=self.send_sems.at[self.used],
            recv_sem=self.recv_sems.at[self.used],
            device_id=partner,
            device_id_type=MESH,
        )
        self.used += 1
        copy.start()
        return copy


def add_up_everywhere(links, steps, buffer):
    for number, (axis, bit) in enumerate(steps):
        copy = links.send(buffer.at[0], buffer.at[number + 1], links.over(axis, bit))
        yield
        copy.wait()
        buffer[0] = buffer[0] + buffer[number + 1]


def axes_of(word):
    steps = {"x": ("seq", CHIP), "Z": ("line", 4), "y": ("dp", 1), "z": ("dp", 2), "w": ("dp", 4)}
    return [steps[letter] for letter in word]


def plain_order(dp_count, blocks):
    scatter = [("dp", 1 << j) for j in range(bits_of(dp_count))]
    collect = [("seq", CHIP)] + scatter[::-1]
    return (scatter + ([("seq", CHIP)] if blocks == 2 else []), collect)


def orders_of(dp_count, plan, blocks, few):
    if dp_count == 8:
        return [(axes_of(scatter), axes_of(collect)) for scatter, collect in plan]
    return [plain_order(dp_count, blocks)] * few


MLP_PLAN = [
    ("zyxw", "wyzx"),
    ("xyzw", "xwzy"),
    ("yzxw", "wzxy"),
    ("zyxw", "xwyz"),
    ("yZx", "Zxy"),
    ("yzxw", "wzyx"),
]
HEAD_PLAN = [
    ("zyw", "xwyz"),
    ("yZ", "Zyx"),
    ("yZ", "Zyx"),
]
AGENDA = [
    [],
    [],
    [],
    ["m4"],
    ["m3"],
    [],
    [],
    ["m0", "m5"],
    ["m4", "m2", "m5", "m1"],
    ["m3"],
    ["m4", "m0"],
    [],
    ["m2", "m3", "m5"],
    [],
    ["m0", "m4", "m1"],
    ["m3", "m2"],
    [],
    ["m5"],
    ["m1"],
    ["m2", "m4"],
    [],
    [],
    [],
    ["m3", "m0"],
    ["m5", "m2", "a0", "m1"],
    ["m1"],
    ["m5", "m3", "a1"],
    ["m1", "a0", "m2"],
    [],
    [],
    ["m0", "m5", "m3"],
    ["m2"],
    [],
    ["m0", "a0", "m4"],
    ["m1", "a1", "m2", "m5", "a2", "a1", "a0", "m0", "m3"],
    ["a2", "a0"],
    ["a1", "a2", "m3", "a0", "m1", "a2", "m2"],
    ["m1", "vec", "m5", "vec", "m0", "vec", "a0", "vec", "m0", "vec", "a1", "a2", "a1", "a0", "m4", "a2"],
]


class Turns:
    def __init__(self, agenda):
        self.agenda, self.tasks, self.ticks = agenda, {}, 0

    def add(self, name, task):
        self.tasks[name] = task
        self.advance(name)

    def advance(self, name):
        task = self.tasks.pop(name, None)
        if task is not None and next(task, "done") != "done":
            self.tasks[name] = task

    def tick(self):
        if self.ticks < len(self.agenda):
            for name in self.agenda[self.ticks]:
                self.advance(name)
        elif not self.agenda and self.tasks:
            self.advance(next(iter(self.tasks)))
        self.ticks += 1

    def finish(self):
        while self.ticks < len(self.agenda):
            self.tick()
        while self.tasks:
            self.advance(next(iter(self.tasks)))


def normalise(rows):
    centred = rows - jnp.mean(rows, axis=-1, keepdims=True)
    inverse = lax.rsqrt(jnp.mean(centred * centred, axis=-1, keepdims=True) + norm_eps)
    return centred * inverse, inverse


def lanes_of(shape):
    return lax.broadcasted_iota(jnp.int32, shape, 1)


def swapped(pairs):
    half = ROT // 2
    return jnp.where(
        lanes_of(pairs.shape) < half, pltpu.roll(pairs, PAIR - half, 1), pltpu.roll(pairs, half, 1)
    )


def head_columns(windows, odd, heads):
    def put(window, h, to):
        def at(place):
            block = window[:, place // 2 * PAIR : (place // 2 + 1) * PAIR]
            return block if place % 2 == to else pltpu.roll(block, E, 1)

        return jnp.where(odd == 1, at(h + 1), at(h))

    query, key, value = windows
    low = lanes_of((key.shape[0], PAIR)) < E
    blocks = []
    for h in range(heads):
        blocks.append(jnp.where(low, put(key, h, 0), put(value, h, 1)))
        blocks.append(jnp.where(low, put(query, h, 0), 0.0))
    return blocks


SMALL_ROWS = 16


def layer_kernel(
    dp_count,
    plans,
    agenda,
    x_in,
    c_in,
    tissue_in,
    small,
    qkv_w,
    out_w,
    up_w,
    down_w,
    turn_in,
    full_mlp,
    full_heads,
    vec_out,
    mixed_out,
    input_grad_out,
    x_all,
    c_all,
    low_t,
    first_t,
    kv,
    q0,
    g0,
    pairs,
    pairs_back,
    w_pairs,
    b_pairs,
    o_pairs,
    u_w,
    d_w,
    pre_grads,
    part,
    grads_mlp,
    grads_heads,
    core_buf,
    kvt,
    label_buf,
    vec_buf,
    sends,
    recvs,
    own_sems,
    *halves,
):
    links = Links(dp_count, sends, recvs)
    rank = links.seq
    chip, core = bit_at(rank, CHIP), bit_at(rank, CORE)
    places, width = x_in.shape
    length = x_all.shape[0]
    local = length // 2
    heads = kv.shape[0]
    hidden = u_w.shape[2]
    pieces = places // CHUNK
    score_scale = 1.0 / math.sqrt(E)
    ranks = (rank, flip(rank, CHIP))
    turns = Turns(agenda)

    loads = [
        (x_in, x_all.at[aligned(rank * places, places)]),
        (c_in, c_all.at[aligned(rank * places, places)]),
    ]
    for at in range(2):
        for which in range(3):
            start = which * H * E + lax.div(heads * ranks[at], 2) * PAIR
            loads.append(
                (
                    qkv_w.at[:, pl.ds(pl.multiple_of(start, PAIR), 2 * PAIR)],
                    part.at[at, pl.ds(0, width), pl.ds(which * 2 * PAIR, 2 * PAIR)],
                )
            )
    for at in range(2):
        loads.append((up_w.at[:, aligned(ranks[at] * hidden, hidden)], u_w.at[at]))
        loads.append((down_w.at[aligned(ranks[at] * hidden, hidden)], d_w.at[at]))
        for h in range(heads):
            loads.append(
                (out_w.at[aligned((ranks[at] * heads + h) * E, E)], o_pairs.at[at, pl.ds(h * PAIR + E, E)])
            )
    loads = [pltpu.make_async_copy(source, target, own_sems.at[i]) for i, (source, target) in enumerate(loads)]
    for copy in loads:
        copy.start()
    links.barrier()

    def rows_of(owner, piece):
        return aligned(owner * places + piece * CHUNK, CHUNK)

    def spread(piece):
        copies = []
        for source, target in ((x_in, x_all), (c_in, c_all)):
            mine = source.at[pl.ds(piece * CHUNK, CHUNK)]
            own = target.at[rows_of(rank, piece)]
            copies.append(links.send(mine, own, links.over("seq", CHIP)))
            copies.append(links.send(mine, own, links.over("seq", CORE)))
        return copies

    def pass_on(piece):
        copies = []
        for target in (x_all, c_all):
            held = target.at[rows_of(flip(rank, CHIP), piece)]
            copies.append(links.send(held, held, links.over("seq", CORE)))
        return copies

    own_label = (lanes_of((8, 128)) == tissue_in[0]).astype(f32)
    label_buf[0] = own_label
    counting = add_up_everywhere(links, [("dp", bit) for bit in links.dp_bits], label_buf)
    next(counting)
    spreads = [spread(piece) for piece in range(pieces)]
    for at in range(2):
        for h in range(heads):
            o_pairs[at, pl.ds(h * PAIR, E), :] = jnp.zeros((E, width), bf16)
    vec_buf[0] = jnp.zeros(vec_buf.shape[1:], f32)
    for copy in loads:
        copy.wait()

    odd = heads * rank % 2
    for at in range(2):
        for tile in range(width // CHUNK):
            rows = pl.ds(tile * CHUNK, CHUNK)
            windows = [part[at, rows, pl.ds(which * 2 * PAIR, 2 * PAIR)].astype(f32) for which in range(3)]
            for number, block in enumerate(head_columns(windows, odd, heads)):
                w_pairs[at, rows, pl.ds(number * PAIR, PAIR)] = block.astype(bf16)
    start = pl.multiple_of(lax.div(heads * rank, 2) * PAIR, PAIR)
    windows = [small[pl.ds(9 + which, 1), pl.ds(start, 2 * PAIR)] for which in range(3)]
    for number, block in enumerate(head_columns(windows, odd, heads)):
        b_pairs[:, pl.ds(number * PAIR, PAIR)] = block

    for _ in counting:
        pass
    count = jnp.sum(label_buf[0] * own_label, axis=1, keepdims=True)[:1]
    weight = dp_count / (TISSUES * count)
    gain1, bias1, gain2, bias2, end_bias = [small[pl.ds(row, 1), :] for row in range(5)]

    def add_vec(row, value):
        vec_buf[0, pl.ds(row, 1), :] += value

    def total(value):
        return jnp.sum(value, axis=0, keepdims=True)

    def turn_of(half, rows):
        table = turn_in[rows, :]
        table = jnp.where(half == 1, pltpu.roll(table, PAIR - 2 * ROT, 1), table)
        lane = lanes_of(table.shape)
        cosine = jnp.where(lane < ROT, table, 1.0)
        sine = jnp.where(lane < ROT, pltpu.roll(table, PAIR - ROT, 1), 0.0)
        return cosine, sine

    second_kept = [(keep, h) for keep in (kv, q0) for h in range(heads)]

    def feed_forward(start):
        rows = aligned(start, CHUNK)
        normed, _ = normalise(x_all[rows, :].astype(f32))
        low = (c_all[rows, :].astype(f32) * weight).astype(bf16)
        c_all[rows, :] = low
        add_vec(4, total(low.astype(f32)) * (places / local))
        second = (normed * gain2 + bias2).astype(bf16)
        near = aligned(start - chip * local, CHUNK)
        rest = aligned(start + (1 - 2 * chip) * local, CHUNK)
        for tile, (keep, h) in enumerate(second_kept):
            keep[h, rest, :] = second[:, tile * PAIR : (tile + 1) * PAIR]
        for at in range(2):
            pre = dot(second, u_w[at], NN) + small[pl.ds(5 + ranks[at], 1), :]
            gate = 0.5 * (1.0 + lax.erf(pre * (1.0 / math.sqrt(2.0))))
            pairs[at, near, :] = (pre * gate).astype(bf16)
            slope = gate + pre * jnp.exp(-0.5 * pre * pre) * (1.0 / math.sqrt(2.0 * math.pi))
            pre_grads[at, near, :] = slope.astype(bf16)

    def feed_back(start):
        rows = aligned(start, CHUNK)
        near = aligned(start - chip * local, CHUNK)
        normed, _ = normalise(x_all[rows, :].astype(f32))
        low = c_all[rows, :]
        branch, second_grad = 0.0, 0.0
        for at in range(2):
            branch += dot(pairs[at, near, :], d_w[at], NN)
            pre_grad = (dot(low, d_w[at], NT) * pre_grads[at, near, :].astype(f32)).astype(bf16)
            add_vec(5 + ranks[at], total(pre_grad.astype(f32)))
            second_grad += dot(pre_grad, u_w[at], NT)
            pre_grads[at, near, :] = pre_grad
        part[0, near, :] = branch.astype(bf16)
        part[1, near, :] = (second_grad * gain2).astype(bf16)
        add_vec(2, total(second_grad * normed))
        add_vec(3, total(second_grad))

    def heads_in(start, scale):
        rows = aligned(start, CHUNK)
        normed, _ = normalise(x_all[rows, :].astype(f32))
        first = normed * gain1 + bias1
        first_t[:, rows] = jnp.transpose(first).astype(bf16)
        first = first.astype(bf16)
        low = c_all[rows, :].astype(f32) * scale
        low_t[:, rows] = jnp.transpose(low).astype(bf16)
        low = low.astype(bf16)
        joint = dot(first, w_pairs[0], NN) + b_pairs[...]
        half = lax.div(start, local)
        cosine, sine = turn_of(half, aligned(start - half * local, CHUNK))
        for h in range(heads):
            pair = joint[:, 2 * h * PAIR : (2 * h + 1) * PAIR]
            kv[h, rows, :] = (pair * cosine + swapped(pair) * sine).astype(bf16)
            pair = joint[:, (2 * h + 1) * PAIR : (2 * h + 2) * PAIR]
            pair = (pair * cosine + swapped(pair) * sine).astype(bf16).astype(f32) * score_scale
            q0[h, rows, :] = pair.astype(bf16)
            g0[h, rows, :] = dot(low, o_pairs[0, pl.ds(h * PAIR, PAIR), :], NT).astype(bf16)

    beside = flip(rank, CORE)

    def near_chunk(index, _):
        @pl.when(index == pieces)
        def _():
            for piece in range(pieces):
                spreads[piece][1].wait()
                spreads[piece][3].wait()

        owner = jnp.where(index < pieces, rank, beside)
        feed_forward(owner * places + index % pieces * CHUNK)
        return 0

    lax.fori_loop(0, 2 * pieces, near_chunk, 0)

    halves = list(halves)

    def one_group(held, full, group, order, own_sem, arrivals):
        scatter, collect = order
        blocks, size, _ = held.shape
        start = 0
        for axis, bit in scatter:
            arrived = arrivals.pop(0)
            if axis == "seq":
                copy = links.send(held.at[pl.ds(1, 1)], arrived, links.over(axis, bit))
                yield
                copy.wait()
                arrived[...] = (held[pl.ds(0, 1)].astype(f32) + arrived[...].astype(f32)).astype(bf16)
            elif axis == "line":
                size //= 4
                mine = links.line()
                copies = []
                for other in (3, 2, 1):
                    partner, place = links.along(other)
                    copies.append(
                        links.send(held.at[:, aligned(place * size, size)], arrived.at[other - 1], partner)
                    )
                yield
                for copy in copies:
                    copy.wait()
                own = held[:, aligned(mine * size, size), :].astype(f32)
                rest = [arrived[number].astype(f32) for number in range(3)]
                arrived[0] = ((own + rest[0]) + (rest[1] + rest[2])).astype(bf16)
                arrived = arrived.at[0]
                start = start + mine * size
            else:
                size //= 2
                mine = bit_at(links.dp, bit)
                copy = links.send(held.at[:, aligned((1 - mine) * size, size)], arrived, links.over(axis, bit))
                yield
                copy.wait()
                own = held[:, aligned(mine * size, size), :].astype(f32)
                arrived[...] = (own + arrived[...].astype(f32)).astype(bf16)
                start = start + mine * size
            held = arrived
        owners = [rank]

        def region(owner):
            return full.at[owner, group, aligned(start, size)]

        own = pltpu.make_async_copy(held.at[0], region(rank), own_sem)
        own.start()
        for number, (axis, bit) in enumerate(collect + [("seq", CORE)]):
            if axis == "line":
                partners = [links.along(other)[0] for other in (3, 2, 1)]
            else:
                partners = [links.over(axis, bit)]
            copies = [
                links.send(region(owner) if number else held.at[0], region(owner), partner)
                for partner in partners
                for owner in owners
            ]
            yield
            if number == 0:
                own.wait()
            for copy in copies:
                copy.wait()
            if axis == "line":
                start = start - links.line() * size
                size *= 4
            elif axis == "dp":
                start = start - bit_at(links.dp, bit) * size
                size *= 2
            else:
                owners = owners + [flip(owner, bit) for owner in owners]

    mlp_plan, head_plan = plans
    arrivals = []
    for scatter, _ in mlp_plan + head_plan:
        arrivals.append(halves[: len(scatter)])
        halves = halves[len(scatter) :]

    def begin(name, grads, full, group, order, number):
        turns.add(name, one_group(grads.at[group], full, group, order, own_sems.at[len(loads) + number], arrivals[number]))

    def fill(grads, group, real):
        spare = grads.shape[2] - real
        if spare:
            blocks = grads.shape[1]
            grads[group, :, pl.ds(real, spare), :] = jnp.zeros((blocks, spare, grads.shape[3]), bf16)

    near_rows = aligned(chip * local, local)
    far_rows = aligned((1 - chip) * local, local)
    mlp_groups = len(mlp_plan)
    mlp_rows = 2 * width // mlp_groups

    def near_back(index, _):
        feed_back(jnp.where(index < pieces, rank, beside) * places + index % pieces * CHUNK)
        return 0

    for number in range(mlp_groups):
        group = (number + mlp_groups // 2) % mlp_groups
        if number == mlp_groups // 2:
            lax.fori_loop(0, 2 * pieces, near_back, 0)
            turns.tick()
        first_tile = group % (mlp_groups // 2) * mlp_rows // PAIR
        for at in range(2):
            for tile in range(mlp_rows // PAIR):
                if group < mlp_groups // 2:
                    keep, h = second_kept[first_tile + tile]
                    term = dot(keep[h, far_rows, :], pre_grads[at], TN)
                else:
                    columns = pl.ds((first_tile + tile) * PAIR, PAIR)
                    term = dot(pairs[at, :, columns], c_all[near_rows, :], TN)
                grads_mlp[group, at, pl.ds(tile * PAIR, PAIR), :] = term.astype(bf16)
        fill(grads_mlp, group, mlp_rows)
        begin("m%d" % group, grads_mlp, full_mlp, group, mlp_plan[group], group)
        if number >= mlp_groups // 2:
            turns.tick()

    one = jnp.ones_like(weight)
    for owner in (rank, beside):

        def near_heads(piece, _):
            heads_in(owner * places + piece * CHUNK, one)
            return 0

        lax.fori_loop(0, pieces, near_heads, 0)
        turns.tick()

    far, across = flip(rank, CHIP), flip(flip(rank, CHIP), CORE)
    for piece in range(pieces):
        turns.tick()
        spreads[piece][0].wait()
        spreads[piece][2].wait()
        onward = pass_on(piece)

        def far_chunk(index, _):
            @pl.when(index == 1)
            def _():
                for copy in onward:
                    copy.wait()

            heads_in(jnp.where(index == 0, far, across) * places + piece * CHUNK, weight)
            return 0

        lax.fori_loop(0, 2, far_chunk, 0)

    blocks = length // CHUNK

    def pair_rows(block):
        return block * CHUNK // local, pl.ds(block * CHUNK % local, CHUNK)

    back = []
    for h in range(heads):
        for i in range(blocks):
            own = pl.ds(i * CHUNK, CHUNK)
            half, rows = pair_rows(i)
            q, g = q0[h, own, :], g0[h, own, :]
            spans = ([(0, i * CHUNK)] if i else []) + [(i * CHUNK, CHUNK)]
            scores = [dot(q, kv[h, pl.ds(at, size), :], NT) for at, size in spans]
            row = lax.broadcasted_iota(jnp.int32, (CHUNK, CHUNK), 0)
            column = lanes_of((CHUNK, CHUNK))
            scores[-1] = jnp.where(column <= row, scores[-1], masked_score)
            largest = functools.reduce(jnp.maximum, [jnp.max(s, axis=1, keepdims=True) for s in scores])
            probs = [jnp.exp(s - largest) for s in scores]
            inverse = 1.0 / sum(jnp.sum(p, axis=1, keepdims=True) for p in probs)
            probs = [p * inverse for p in probs]
            lows = [p.astype(bf16) for p in probs]
            attended = sum(dot(low, kv[h, pl.ds(at, size), :], NN) for low, (at, size) in zip(lows, spans))
            delta = jnp.sum(attended * g.astype(f32), axis=1, keepdims=True)
            score_grads = [
                (p * (dot(g, kv[h, pl.ds(at, size), :], NT) - delta)).astype(bf16)
                for p, (at, size) in zip(probs, spans)
            ]
            q_grad = sum(dot(s, kv[h, pl.ds(at, size), :], NN) for s, (at, size) in zip(score_grads, spans))
            q_grad = q_grad * score_scale
            cosine, sine = turn_of(half, rows)
            q_grad = q_grad * cosine - swapped(q_grad) * sine
            tail = jnp.where(lanes_of(q_grad.shape) < E, q_grad, attended)
            pairs[half, rows, pl.ds((2 * h + 1) * PAIR, PAIR)] = tail.astype(bf16)
            for s, low, (at, size) in zip(score_grads, lows, spans):
                term = dot(q, s, TN) + dot(g, low, TN)
                if at:
                    kvt[:, pl.ds(at, size)] = term
                elif i == 0:
                    kvt[:, pl.ds(0, size)] = term
                else:
                    kvt[:, pl.ds(0, size)] += term
            turns.tick()
        for i in range(blocks):
            own = pl.ds(i * CHUNK, CHUNK)
            half, rows = pair_rows(i)
            cosine, sine = turn_of(half, rows)
            pair = jnp.transpose(kvt[:, own])
            pair = pair * cosine - swapped(pair) * sine
            pairs[half, rows, pl.ds(2 * h * PAIR, PAIR)] = pair.astype(bf16)

        columns = pl.ds(2 * h * PAIR, 2 * PAIR)
        back.append(links.send(pairs.at[1 - chip, :, columns], pairs_back.at[:, columns], links.over("seq", CHIP)))

        head_groups = len(head_plan) // heads
        head_rows = width // head_groups
        for number in range(head_groups):
            group = h * head_groups + number
            rows = pl.ds(number * head_rows, head_rows)
            term = sum(
                dot(first_t[rows, pl.ds(half * local, local)], pairs[half, :, columns], NN) for half in range(2)
            )
            out_term = sum(
                dot(
                    low_t[rows, pl.ds(half * local, local)],
                    pairs[half, :, pl.ds((2 * h + 1) * PAIR, PAIR)],
                    NN,
                )
                for half in range(2)
            )
            tail = jnp.where(lanes_of(out_term.shape) < E, term[:, PAIR:], out_term)
            grads_heads[group, 0, pl.ds(0, head_rows), pl.ds(0, PAIR)] = term[:, :PAIR].astype(bf16)
            grads_heads[group, 0, pl.ds(0, head_rows), pl.ds(PAIR, PAIR)] = tail.astype(bf16)
            fill(grads_heads, group, head_rows)
            begin("a%d" % group, grads_heads, full_heads, group, head_plan[group], mlp_groups + group)
        turns.tick()

    add_vec(9 + rank, total(pairs[0].astype(f32)) + total(pairs[1].astype(f32)))
    for copy in back:
        copy.wait()

    def last(owner, piece):
        near = aligned((owner - chip * 2) * places + piece * CHUNK, CHUNK)
        normed, _ = normalise(x_all[aligned(owner * places + piece * CHUNK, CHUNK), :].astype(f32))
        own, other = pairs[chip, near, :], pairs_back[near, :]
        attn = 0.0
        for h in range(heads):
            tail = slice((2 * h + 1) * PAIR, (2 * h + 2) * PAIR)
            attn += dot(own[:, tail], o_pairs[0, pl.ds(h * PAIR, PAIR), :], NN)
            attn += dot(other[:, tail], o_pairs[1, pl.ds(h * PAIR, PAIR), :], NN)
        first_grad = dot(own, w_pairs[0], NT) + dot(other, w_pairs[1], NT)
        part[0, near, :] = (part[0, near, :].astype(f32) + attn).astype(bf16)
        part[1, near, :] = (part[1, near, :].astype(f32) + first_grad * gain1).astype(bf16)
        add_vec(0, total(first_grad * normed))
        add_vec(1, total(first_grad))

    def last_loop(owner):
        def one(piece, _):
            last(owner, piece)
            return 0

        lax.fori_loop(0, pieces, one, 0)

    last_loop(beside)
    given = part.at[:, aligned((1 - core) * places, places)]
    crossing = links.send(given, core_buf, links.over("seq", CORE))
    turns.tick()
    last_loop(rank)
    vec_steps = [("seq", CORE), ("seq", CHIP)] + [("dp", bit) for bit in links.dp_bits]
    turns.add("vec", add_up_everywhere(links, vec_steps, vec_buf))
    turns.tick()

    reload = pltpu.make_async_copy(c_in, c_all.at[aligned(rank * places, places)], own_sems.at[0])
    reload.start()
    crossing.wait()
    reload.wait()
    for piece in range(pieces):
        rows = pl.ds(piece * CHUNK, CHUNK)
        own_rows = rows_of(rank, piece)
        near = aligned(core * places + piece * CHUNK, CHUNK)
        x = x_all[own_rows, :].astype(f32)
        sums = [part[which, near, :].astype(f32) + core_buf[which, rows, :].astype(f32) for which in range(2)]
        mixed_out[rows, :] = (x + sums[0] + end_bias).astype(bf16)
        normed, inverse = normalise(x)
        scaled = sums[1]
        rows_grad = inverse * (
            scaled
            - jnp.mean(scaled, axis=-1, keepdims=True)
            - normed * jnp.mean(scaled * normed, axis=-1, keepdims=True)
        )
        input_grad_out[rows, :] = c_all[own_rows, :].astype(f32) * weight + rows_grad
    turns.finish()
    vec_out[...] = vec_buf[0]


def padded(rows, dp_count):
    return -(-rows // (16 * dp_count)) * 16 * dp_count


def arrivals_of(order, blocks, rows, width):
    shapes = []
    for axis, _ in order[0]:
        if axis == "seq":
            blocks = 1
        else:
            rows //= 4 if axis == "line" else 2
        shape = (blocks, rows, width)
        shapes.append(pltpu.VMEM((3,) + shape if axis == "line" else shape, bf16))
    return shapes


def layer(dp_count, seq_count, *operands):
    places, width = operands[0].shape
    length = places * seq_count
    local = length // 2
    heads = H // seq_count
    hidden = operands[6].shape[1] // seq_count
    bits = bits_of(dp_count)
    mlp_plan = orders_of(dp_count, MLP_PLAN, 2, 2)
    head_plan = orders_of(dp_count, HEAD_PLAN, 1, heads)
    mlp_rows = padded(2 * width // len(mlp_plan), dp_count)
    head_rows = padded(width * heads // len(head_plan), dp_count)
    pieces = places // CHUNK
    copies = bits + 6 * pieces + (len(mlp_plan) + len(head_plan)) * 20
    copies += heads + 1 + bits + 2
    loads = 2 + 6 + 2 * (2 + heads)
    scratch = [
        pltpu.VMEM((length, width), bf16),
        pltpu.VMEM((length, width), bf16),
        pltpu.VMEM((width, length), bf16),
        pltpu.VMEM((width, length), bf16),
        pltpu.VMEM((heads, length, PAIR), bf16),
        pltpu.VMEM((heads, length, PAIR), bf16),
        pltpu.VMEM((heads, length, PAIR), bf16),
        pltpu.VMEM((2, local, 2 * heads * PAIR), bf16),
        pltpu.VMEM((local, 2 * heads * PAIR), bf16),
        pltpu.VMEM((2, width, 2 * heads * PAIR), bf16),
        pltpu.VMEM((1, 2 * heads * PAIR), f32),
        pltpu.VMEM((2, heads * PAIR, width), bf16),
        pltpu.VMEM((2, width, hidden), bf16),
        pltpu.VMEM((2, hidden, width), bf16),
        pltpu.VMEM((2, local, hidden), bf16),
        pltpu.VMEM((2, local, width), bf16),
        pltpu.VMEM((len(mlp_plan), 2, mlp_rows, width), bf16),
        pltpu.VMEM((len(head_plan), 1, head_rows, 2 * PAIR), bf16),
        pltpu.VMEM((2, places, width), bf16),
        pltpu.VMEM((PAIR, length), f32),
        pltpu.VMEM((bits + 1, 8, 128), f32),
        pltpu.VMEM((bits + 3, VECTOR_ROWS, width), f32),
        pltpu.SemaphoreType.DMA((copies,)),
        pltpu.SemaphoreType.DMA((copies,)),
        pltpu.SemaphoreType.DMA((loads + len(mlp_plan) + len(head_plan),)),
    ]
    for order in mlp_plan:
        scratch += arrivals_of(order, 2, mlp_rows, width)
    for order in head_plan:
        scratch += arrivals_of(order, 1, head_rows, 2 * PAIR)
    smem = pl.BlockSpec(memory_space=pltpu.SMEM)
    return pl.pallas_call(
        functools.partial(
            layer_kernel, dp_count, (mlp_plan, head_plan), AGENDA if dp_count == 8 else []
        ),
        out_shape=(
            jax.ShapeDtypeStruct((seq_count, len(mlp_plan), mlp_rows, width), bf16),
            jax.ShapeDtypeStruct((seq_count, len(head_plan), head_rows, 2 * PAIR), bf16),
            jax.ShapeDtypeStruct((VECTOR_ROWS, width), f32),
            jax.ShapeDtypeStruct((places, width), bf16),
            jax.ShapeDtypeStruct((places, width), f32),
        ),
        in_specs=[ANY, ANY, smem, VMEM, ANY, ANY, ANY, ANY, VMEM],
        out_specs=(ANY, ANY, VMEM, VMEM, VMEM),
        scratch_shapes=scratch,
        compiler_params=pltpu.CompilerParams(
            collective_id=0, has_side_effects=True, vmem_limit_bytes=63 * 2**20
        ),
        name="layer",
    )(*operands)


def finish_kernel(mlp_in, heads_in, vec, mixed_in, grad_in, *rest):
    up_out, down_out, qkv_out, out_out, mixed_out, grad_out = rest[:6]
    vectors = rest[6:14]
    mlp, mix, mixed, grad, up_wide, down_wide, qkv_wide, out_wide, in_sems, out_sems = rest[14:]
    owners, mlp_groups, rows, width = mlp.shape
    _, head_groups, mix_rows, _ = mix.shape
    heads = H // owners
    per_head = head_groups // heads
    begun = []

    def begin(source, target, sems):
        copy = pltpu.make_async_copy(source, target, sems.at[begin.used])
        begin.used += 1
        copy.start()
        return copy

    begin.used = 0
    arriving = {"mixed": begin(mixed_in, mixed, in_sems), "grad": begin(grad_in, grad, in_sems)}
    for group in range(per_head):
        for r in range(owners):
            for h in range(heads):
                at = h * per_head + group
                arriving["mix", r, at] = begin(heads_in.at[r, at, pl.ds(0, mix_rows)], mix.at[r, at], in_sems)
    for group in range(mlp_groups):
        for r in range(owners):
            arriving["mlp", r, group] = begin(mlp_in.at[r, group, pl.ds(0, rows)], mlp.at[r, group], in_sems)
    begin.used = 0

    gain1, bias1, gain2, bias2, low1, low2, qkv, up = vectors
    for target, row in zip((gain1, bias1, gain2, bias2, low1, low2), (0, 1, 2, 3, 4, 4)):
        target[...] = vec[row]
    parts = [[], [], []]
    for r in range(owners):
        line = vec[pl.ds(5 + owners + r, 1), :]
        for h in range(heads):
            at = 2 * h * PAIR
            parts[0].append(line[:, at + PAIR : at + PAIR + E])
            parts[1].append(line[:, at : at + E])
            parts[2].append(line[:, at + E : at + PAIR])
    qkv[...] = jnp.concatenate(parts[0] + parts[1] + parts[2], axis=1)[0]
    up[...] = jnp.concatenate([vec[pl.ds(5 + r, 1), :] for r in range(owners)], axis=1)[0]

    tile = PAIR
    for group in range(per_head):
        for r in range(owners):
            for h in range(heads):
                arriving["mix", r, h * per_head + group].wait()
        for sub in range(mix_rows // tile):
            at_rows = pl.ds(group * mix_rows + sub * tile, tile)
            for r in range(owners):
                for h in range(heads):
                    head = r * heads + h
                    block = mix[r, h * per_head + group, pl.ds(sub * tile, tile), :].astype(f32)
                    tail = block[:, PAIR:]
                    qkv_wide[at_rows, pl.ds(head * E, E)] = tail[:, :E]
                    qkv_wide[at_rows, pl.ds((H + head) * E, E)] = block[:, :E]
                    qkv_wide[at_rows, pl.ds((2 * H + head) * E, E)] = block[:, E:PAIR]
                    out_wide[pl.ds(head * E, E), at_rows] = jnp.transpose(tail)[E:, :]
            begun.append(begin(qkv_wide.at[at_rows], qkv_out.at[at_rows], out_sems))
    begun.append(begin(out_wide, out_out, out_sems))
    for name, held, target in (("mixed", mixed, mixed_out), ("grad", grad, grad_out)):
        arriving[name].wait()
        begun.append(begin(held, target, out_sems))
    for group in range(mlp_groups):
        for r in range(owners):
            arriving["mlp", r, group].wait()
            wide = mlp[r, group].astype(f32)
            if group < mlp_groups // 2:
                place = (pl.ds(group * rows, rows), pl.ds(r * width, width))
                target, held = up_out, up_wide
            else:
                place = (pl.ds(r * width + (group - mlp_groups // 2) * rows, rows), pl.ds(0, width))
                target, held = down_out, down_wide
            held[place] = wide
            begun.append(begin(held.at[place], target.at[place], out_sems))
    for copy in begun:
        copy.wait()


def finish(full_mlp, full_heads, vec, mixed, input_grad):
    owners, mlp_groups, _, width = full_mlp.shape
    head_groups = full_heads.shape[1]
    rows = 2 * width // mlp_groups
    mix_rows = width * (H // owners) // head_groups
    lines = [width] * 6 + [3 * H * E, owners * width]
    wides = [(width, owners * width), (owners * width, width), (width, 3 * H * E), (H * E, width)]
    count = owners * (mlp_groups + head_groups) + 2
    return pl.pallas_call(
        finish_kernel,
        out_shape=tuple(jax.ShapeDtypeStruct(shape, f32) for shape in wides)
        + (
            jax.ShapeDtypeStruct(mixed.shape, mixed.dtype),
            jax.ShapeDtypeStruct(input_grad.shape, input_grad.dtype),
        )
        + tuple(jax.ShapeDtypeStruct((size,), f32) for size in lines),
        in_specs=[ANY, ANY, VMEM, ANY, ANY],
        out_specs=(ANY,) * 6 + (VMEM,) * len(lines),
        scratch_shapes=[
            pltpu.VMEM((owners, mlp_groups, rows, width), bf16),
            pltpu.VMEM((owners, head_groups, mix_rows, 2 * PAIR), bf16),
            pltpu.VMEM(mixed.shape, mixed.dtype),
            pltpu.VMEM(input_grad.shape, input_grad.dtype),
        ]
        + [pltpu.VMEM(shape, f32) for shape in wides]
        + [
            pltpu.SemaphoreType.DMA((count,)),
            pltpu.SemaphoreType.DMA((owners * mlp_groups + width // PAIR + 3,)),
        ],
        compiler_params=pltpu.CompilerParams(vmem_limit_bytes=60 * 2**20),
        name="finish",
    )(full_mlp, full_heads, vec, mixed, input_grad)


def turn_table(length):
    half = ROT // 2
    frequency = (10000.0 ** (-2.0 * np.arange(half, dtype=np.float32) / ROT)).astype(np.float32)
    angles = np.arange(length, dtype=np.float32)[:, None] * frequency[None, :]
    cosine, sine = np.cos(angles), np.sin(angles)
    table = np.concatenate([cosine, cosine, -sine, sine], axis=1).astype(np.float32)
    rest = np.zeros((length // 2, PAIR - 4 * ROT), np.float32)
    return jnp.asarray(np.concatenate([table[: length // 2], table[length // 2 :], rest], axis=1))


def body(
    tokens,
    tissue,
    norm1_gain,
    norm1_bias,
    norm2_gain,
    norm2_bias,
    qkv_weight,
    qkv_bias,
    out_weight,
    out_bias,
    up_weight,
    up_bias,
    down_weight,
    down_bias,
    cotangent,
):
    dp_count, seq_count = lax.axis_size("dp"), lax.axis_size("seq")
    _, places, width = tokens.shape
    lines = [norm1_gain, norm1_bias, norm2_gain, norm2_bias, out_bias + down_bias]
    for bias in (up_bias, qkv_bias):
        lines += [bias[at : at + width] for at in range(0, bias.shape[0], width)]
    row = lax.broadcasted_iota(jnp.int32, (SMALL_ROWS, width), 0)
    small = jnp.zeros((SMALL_ROWS, width), f32)
    for number, line in enumerate(lines):
        small = jnp.where(row == number, line[None], small)
    full_mlp, full_heads, vec, mixed, input_grad = layer(
        dp_count,
        seq_count,
        tokens.reshape(places, width),
        cotangent.reshape(places, width),
        tissue,
        small,
        qkv_weight,
        out_weight,
        up_weight,
        down_weight,
        turn_table(places * seq_count),
    )
    results = finish(full_mlp, full_heads, vec, mixed, input_grad)
    up, down, qkv, out, mixed, input_grad, gain1, bias1, gain2, bias2, low1, low2, qkv_b, up_b = results
    return (
        mixed.reshape(tokens.shape),
        input_grad.reshape(tokens.shape),
        gain1,
        bias1,
        gain2,
        bias2,
        qkv,
        qkv_b,
        out,
        low1,
        up,
        up_b,
        down,
        low2,
    )


def solution(mesh):
    rows = P("dp", "seq", None)
    return jax.shard_map(
        body,
        mesh=mesh,
        in_specs=(rows, P("dp")) + (P(),) * 12 + (rows,),
        out_specs=(rows, rows) + (P(),) * 12,
        check_vma=False,
    )
```

```python
import functools
import math

import jax
import jax.numpy as jnp
import numpy as np
from jax import lax
from jax.experimental import pallas as pl
from jax.experimental.pallas import tpu as pltpu
from jax.sharding import PartitionSpec as P

H = 12
E = 64
ROT = 16
TISSUES = 16
norm_eps = 1e-05
masked_score = -1e30
f32 = jnp.float32
bf16 = jnp.bfloat16
MESH = pl.DeviceIdType.MESH
ANY = pl.BlockSpec(memory_space=pl.ANY)
VMEM = pl.BlockSpec(memory_space=pltpu.VMEM)
VECTOR_ROWS = 16
CORE, CHIP = 1, 2
PAIR = 2 * E
CHUNK = 256

NN = ((1,), (0,))
NT = ((1,), (1,))
TN = ((0,), (0,))


def dot(a, b, dims):
    return lax.dot_general(a, b, (dims, ((), ())), preferred_element_type=f32)


def bits_of(count):
    return count.bit_length() - 1


def bit_at(index, bit):
    return lax.div(index, bit) % 2


def flip(index, bit):
    return index + bit - 2 * bit * bit_at(index, bit)


def aligned(start, size):
    return pl.ds(pl.multiple_of(start, size), size)


class Links:
    def __init__(self, dp_count, send_sems, recv_sems):
        self.dp = lax.axis_index("dp")
        self.seq = lax.axis_index("seq")
        self.dp_bits = [1 << j for j in range(bits_of(dp_count))]
        self.send_sems, self.recv_sems, self.used = send_sems, recv_sems, 0

    def over(self, axis, bit):
        if axis == "seq":
            return (self.dp, flip(self.seq, bit))
        return (flip(self.dp, bit), self.seq)

    def line(self):
        return lax.div(self.dp, 2) % 4

    def along(self, other):
        dp = self.dp
        for bit in (1, 2):
            if other & bit:
                dp = flip(dp, 2 * bit)
        return (dp, self.seq), lax.div(dp, 2) % 4

    def barrier(self):
        semaphore = pltpu.get_barrier_semaphore()
        partners = [self.over("seq", CORE), self.over("seq", CHIP)]
        partners += [self.over("dp", bit) for bit in self.dp_bits]
        if len(self.dp_bits) == 3:
            partners.append(self.along(3)[0])
        for partner in partners:
            pl.semaphore_signal(semaphore, inc=1, device_id=partner, device_id_type=MESH)
        pl.semaphore_wait(semaphore, len(partners))

    def send(self, source, target, partner):
        copy = pltpu.make_async_remote_copy(
            src_ref=source,
            dst_ref=target,
            send_sem=self.send_sems.at[self.used],
            recv_sem=self.recv_sems.at[self.used],
            device_id=partner,
            device_id_type=MESH,
        )
        self.used += 1
        copy.start()
        return copy


def add_up_everywhere(links, steps, buffer):
    for number, (axis, bit) in enumerate(steps):
        copy = links.send(buffer.at[0], buffer.at[number + 1], links.over(axis, bit))
        yield
        copy.wait()
        buffer[0] = buffer[0] + buffer[number + 1]


def axes_of(word):
    steps = {"x": ("seq", CHIP), "Z": ("line", 4), "y": ("dp", 1), "z": ("dp", 2), "w": ("dp", 4)}
    return [steps[letter] for letter in word]


def plain_order(dp_count, blocks):
    scatter = [("dp", 1 << j) for j in range(bits_of(dp_count))]
    collect = [("seq", CHIP)] + scatter[::-1]
    return (scatter + ([("seq", CHIP)] if blocks == 2 else []), collect)


def orders_of(dp_count, plan, blocks, few):
    if dp_count == 8:
        return [(axes_of(scatter), axes_of(collect)) for scatter, collect in plan]
    return [plain_order(dp_count, blocks)] * few


MLP_PLAN = [
    ("yxZ", "Zxy"),
    ("yxzw", "wzyx"),
    ("zyxw", "wxyz"),
    ("yZx", "Zxy"),
    ("zyxw", "xwyz"),
    ("zxyw", "wxyz"),
]
HEAD_PLAN = [
    ("yzw", "wzyx"),
    ("yzw", "wzyx"),
    ("yZ", "Zxy"),
]
AGENDA = [
    [],
    [],
    [],
    [],
    [],
    [],
    [],
    ["m0", "m4", "m5", "m3"],
    [],
    [],
    ["m4", "m2"],
    ["m1", "m0"],
    [],
    [],
    ["m4", "m2"],
    ["m0", "m3", "m5", "m1"],
    [],
    [],
    [],
    [],
    ["m3", "m4"],
    ["m5", "m0"],
    ["m1"],
    [],
    [],
    [],
    ["m4", "a0", "m1"],
    ["m2"],
    ["m0"],
    [],
    [],
    ["m3", "m4", "m5"],
    ["m1", "a0"],
    ["m2", "m5", "a1"],
    ["m1", "a0", "a1", "a0", "a2", "m5", "m2", "a0", "a1", "a2", "m1", "m3", "a1", "m4"],
    [],
    ["a2", "m5", "m2"],
    ["vec", "a0", "a1", "m4", "m3", "vec", "a2", "m2", "a1", "vec", "m3", "m1", "m0", "m5", "a0", "m0", "a2", "m2", "vec", "a1", "m4", "a0", "a2", "m2", "m5", "m1", "vec", "a1"],
]


class Turns:
    def __init__(self, agenda):
        self.agenda, self.tasks, self.ticks = agenda, {}, 0

    def add(self, name, task):
        self.tasks[name] = task
        self.advance(name)

    def advance(self, name):
        task = self.tasks.pop(name, None)
        if task is not None and next(task, "done") != "done":
            self.tasks[name] = task

    def tick(self):
        if self.ticks < len(self.agenda):
            for name in self.agenda[self.ticks]:
                self.advance(name)
        elif not self.agenda and self.tasks:
            self.advance(next(iter(self.tasks)))
        self.ticks += 1

    def finish(self):
        while self.ticks < len(self.agenda):
            self.tick()
        while self.tasks:
            self.advance(next(iter(self.tasks)))


def normalise(rows):
    centred = rows - jnp.mean(rows, axis=-1, keepdims=True)
    inverse = lax.rsqrt(jnp.mean(centred * centred, axis=-1, keepdims=True) + norm_eps)
    return centred * inverse, inverse


def lanes_of(shape):
    return lax.broadcasted_iota(jnp.int32, shape, 1)


def swapped(pairs):
    half = ROT // 2
    return jnp.where(
        lanes_of(pairs.shape) < half, pltpu.roll(pairs, PAIR - half, 1), pltpu.roll(pairs, half, 1)
    )


def head_columns(windows, odd, heads):
    def put(window, h, to):
        def at(place):
            block = window[:, place // 2 * PAIR : (place // 2 + 1) * PAIR]
            return block if place % 2 == to else pltpu.roll(block, E, 1)

        return jnp.where(odd == 1, at(h + 1), at(h))

    query, key, value = windows
    low = lanes_of((key.shape[0], PAIR)) < E
    blocks = []
    for h in range(heads):
        blocks.append(jnp.where(low, put(key, h, 0), put(value, h, 1)))
        blocks.append(jnp.where(low, put(query, h, 0), 0.0))
    return blocks


SMALL_ROWS = 16


def layer_kernel(
    dp_count,
    plans,
    agenda,
    x_in,
    c_in,
    tissue_in,
    gain1_in,
    bias1_in,
    gain2_in,
    bias2_in,
    out_b,
    down_b,
    up_b,
    qkv_b,
    qkv_w,
    out_w,
    up_w,
    down_w,
    turn_in,
    full_mlp,
    full_heads,
    vec_out,
    mixed_out,
    input_grad_out,
    x_all,
    c_all,
    low_t,
    first_t,
    kv,
    q0,
    g0,
    pairs,
    pairs_back,
    w_pairs,
    b_pairs,
    o_pairs,
    u_w,
    d_w,
    pre_grads,
    part,
    grads_mlp,
    grads_heads,
    core_buf,
    kvt,
    small,
    label_buf,
    vec_buf,
    sends,
    recvs,
    own_sems,
    *halves,
):
    links = Links(dp_count, sends, recvs)
    rank = links.seq
    chip, core = bit_at(rank, CHIP), bit_at(rank, CORE)
    places, width = x_in.shape
    length = x_all.shape[0]
    local = length // 2
    heads = kv.shape[0]
    hidden = u_w.shape[2]
    pieces = places // CHUNK
    score_scale = 1.0 / math.sqrt(E)
    ranks = (rank, flip(rank, CHIP))
    turns = Turns(agenda)

    loads = [
        (x_in, x_all.at[aligned(rank * places, places)]),
        (c_in, c_all.at[aligned(rank * places, places)]),
    ]
    for at in range(2):
        loads.append((up_w.at[:, aligned(ranks[at] * hidden, hidden)], u_w.at[at]))
    for at in range(2):
        loads.append((down_w.at[aligned(ranks[at] * hidden, hidden)], d_w.at[at]))
    for at in range(2):
        for which in range(3):
            start = which * H * E + lax.div(heads * ranks[at], 2) * PAIR
            loads.append(
                (
                    qkv_w.at[:, pl.ds(pl.multiple_of(start, PAIR), 2 * PAIR)],
                    first_t.at[:, pl.ds((3 * at + which) * 2 * PAIR, 2 * PAIR)],
                )
            )
    for at in range(2):
        for h in range(heads):
            loads.append(
                (out_w.at[aligned((ranks[at] * heads + h) * E, E)], o_pairs.at[at, pl.ds(h * PAIR + E, E)])
            )
    loads = [pltpu.make_async_copy(source, target, own_sems.at[i]) for i, (source, target) in enumerate(loads)]
    for copy in loads:
        copy.start()
    links.barrier()

    def rows_of(owner, piece):
        return aligned(owner * places + piece * CHUNK, CHUNK)

    def spread(piece):
        copies = []
        for source, target in ((x_in, x_all), (c_in, c_all)):
            mine = source.at[pl.ds(piece * CHUNK, CHUNK)]
            own = target.at[rows_of(rank, piece)]
            copies.append(links.send(mine, own, links.over("seq", CHIP)))
            copies.append(links.send(mine, own, links.over("seq", CORE)))
        return copies

    def pass_on(piece):
        copies = []
        for target in (x_all, c_all):
            held = target.at[rows_of(flip(rank, CHIP), piece)]
            copies.append(links.send(held, held, links.over("seq", CORE)))
        return copies

    own_label = (lanes_of((8, 128)) == tissue_in[0]).astype(f32)
    label_buf[0] = own_label
    counting = add_up_everywhere(links, [("dp", bit) for bit in links.dp_bits], label_buf)
    next(counting)
    spreads = [spread(piece) for piece in range(pieces)]
    for at in range(2):
        for h in range(heads):
            o_pairs[at, pl.ds(h * PAIR, E), :] = jnp.zeros((E, width), bf16)
    vec_buf[0] = jnp.zeros(vec_buf.shape[1:], f32)
    for copy in loads[:6]:
        copy.wait()

    for row, line in enumerate((gain1_in, bias1_in, gain2_in, bias2_in)):
        small[pl.ds(row, 1), :] = line[...].reshape(1, width)
    small[pl.ds(4, 1), :] = (out_b[...] + down_b[...]).reshape(1, width)
    for first_row, lines in ((5, up_b), (9, qkv_b)):
        for row in range(lines.shape[0] // width):
            small[pl.ds(first_row + row, 1), :] = lines[pl.ds(row * width, width)].reshape(1, width)
    gain1, bias1, gain2, bias2, end_bias = [small[pl.ds(row, 1), :] for row in range(5)]

    def add_vec(row, value):
        vec_buf[0, pl.ds(row, 1), :] += value

    def total(value):
        return jnp.sum(value, axis=0, keepdims=True)

    def turn_of(half, rows):
        table = turn_in[rows, :]
        table = jnp.where(half == 1, pltpu.roll(table, PAIR - 2 * ROT, 1), table)
        lane = lanes_of(table.shape)
        cosine = jnp.where(lane < ROT, table, 1.0)
        sine = jnp.where(lane < ROT, pltpu.roll(table, PAIR - ROT, 1), 0.0)
        return cosine, sine

    second_kept = [(keep, h) for keep in (kv, q0) for h in range(heads)]

    def feed_forward(start):
        rows = aligned(start, CHUNK)
        normed, _ = normalise(x_all[rows, :].astype(f32))
        second = (normed * gain2 + bias2).astype(bf16)
        near = aligned(start - chip * local, CHUNK)
        rest = aligned(start + (1 - 2 * chip) * local, CHUNK)
        for tile, (keep, h) in enumerate(second_kept):
            keep[h, rest, :] = second[:, tile * PAIR : (tile + 1) * PAIR]
        for at in range(2):
            pre = dot(second, u_w[at], NN) + small[pl.ds(5 + ranks[at], 1), :]
            gate = 0.5 * (1.0 + lax.erf(pre * (1.0 / math.sqrt(2.0))))
            pairs[at, near, :] = (pre * gate).astype(bf16)
            slope = gate + pre * jnp.exp(-0.5 * pre * pre) * (1.0 / math.sqrt(2.0 * math.pi))
            pre_grads[at, near, :] = slope.astype(bf16)

    def feed_back(start):
        rows = aligned(start, CHUNK)
        near = aligned(start - chip * local, CHUNK)
        normed, _ = normalise(x_all[rows, :].astype(f32))
        low = c_all[rows, :]
        branch, second_grad = 0.0, 0.0
        for at in range(2):
            branch += dot(pairs[at, near, :], d_w[at], NN)
            pre_grad = (dot(low, d_w[at], NT) * pre_grads[at, near, :].astype(f32)).astype(bf16)
            add_vec(5 + ranks[at], total(pre_grad.astype(f32)))
            second_grad += dot(pre_grad, u_w[at], NT)
            pre_grads[at, near, :] = pre_grad
        part[0, near, :] = branch.astype(bf16)
        part[1, near, :] = (second_grad * gain2).astype(bf16)
        add_vec(2, total(second_grad * normed))
        add_vec(3, total(second_grad))

    def heads_in(start, scale):
        rows = aligned(start, CHUNK)
        normed, _ = normalise(x_all[rows, :].astype(f32))
        first = normed * gain1 + bias1
        first_t[:, rows] = jnp.transpose(first).astype(bf16)
        first = first.astype(bf16)
        low = c_all[rows, :].astype(f32) * scale
        low_t[:, rows] = jnp.transpose(low).astype(bf16)
        low = low.astype(bf16)
        joint = dot(first, w_pairs[0], NN) + b_pairs[...]
        half = lax.div(start, local)
        cosine, sine = turn_of(half, aligned(start - half * local, CHUNK))
        for h in range(heads):
            pair = joint[:, 2 * h * PAIR : (2 * h + 1) * PAIR]
            kv[h, rows, :] = (pair * cosine + swapped(pair) * sine).astype(bf16)
            pair = joint[:, (2 * h + 1) * PAIR : (2 * h + 2) * PAIR]
            pair = (pair * cosine + swapped(pair) * sine).astype(bf16).astype(f32) * score_scale
            q0[h, rows, :] = pair.astype(bf16)
            g0[h, rows, :] = dot(low, o_pairs[0, pl.ds(h * PAIR, PAIR), :], NT).astype(bf16)

    beside = flip(rank, CORE)

    def near_rows_of(index):
        return jnp.where(index < pieces, rank, beside) * places + index % pieces * CHUNK

    def near_loop(first_one, last_one, step):
        def one(index, _):
            step(near_rows_of(index))
            return 0

        lax.fori_loop(first_one, last_one, one, 0)

    near_loop(0, pieces, feed_forward)
    next(counting, None)
    for piece in range(pieces):
        spreads[piece][1].wait()
        spreads[piece][3].wait()
    near_loop(pieces, 2 * pieces, feed_forward)

    for _ in counting:
        pass
    count = jnp.sum(label_buf[0] * own_label, axis=1, keepdims=True)[:1]
    weight = dp_count / (TISSUES * count)

    def weigh(start):
        rows = aligned(start, CHUNK)
        low = (c_all[rows, :].astype(f32) * weight).astype(bf16)
        c_all[rows, :] = low
        add_vec(4, total(low.astype(f32)) * (places / local))

    near_loop(0, 2 * pieces, weigh)

    halves = list(halves)

    def one_group(held, full, group, order, own_sem, arrivals):
        scatter, collect = order
        blocks, size, _ = held.shape
        start = 0
        for axis, bit in scatter:
            arrived = arrivals.pop(0)
            if axis == "seq":
                copy = links.send(held.at[pl.ds(1, 1)], arrived, links.over(axis, bit))
                yield
                copy.wait()
                arrived[...] = (held[pl.ds(0, 1)].astype(f32) + arrived[...].astype(f32)).astype(bf16)
            elif axis == "line":
                size //= 4
                mine = links.line()
                copies = []
                for other in (3, 2, 1):
                    partner, place = links.along(other)
                    copies.append(
                        links.send(held.at[:, aligned(place * size, size)], arrived.at[other - 1], partner)
                    )
                yield
                for copy in copies:
                    copy.wait()
                own = held[:, aligned(mine * size, size), :].astype(f32)
                rest = [arrived[number].astype(f32) for number in range(3)]
                arrived[0] = ((own + rest[0]) + (rest[1] + rest[2])).astype(bf16)
                arrived = arrived.at[0]
                start = start + mine * size
            else:
                size //= 2
                mine = bit_at(links.dp, bit)
                copy = links.send(held.at[:, aligned((1 - mine) * size, size)], arrived, links.over(axis, bit))
                yield
                copy.wait()
                own = held[:, aligned(mine * size, size), :].astype(f32)
                arrived[...] = (own + arrived[...].astype(f32)).astype(bf16)
                start = start + mine * size
            held = arrived
        owners = [rank]

        def region(owner):
            return full.at[owner, group, aligned(start, size)]

        own = pltpu.make_async_copy(held.at[0], region(rank), own_sem)
        own.start()
        for number, (axis, bit) in enumerate(collect + [("seq", CORE)]):
            if axis == "line":
                partners = [links.along(other)[0] for other in (3, 2, 1)]
            else:
                partners = [links.over(axis, bit)]
            copies = [
                links.send(region(owner) if number else held.at[0], region(owner), partner)
                for partner in partners
                for owner in owners
            ]
            yield
            if number == 0:
                own.wait()
            for copy in copies:
                copy.wait()
            if axis == "line":
                start = start - links.line() * size
                size *= 4
            elif axis == "dp":
                start = start - bit_at(links.dp, bit) * size
                size *= 2
            else:
                owners = owners + [flip(owner, bit) for owner in owners]

    mlp_plan, head_plan = plans
    arrivals = []
    for scatter, _ in mlp_plan + head_plan:
        arrivals.append(halves[: len(scatter)])
        halves = halves[len(scatter) :]

    def begin(name, grads, full, group, order, number):
        turns.add(name, one_group(grads.at[group], full, group, order, own_sems.at[len(loads) + number], arrivals[number]))

    def fill(grads, group, real):
        spare = grads.shape[2] - real
        if spare:
            blocks = grads.shape[1]
            grads[group, :, pl.ds(real, spare), :] = jnp.zeros((blocks, spare, grads.shape[3]), bf16)

    near_rows = aligned(chip * local, local)
    far_rows = aligned((1 - chip) * local, local)
    mlp_groups = len(mlp_plan)
    mlp_rows = 2 * width // mlp_groups

    for number in range(mlp_groups):
        group = (number + mlp_groups // 2) % mlp_groups
        if number == mlp_groups // 2:
            near_loop(0, 2 * pieces, feed_back)
            turns.tick()
        first_tile = group % (mlp_groups // 2) * mlp_rows // PAIR
        for at in range(2):
            for tile in range(mlp_rows // PAIR):
                if group < mlp_groups // 2:
                    keep, h = second_kept[first_tile + tile]
                    term = dot(keep[h, far_rows, :], pre_grads[at], TN)
                else:
                    columns = pl.ds((first_tile + tile) * PAIR, PAIR)
                    term = dot(pairs[at, :, columns], c_all[near_rows, :], TN)
                grads_mlp[group, at, pl.ds(tile * PAIR, PAIR), :] = term.astype(bf16)
        fill(grads_mlp, group, mlp_rows)
        begin("m%d" % group, grads_mlp, full_mlp, group, mlp_plan[group], group)
        if number >= mlp_groups // 2:
            turns.tick()

    for copy in loads[6:]:
        copy.wait()
    odd = heads * rank % 2
    for at in range(2):
        for tile in range(width // CHUNK):
            rows = pl.ds(tile * CHUNK, CHUNK)
            windows = [first_t[rows, pl.ds((3 * at + which) * 2 * PAIR, 2 * PAIR)].astype(f32) for which in range(3)]
            for number, block in enumerate(head_columns(windows, odd, heads)):
                w_pairs[at, rows, pl.ds(number * PAIR, PAIR)] = block.astype(bf16)
    start = pl.multiple_of(lax.div(heads * rank, 2) * PAIR, PAIR)
    windows = [small[pl.ds(9 + which, 1), pl.ds(start, 2 * PAIR)] for which in range(3)]
    for number, block in enumerate(head_columns(windows, odd, heads)):
        b_pairs[:, pl.ds(number * PAIR, PAIR)] = block

    one = jnp.ones_like(weight)
    for owner in (rank, beside):

        def near_heads(piece, _):
            heads_in(owner * places + piece * CHUNK, one)
            return 0

        lax.fori_loop(0, pieces, near_heads, 0)
        turns.tick()

    far, across = flip(rank, CHIP), flip(flip(rank, CHIP), CORE)
    for piece in range(pieces):
        turns.tick()
        spreads[piece][0].wait()
        spreads[piece][2].wait()
        onward = pass_on(piece)

        def far_chunk(index, _):
            @pl.when(index == 1)
            def _():
                for copy in onward:
                    copy.wait()

            heads_in(jnp.where(index == 0, far, across) * places + piece * CHUNK, weight)
            return 0

        lax.fori_loop(0, 2, far_chunk, 0)

    blocks = length // CHUNK

    def pair_rows(block):
        return block * CHUNK // local, pl.ds(block * CHUNK % local, CHUNK)

    back = []
    for h in range(heads):
        for i in range(blocks):
            own = pl.ds(i * CHUNK, CHUNK)
            half, rows = pair_rows(i)
            q, g = q0[h, own, :], g0[h, own, :]
            spans = ([(0, i * CHUNK)] if i else []) + [(i * CHUNK, CHUNK)]
            scores = [dot(q, kv[h, pl.ds(at, size), :], NT) for at, size in spans]
            row = lax.broadcasted_iota(jnp.int32, (CHUNK, CHUNK), 0)
            column = lanes_of((CHUNK, CHUNK))
            scores[-1] = jnp.where(column <= row, scores[-1], masked_score)
            largest = functools.reduce(jnp.maximum, [jnp.max(s, axis=1, keepdims=True) for s in scores])
            probs = [jnp.exp(s - largest) for s in scores]
            inverse = 1.0 / sum(jnp.sum(p, axis=1, keepdims=True) for p in probs)
            probs = [p * inverse for p in probs]
            lows = [p.astype(bf16) for p in probs]
            attended = sum(dot(low, kv[h, pl.ds(at, size), :], NN) for low, (at, size) in zip(lows, spans))
            delta = jnp.sum(attended * g.astype(f32), axis=1, keepdims=True)
            score_grads = [
                (p * (dot(g, kv[h, pl.ds(at, size), :], NT) - delta)).astype(bf16)
                for p, (at, size) in zip(probs, spans)
            ]
            q_grad = sum(dot(s, kv[h, pl.ds(at, size), :], NN) for s, (at, size) in zip(score_grads, spans))
            q_grad = q_grad * score_scale
            cosine, sine = turn_of(half, rows)
            q_grad = q_grad * cosine - swapped(q_grad) * sine
            tail = jnp.where(lanes_of(q_grad.shape) < E, q_grad, attended)
            pairs[half, rows, pl.ds((2 * h + 1) * PAIR, PAIR)] = tail.astype(bf16)
            for s, low, (at, size) in zip(score_grads, lows, spans):
                term = dot(q, s, TN) + dot(g, low, TN)
                if at:
                    kvt[:, pl.ds(at, size)] = term
                elif i == 0:
                    kvt[:, pl.ds(0, size)] = term
                else:
                    kvt[:, pl.ds(0, size)] += term
            turns.tick()
        for i in range(blocks):
            own = pl.ds(i * CHUNK, CHUNK)
            half, rows = pair_rows(i)
            cosine, sine = turn_of(half, rows)
            pair = jnp.transpose(kvt[:, own])
            pair = pair * cosine - swapped(pair) * sine
            pairs[half, rows, pl.ds(2 * h * PAIR, PAIR)] = pair.astype(bf16)

        columns = pl.ds(2 * h * PAIR, 2 * PAIR)
        back.append(links.send(pairs.at[1 - chip, :, columns], pairs_back.at[:, columns], links.over("seq", CHIP)))

        head_groups = len(head_plan) // heads
        head_rows = width // head_groups
        for number in range(head_groups):
            group = h * head_groups + number
            rows = pl.ds(number * head_rows, head_rows)
            term = sum(
                dot(first_t[rows, pl.ds(half * local, local)], pairs[half, :, columns], NN) for half in range(2)
            )
            out_term = sum(
                dot(
                    low_t[rows, pl.ds(half * local, local)],
                    pairs[half, :, pl.ds((2 * h + 1) * PAIR, PAIR)],
                    NN,
                )
                for half in range(2)
            )
            tail = jnp.where(lanes_of(out_term.shape) < E, term[:, PAIR:], out_term)
            grads_heads[group, 0, pl.ds(0, head_rows), pl.ds(0, PAIR)] = term[:, :PAIR].astype(bf16)
            grads_heads[group, 0, pl.ds(0, head_rows), pl.ds(PAIR, PAIR)] = tail.astype(bf16)
            fill(grads_heads, group, head_rows)
            begin("a%d" % group, grads_heads, full_heads, group, head_plan[group], mlp_groups + group)
        turns.tick()

    add_vec(9 + rank, total(pairs[0].astype(f32)) + total(pairs[1].astype(f32)))
    for copy in back:
        copy.wait()

    def last(owner, piece):
        near = aligned((owner - chip * 2) * places + piece * CHUNK, CHUNK)
        normed, _ = normalise(x_all[aligned(owner * places + piece * CHUNK, CHUNK), :].astype(f32))
        own, other = pairs[chip, near, :], pairs_back[near, :]
        attn = 0.0
        for h in range(heads):
            tail = slice((2 * h + 1) * PAIR, (2 * h + 2) * PAIR)
            attn += dot(own[:, tail], o_pairs[0, pl.ds(h * PAIR, PAIR), :], NN)
            attn += dot(other[:, tail], o_pairs[1, pl.ds(h * PAIR, PAIR), :], NN)
        first_grad = dot(own, w_pairs[0], NT) + dot(other, w_pairs[1], NT)
        part[0, near, :] = (part[0, near, :].astype(f32) + attn).astype(bf16)
        part[1, near, :] = (part[1, near, :].astype(f32) + first_grad * gain1).astype(bf16)
        add_vec(0, total(first_grad * normed))
        add_vec(1, total(first_grad))

    def last_loop(owner):
        def one(piece, _):
            last(owner, piece)
            return 0

        lax.fori_loop(0, pieces, one, 0)

    last_loop(beside)
    given = part.at[:, aligned((1 - core) * places, places)]
    crossing = links.send(given, core_buf, links.over("seq", CORE))
    turns.tick()
    last_loop(rank)
    vec_steps = [("seq", CORE), ("seq", CHIP)] + [("dp", bit) for bit in links.dp_bits]
    turns.add("vec", add_up_everywhere(links, vec_steps, vec_buf))
    turns.tick()

    reload = pltpu.make_async_copy(c_in, c_all.at[aligned(rank * places, places)], own_sems.at[0])
    reload.start()
    crossing.wait()
    reload.wait()
    for piece in range(pieces):
        rows = pl.ds(piece * CHUNK, CHUNK)
        own_rows = rows_of(rank, piece)
        near = aligned(core * places + piece * CHUNK, CHUNK)
        x = x_all[own_rows, :].astype(f32)
        sums = [part[which, near, :].astype(f32) + core_buf[which, rows, :].astype(f32) for which in range(2)]
        mixed_out[rows, :] = (x + sums[0] + end_bias).astype(bf16)
        normed, inverse = normalise(x)
        scaled = sums[1]
        rows_grad = inverse * (
            scaled
            - jnp.mean(scaled, axis=-1, keepdims=True)
            - normed * jnp.mean(scaled * normed, axis=-1, keepdims=True)
        )
        input_grad_out[rows, :] = c_all[own_rows, :].astype(f32) * weight + rows_grad
    turns.finish()
    vec_out[...] = vec_buf[0]


def padded(rows, dp_count):
    return -(-rows // (16 * dp_count)) * 16 * dp_count


def arrivals_of(order, blocks, rows, width):
    shapes = []
    for axis, _ in order[0]:
        if axis == "seq":
            blocks = 1
        else:
            rows //= 4 if axis == "line" else 2
        shape = (blocks, rows, width)
        shapes.append(pltpu.VMEM((3,) + shape if axis == "line" else shape, bf16))
    return shapes


def layer(dp_count, seq_count, *operands):
    places, width = operands[0].shape
    length = places * seq_count
    local = length // 2
    heads = H // seq_count
    hidden = operands[13].shape[1] // seq_count
    bits = bits_of(dp_count)
    mlp_plan = orders_of(dp_count, MLP_PLAN, 2, 2)
    head_plan = orders_of(dp_count, HEAD_PLAN, 1, heads)
    mlp_rows = padded(2 * width // len(mlp_plan), dp_count)
    head_rows = padded(width * heads // len(head_plan), dp_count)
    pieces = places // CHUNK
    copies = bits + 6 * pieces + (len(mlp_plan) + len(head_plan)) * 20
    copies += heads + 1 + bits + 2
    loads = 2 + 6 + 2 * (2 + heads)
    scratch = [
        pltpu.VMEM((length, width), bf16),
        pltpu.VMEM((length, width), bf16),
        pltpu.VMEM((width, length), bf16),
        pltpu.VMEM((width, length), bf16),
        pltpu.VMEM((heads, length, PAIR), bf16),
        pltpu.VMEM((heads, length, PAIR), bf16),
        pltpu.VMEM((heads, length, PAIR), bf16),
        pltpu.VMEM((2, local, 2 * heads * PAIR), bf16),
        pltpu.VMEM((local, 2 * heads * PAIR), bf16),
        pltpu.VMEM((2, width, 2 * heads * PAIR), bf16),
        pltpu.VMEM((1, 2 * heads * PAIR), f32),
        pltpu.VMEM((2, heads * PAIR, width), bf16),
        pltpu.VMEM((2, width, hidden), bf16),
        pltpu.VMEM((2, hidden, width), bf16),
        pltpu.VMEM((2, local, hidden), bf16),
        pltpu.VMEM((2, local, width), bf16),
        pltpu.VMEM((len(mlp_plan), 2, mlp_rows, width), bf16),
        pltpu.VMEM((len(head_plan), 1, head_rows, 2 * PAIR), bf16),
        pltpu.VMEM((2, places, width), bf16),
        pltpu.VMEM((PAIR, length), f32),
        pltpu.VMEM((SMALL_ROWS, width), f32),
        pltpu.VMEM((bits + 1, 8, 128), f32),
        pltpu.VMEM((bits + 3, VECTOR_ROWS, width), f32),
        pltpu.SemaphoreType.DMA((copies,)),
        pltpu.SemaphoreType.DMA((copies,)),
        pltpu.SemaphoreType.DMA((loads + len(mlp_plan) + len(head_plan),)),
    ]
    for order in mlp_plan:
        scratch += arrivals_of(order, 2, mlp_rows, width)
    for order in head_plan:
        scratch += arrivals_of(order, 1, head_rows, 2 * PAIR)
    smem = pl.BlockSpec(memory_space=pltpu.SMEM)
    return pl.pallas_call(
        functools.partial(
            layer_kernel, dp_count, (mlp_plan, head_plan), AGENDA if dp_count == 8 else []
        ),
        out_shape=(
            jax.ShapeDtypeStruct((seq_count, len(mlp_plan), mlp_rows, width), bf16),
            jax.ShapeDtypeStruct((seq_count, len(head_plan), head_rows, 2 * PAIR), bf16),
            jax.ShapeDtypeStruct((VECTOR_ROWS, width), f32),
            jax.ShapeDtypeStruct((places, width), bf16),
            jax.ShapeDtypeStruct((places, width), f32),
        ),
        in_specs=[ANY, ANY, smem] + [VMEM] * 8 + [ANY] * 4 + [VMEM],
        out_specs=(ANY, ANY, VMEM, VMEM, VMEM),
        scratch_shapes=scratch,
        compiler_params=pltpu.CompilerParams(
            collective_id=0, has_side_effects=True, vmem_limit_bytes=63 * 2**20
        ),
        name="layer",
    )(*operands)


def finish_kernel(mlp_in, heads_in, vec, mixed_in, grad_in, *rest):
    up_out, down_out, qkv_out, out_out, mixed_out, grad_out = rest[:6]
    vectors = rest[6:14]
    mlp, mix, mixed, grad, up_wide, down_wide, qkv_wide, out_wide, in_sems, out_sems = rest[14:]
    owners, mlp_groups, rows, width = mlp.shape
    _, head_groups, mix_rows, _ = mix.shape
    heads = H // owners
    per_head = head_groups // heads
    begun = []

    def begin(source, target, sems):
        copy = pltpu.make_async_copy(source, target, sems.at[begin.used])
        begin.used += 1
        copy.start()
        return copy

    begin.used = 0
    arriving = {"mixed": begin(mixed_in, mixed, in_sems), "grad": begin(grad_in, grad, in_sems)}
    for group in range(per_head):
        for r in range(owners):
            for h in range(heads):
                at = h * per_head + group
                arriving["mix", r, at] = begin(heads_in.at[r, at, pl.ds(0, mix_rows)], mix.at[r, at], in_sems)
    for group in range(mlp_groups):
        for r in range(owners):
            arriving["mlp", r, group] = begin(mlp_in.at[r, group, pl.ds(0, rows)], mlp.at[r, group], in_sems)
    begin.used = 0

    gain1, bias1, gain2, bias2, low1, low2, qkv, up = vectors
    for target, row in zip((gain1, bias1, gain2, bias2, low1, low2), (0, 1, 2, 3, 4, 4)):
        target[...] = vec[row]
    parts = [[], [], []]
    for r in range(owners):
        line = vec[pl.ds(5 + owners + r, 1), :]
        for h in range(heads):
            at = 2 * h * PAIR
            parts[0].append(line[:, at + PAIR : at + PAIR + E])
            parts[1].append(line[:, at : at + E])
            parts[2].append(line[:, at + E : at + PAIR])
    qkv[...] = jnp.concatenate(parts[0] + parts[1] + parts[2], axis=1)[0]
    up[...] = jnp.concatenate([vec[pl.ds(5 + r, 1), :] for r in range(owners)], axis=1)[0]

    tile = PAIR
    for group in range(per_head):
        for r in range(owners):
            for h in range(heads):
                arriving["mix", r, h * per_head + group].wait()
        for sub in range(mix_rows // tile):
            at_rows = pl.ds(group * mix_rows + sub * tile, tile)
            for r in range(owners):
                for h in range(heads):
                    head = r * heads + h
                    block = mix[r, h * per_head + group, pl.ds(sub * tile, tile), :].astype(f32)
                    tail = block[:, PAIR:]
                    qkv_wide[at_rows, pl.ds(head * E, E)] = tail[:, :E]
                    qkv_wide[at_rows, pl.ds((H + head) * E, E)] = block[:, :E]
                    qkv_wide[at_rows, pl.ds((2 * H + head) * E, E)] = block[:, E:PAIR]
                    out_wide[pl.ds(head * E, E), at_rows] = jnp.transpose(tail)[E:, :]
            begun.append(begin(qkv_wide.at[at_rows], qkv_out.at[at_rows], out_sems))
    begun.append(begin(out_wide, out_out, out_sems))
    for name, held, target in (("mixed", mixed, mixed_out), ("grad", grad, grad_out)):
        arriving[name].wait()
        begun.append(begin(held, target, out_sems))
    for group in range(mlp_groups):
        for r in range(owners):
            arriving["mlp", r, group].wait()
            wide = mlp[r, group].astype(f32)
            if group < mlp_groups // 2:
                place = (pl.ds(group * rows, rows), pl.ds(r * width, width))
                target, held = up_out, up_wide
            else:
                place = (pl.ds(r * width + (group - mlp_groups // 2) * rows, rows), pl.ds(0, width))
                target, held = down_out, down_wide
            held[place] = wide
            begun.append(begin(held.at[place], target.at[place], out_sems))
    for copy in begun:
        copy.wait()


def finish(full_mlp, full_heads, vec, mixed, input_grad):
    owners, mlp_groups, _, width = full_mlp.shape
    head_groups = full_heads.shape[1]
    rows = 2 * width // mlp_groups
    mix_rows = width * (H // owners) // head_groups
    lines = [width] * 6 + [3 * H * E, owners * width]
    wides = [(width, owners * width), (owners * width, width), (width, 3 * H * E), (H * E, width)]
    count = owners * (mlp_groups + head_groups) + 2
    return pl.pallas_call(
        finish_kernel,
        out_shape=tuple(jax.ShapeDtypeStruct(shape, f32) for shape in wides)
        + (
            jax.ShapeDtypeStruct(mixed.shape, mixed.dtype),
            jax.ShapeDtypeStruct(input_grad.shape, input_grad.dtype),
        )
        + tuple(jax.ShapeDtypeStruct((size,), f32) for size in lines),
        in_specs=[ANY, ANY, VMEM, ANY, ANY],
        out_specs=(ANY,) * 6 + (VMEM,) * len(lines),
        scratch_shapes=[
            pltpu.VMEM((owners, mlp_groups, rows, width), bf16),
            pltpu.VMEM((owners, head_groups, mix_rows, 2 * PAIR), bf16),
            pltpu.VMEM(mixed.shape, mixed.dtype),
            pltpu.VMEM(input_grad.shape, input_grad.dtype),
        ]
        + [pltpu.VMEM(shape, f32) for shape in wides]
        + [
            pltpu.SemaphoreType.DMA((count,)),
            pltpu.SemaphoreType.DMA((owners * mlp_groups + width // PAIR + 3,)),
        ],
        compiler_params=pltpu.CompilerParams(vmem_limit_bytes=60 * 2**20),
        name="finish",
    )(full_mlp, full_heads, vec, mixed, input_grad)


def turn_table(length):
    half = ROT // 2
    frequency = (10000.0 ** (-2.0 * np.arange(half, dtype=np.float32) / ROT)).astype(np.float32)
    angles = np.arange(length, dtype=np.float32)[:, None] * frequency[None, :]
    cosine, sine = np.cos(angles), np.sin(angles)
    table = np.concatenate([cosine, cosine, -sine, sine], axis=1).astype(np.float32)
    rest = np.zeros((length // 2, PAIR - 4 * ROT), np.float32)
    return jnp.asarray(np.concatenate([table[: length // 2], table[length // 2 :], rest], axis=1))


def body(
    tokens,
    tissue,
    norm1_gain,
    norm1_bias,
    norm2_gain,
    norm2_bias,
    qkv_weight,
    qkv_bias,
    out_weight,
    out_bias,
    up_weight,
    up_bias,
    down_weight,
    down_bias,
    cotangent,
):
    dp_count, seq_count = lax.axis_size("dp"), lax.axis_size("seq")
    _, places, width = tokens.shape
    full_mlp, full_heads, vec, mixed, input_grad = layer(
        dp_count,
        seq_count,
        tokens.reshape(places, width),
        cotangent.reshape(places, width),
        tissue,
        norm1_gain,
        norm1_bias,
        norm2_gain,
        norm2_bias,
        out_bias,
        down_bias,
        up_bias,
        qkv_bias,
        qkv_weight,
        out_weight,
        up_weight,
        down_weight,
        turn_table(places * seq_count),
    )
    results = finish(full_mlp, full_heads, vec, mixed, input_grad)
    up, down, qkv, out, mixed, input_grad, gain1, bias1, gain2, bias2, low1, low2, qkv_b, up_b = results
    return (
        mixed.reshape(tokens.shape),
        input_grad.reshape(tokens.shape),
        gain1,
        bias1,
        gain2,
        bias2,
        qkv,
        qkv_b,
        out,
        low1,
        up,
        up_b,
        down,
        low2,
    )


def solution(mesh):
    rows = P("dp", "seq", None)
    return jax.shard_map(
        body,
        mesh=mesh,
        in_specs=(rows, P("dp")) + (P(),) * 12 + (rows,),
        out_specs=(rows, rows) + (P(),) * 12,
        check_vma=False,
    )
```
